32 devices in a mesh: dp: 2 (over core), fsdp: 16 (over z, y, x).
Axes of the slice: x: 2, y: 2, z: 4, core: 2. Of those that a mesh axis runs over, the one named last changes fastest.
Arguments:
- tokens: bfloat16 [64, 512, 768], P(('dp', 'fsdp')), may hold values from -6 to 6
- lengths: int32 [64], P(('dp', 'fsdp')), may hold values from 65 to 512, as said below
- query_key_value_weight: bfloat16 [768, 2304], P('fsdp'), may hold values from -0.21875 to 0.21875
- qv_bias: bfloat16 [1536], P('fsdp'), may hold values from -3 to 3
- output_projection_weight: bfloat16 [768, 768], P('fsdp'), may hold values from -0.875 to 0.875
- output_projection_bias: bfloat16 [768], P('fsdp'), may hold values from -3 to 3
- gain_one: bfloat16 [768], P('fsdp'), may hold values from 0.25 to 1.75
- shift_one: bfloat16 [768], P('fsdp'), may hold values from -2 to 2
- widening_matrix: bfloat16 [768, 3072], P('fsdp'), may hold values from -0.21875 to 0.21875
- widening_offset_vector: bfloat16 [3072], P('fsdp'), may hold values from -3 to 3
- down_projection_weight: bfloat16 [3072, 768], P('fsdp'), may hold values from -0.109375 to 0.109375
- down_projection_bias: bfloat16 [768], P('fsdp'), may hold values from -2 to 2
- gain_two: bfloat16 [768], P('fsdp'), may hold values from 0.25 to 1.75
- shift_two: bfloat16 [768], P('fsdp'), may hold values from -2 to 2
- cotangent: bfloat16 [64, 512, 768], P(('dp', 'fsdp')), may hold values from -6 to 6
Outputs:
- output: bfloat16 [64, 512, 768], P(('dp', 'fsdp'))
- grad_tokens: bfloat16 [64, 512, 768], P(('dp', 'fsdp'))
- grad_qkv_weight: float32 [768, 2304], P('fsdp')
- grad_qv_bias: float32 [1536], P('fsdp')
- grad_out_weight: float32 [768, 768], P('fsdp')
- grad_out_bias: float32 [768], P('fsdp')
- grad_gain_one: float32 [768], P('fsdp')
- grad_shift_one: float32 [768], P('fsdp')
- grad_up_weight: float32 [768, 3072], P('fsdp')
- grad_up_bias: float32 [3072], P('fsdp')
- grad_down_weight: float32 [3072, 768], P('fsdp')
- grad_down_bias: float32 [768], P('fsdp')
- grad_gain_two: float32 [768], P('fsdp')
- grad_shift_two: float32 [768], P('fsdp')
The draws below stay inside these ranges and needn't reach their ends.
Inputs may be any that keep to these rules, and one draw needn't show every extreme that they name: `lengths`: each length lies in the upper half of one of the bucket sizes 512/4, 256 and 512; some sequence has length 512.
All inputs are finite; a program needn't handle non-finite values.
Results may differ from the reference program's by a relative error of at most 0.015.
Values may be sent and summed in bfloat16 or wider, within the bound.
No kernel may reach another device: no remote copies, remote signals or barrier semaphores. Data moves between devices by JAX's collectives and lax.ppermute only.
A program may use at most 192 MiB of HBM per device.

```python
import jax
import jax.numpy as jnp
from jax import lax

D = 768
HEAD_DIM = 64
FF = 3072
LEN = 512
SEQ_DEV = 2
SEQS = 64


def draw_lengths(key, part):
    key = jax.random.fold_in(key, 7)
    level_key, cut_key, full_key = jax.random.split(key, 3)
    levels = jax.random.randint(level_key, (SEQS,), 0, 3)
    capacity = jnp.where(levels == 0, LEN // 4, jnp.where(levels == 1, LEN // 2, LEN))
    cutoff = jax.random.randint(cut_key, (SEQS,), 0, 1 << 20) % (capacity // 2)
    chosen = jax.random.randint(full_key, (), 0, SEQS)
    lengths_out = jnp.where(jnp.arange(SEQS) == chosen, LEN, capacity - cutoff)
    return lengths_out.astype(jnp.int32)


def level_of(stream_key, dims, pieces, least, high):
    def one(axis_at, parts):
        steps = jax.random.uniform(jax.random.fold_in(jax.random.fold_in(stream_key, 6), axis_at), (parts,), jnp.float32, least / len(pieces), high / len(pieces))
        return jnp.repeat(jnp.exp(steps), dims[axis_at] // parts).reshape((-1,) + (1,) * (len(dims) - axis_at - 1))

    loudness = one(*pieces[0])
    for cut in pieces[1:]:
        loudness = loudness * one(*cut)
    return loudness


def scatter_about(key, dims, deviation, most, shards=(), held_as=jnp.bfloat16):
    factor_of = level_of(key, dims, shards, -0.22, 0.18) if shards else 1.0
    values = jax.random.normal(key, dims, jnp.float32) * deviation * factor_of
    return jnp.minimum(jnp.maximum(values, -most), most).astype(held_as)


def setup_inputs(seed: int = 0) -> dict:
    streams_of = jax.random.split(jax.random.key(seed), 16)
    return {
        "tokens": scatter_about(streams_of[0], (SEQS, LEN, D), 1.0, 6.0, ((0, 32),)),
        "lengths": draw_lengths(jax.random.fold_in(streams_of[15], 71), 0),
        "query_key_value_weight": scatter_about(streams_of[2], (D, 3 * D), D ** -0.5, 0.21875, ((0, 16),)),
        "qv_bias": scatter_about(streams_of[3], (2 * D,), 0.5, 3.0, ((0, 16),)),
        "output_projection_weight": scatter_about(streams_of[4], (D, D), (D // 16) ** -0.5, 0.875, ((0, 16),)),
        "output_projection_bias": scatter_about(streams_of[5], (D,), 0.5, 3.0, ((0, 16),)),
        "gain_one": jnp.clip(1.0 + 0.15 * jax.random.normal(streams_of[6], (D,), jnp.float32), 0.25, 1.75).astype(jnp.bfloat16),
        "shift_one": scatter_about(streams_of[7], (D,), 0.3, 2.0, ((0, 16),)),
        "widening_matrix": scatter_about(streams_of[8], (D, FF), D ** -0.5, 0.21875, ((0, 16),)),
        "widening_offset_vector": scatter_about(streams_of[9], (FF,), 0.5, 3.0, ((0, 16),)),
        "down_projection_weight": scatter_about(streams_of[10], (FF, D), FF ** -0.5, 0.109375, ((0, 16),)),
        "down_projection_bias": scatter_about(streams_of[11], (D,), 0.3, 2.0, ((0, 16),)),
        "gain_two": jnp.clip(1.0 + 0.15 * jax.random.normal(streams_of[12], (D,), jnp.float32), 0.25, 1.75).astype(jnp.bfloat16),
        "shift_two": scatter_about(streams_of[13], (D,), 0.3, 2.0, ((0, 16),)),
        "cotangent": scatter_about(streams_of[14], (SEQS, LEN, D), 1.0, 6.0, ((0, 32),)),
    }


EPSILON = 1e-12
MASKED = -1e+30
EXACT_ARITHMETIC = lax.Precision.HIGHEST

@jax.custom_vjp
def low(v):
    return lax.optimization_barrier(v.astype(jnp.bfloat16)).astype(jnp.float32)

@jax.custom_vjp
def summed_gradient_pass(v):
    return v

def low_keep(v):
    return (low(v), None)

def low_pass(kept, grad):
    return (grad,)

def back_keep(v):
    return (v, None)

def back_low(kept, grad):
    return (low(grad),)
low.defvjp(low_keep, low_pass)
summed_gradient_pass.defvjp(back_keep, back_low)

def both_low(values):
    return summed_gradient_pass(low(values))

def layer_norm(values, gain_vec, shift_vec):
    centred = values - lax.optimization_barrier(jnp.mean(values, axis=-1, keepdims=True))
    scaled = centred * lax.rsqrt(lax.optimization_barrier(jnp.mean(centred * centred, axis=-1, keepdims=True)) + EPSILON)
    return scaled * gain_vec + shift_vec

def gelu_exact(values):
    return 0.5 * values * (1.0 + lax.erf(values * 0.7071067811865476))

def forward(weights_all, sequence_tokens, seq_lengths):
    query_key_value_weight, qv_bias, output_projection_weight, output_projection_bias, gain_one, shift_one, widening_matrix, widening_offset_vector, down_projection_weight, down_projection_bias, gain_two, shift_two = weights_all
    seq_count, seq_length, model_width = sequence_tokens.shape
    head_count = model_width // HEAD_DIM
    every_bias = jnp.concatenate([qv_bias[:model_width], jnp.zeros((model_width,), jnp.float32), qv_bias[model_width:]])
    residual_mixed = jnp.einsum('cit,tk->cik', sequence_tokens, query_key_value_weight, precision=EXACT_ARITHMETIC) + every_bias
    residual_mixed = both_low(residual_mixed).reshape(seq_count, seq_length, 3, head_count, HEAD_DIM)
    key_valid = jnp.arange(seq_length)[None, :] < seq_lengths[:, None]
    raw_scores = jnp.einsum('sqhc,skhc->shqk', residual_mixed[:, :, 0], residual_mixed[:, :, 1], precision=EXACT_ARITHMETIC) * 0.125
    scores = summed_gradient_pass(jnp.where(key_valid[:, None, None, :], raw_scores, MASKED))
    row_top = lax.optimization_barrier(jnp.max(scores, axis=-1, keepdims=True))
    exp_scores = jnp.exp(scores - row_top)
    softmax_vals = exp_scores / lax.optimization_barrier(jnp.sum(exp_scores, axis=-1, keepdims=True))
    attention_output = jnp.einsum('shqk,skhc->sqhc', low(softmax_vals), residual_mixed[:, :, 2], precision=EXACT_ARITHMETIC)
    attention_output = both_low(attention_output.reshape(seq_count, seq_length, model_width))
    attention_branch = summed_gradient_pass(jnp.einsum('cit,tk->cik', attention_output, output_projection_weight, precision=EXACT_ARITHMETIC) + output_projection_bias)
    initial_standardised_rows = low(layer_norm(sequence_tokens + attention_branch, gain_one, shift_one))
    hidden_before_gelu = summed_gradient_pass(jnp.einsum('xit,tm->xim', initial_standardised_rows, widening_matrix, precision=EXACT_ARITHMETIC) + widening_offset_vector)
    activation_output = low(gelu_exact(hidden_before_gelu))
    feedforward_branch = summed_gradient_pass(jnp.einsum('vno,ou->vnu', activation_output, down_projection_weight, precision=EXACT_ARITHMETIC) + down_projection_bias)
    return layer_norm(initial_standardised_rows + feedforward_branch, gain_two, shift_two)

def reference(tokens, lengths, query_key_value_weight, qv_bias, output_projection_weight, output_projection_bias, gain_one, shift_one, widening_matrix, widening_offset_vector, down_projection_weight, down_projection_bias, gain_two, shift_two, cotangent):
    weights_all = tuple((weight.astype(jnp.float32) for weight in (query_key_value_weight, qv_bias, output_projection_weight, output_projection_bias, gain_one, shift_one, widening_matrix, widening_offset_vector, down_projection_weight, down_projection_bias, gain_two, shift_two)))
    group_count = tokens.shape[0] // SEQ_DEV
    token_groups = tokens.astype(jnp.float32).reshape(group_count, SEQ_DEV, LEN, D)
    length_groups = lengths.reshape(group_count, SEQ_DEV)
    cot_groups = cotangent.astype(jnp.float32).reshape(group_count, SEQ_DEV, LEN, D)

    def one_group(totals, inputs):
        group_tokens, group_lengths, group_cot = inputs

        def encoder_block_forward(weight_set, token_set):
            return forward(weight_set, token_set, group_lengths)
        result, pullback = jax.vjp(encoder_block_forward, weights_all, group_tokens)
        weight_grads, token_grads = pullback(group_cot)
        totals = jax.tree.map(lambda left, right: left + right, totals, weight_grads)
        return (totals, (result.astype(jnp.bfloat16), token_grads.astype(jnp.bfloat16)))
    start_totals = jax.tree.map(jnp.zeros_like, weights_all)
    totals, (outputs, token_grads) = lax.scan(one_group, start_totals, (token_groups, length_groups, cot_groups))
    return (outputs.reshape(tokens.shape), token_grads.reshape(tokens.shape), totals[0], totals[1], totals[2], totals[3], totals[4], totals[5], totals[6], totals[7], totals[8], totals[9], totals[10], totals[11])
```

```python
import functools

import jax
import jax.numpy as jnp
from jax import lax
from jax.experimental import pallas as pl
from jax.experimental.pallas import tpu as pltpu
from jax.sharding import PartitionSpec as P

HEAD_DIM = 64
GROUP = 256
HEADS = GROUP // HEAD_DIM
LANES = 128
PIECES = 16
TILE = 256
EPSILON = 1e-12
MASKED = -1e30
VMEM = 60 << 20
NN = (((1,), (0,)), ((), ()))
NT = (((1,), (1,)), ((), ()))
TN = (((0,), (0,)), ((), ()))
LOW, FULL = jnp.bfloat16, jnp.float32
ANY = pl.BlockSpec(memory_space=pl.ANY)


def dot(left, right, dims=NN):
    return lax.dot_general(left, right, dims, preferred_element_type=FULL)


def shape(dims, dtype):
    return jax.ShapeDtypeStruct(dims, dtype)


def whole(dims):
    return pl.BlockSpec(dims, lambda *at: (0,) * len(dims))


def params():
    return pltpu.CompilerParams(vmem_limit_bytes=VMEM)


def cost(flops, moved, exps=0):
    return pl.CostEstimate(flops=int(flops), bytes_accessed=int(moved), transcendentals=int(exps))


def norm_parts(values):
    centred = values - jnp.mean(values, axis=-1, keepdims=True)
    inv_root = lax.rsqrt(jnp.mean(centred * centred, axis=-1, keepdims=True) + EPSILON)
    return centred * inv_root, inv_root


def norm_back(grad_in, standard, inv_root, gain_vec):
    scaled = grad_in * gain_vec
    return inv_root * (
        scaled
        - jnp.mean(scaled, axis=-1, keepdims=True)
        - standard * jnp.mean(scaled * standard, axis=-1, keepdims=True)
    )


def column_sum(values):
    return jnp.sum(values, axis=0, keepdims=True)


def swap_cores(values):
    return lax.ppermute(values, "dp", [(0, 1), (1, 0)])


def plane_swap(values, step):
    first, second = (1, 2) if step == 0 else (2, 1)
    pairs = [(i, i ^ first) for i in range(16)] + [(16 + i, 16 + (i ^ second)) for i in range(16)]
    return lax.ppermute(values, ("dp", "fsdp"), pairs)


def z_swap(values, m):
    return lax.ppermute(values, "fsdp", [(i, i ^ (4 * m)) for i in range(16)])


def piece_of(place, core, k):
    mz, m1, m2 = k % 4, (k // 4) % 2, k // 8
    low = jnp.where(core == 0, m1 + 2 * m2, 2 * m1 + m2)
    return place ^ (4 * mz + low)


def gather_halves(piece):
    first = jnp.stack([piece] + [z_swap(piece, m) for m in (1, 2, 3)])
    second = jnp.concatenate([first, plane_swap(first, 0)])
    third = plane_swap(second, 1)
    return second, third, swap_cores(second), swap_cores(third)


def add_low(left, right):
    return (left.astype(FULL) + right.astype(FULL)).astype(LOW)


def scatter_halves(mine, theirs):
    came = swap_cores(theirs)
    sent = plane_swap(add_low(mine[8:], came[8:]), 1)
    half = mine[:8].astype(FULL) + came[:8].astype(FULL) + sent.astype(FULL)
    sent = plane_swap(half[4:].astype(LOW), 0)
    quarter = half[:4] + sent.astype(FULL)
    parts = [z_swap(quarter[m].astype(LOW), m) for m in (1, 2, 3)]
    return quarter[0] + sum(p.astype(FULL) for p in parts)


def half_of(values, which, axis=1):
    width = values.shape[axis] // 2
    return lax.dynamic_slice_in_dim(values, which * width, width, axis)


def join_halves(mine, core):
    other = swap_cores(mine)
    return jnp.where(
        core == 0, jnp.concatenate([mine, other], axis=1), jnp.concatenate([other, mine], axis=1)
    )


def copies_of(table, stacks, rows, width, skip, target, column_stride, sem):
    copies = []
    for half in range(2):
        for k in range(PIECES):
            row = pl.multiple_of(table[half, k] * rows, 16)
            column = pl.multiple_of(table[2, half] * column_stride, LANES)
            copies.append(
                pltpu.make_async_copy(
                    stacks[2 * half + k // 8].at[k % 8, :, pl.ds(skip, width)],
                    target.at[pl.ds(row, rows), pl.ds(column, width)],
                    sem,
                )
            )
    return copies


def start(copies):
    for copy in copies:
        copy.start()


def wait(copies):
    for copy in copies:
        copy.wait()


def head_mask(h, dims):
    lane = lax.broadcasted_iota(jnp.int32, dims, 1)
    return (lane >= HEAD_DIM * h) & (lane < HEAD_DIM * (h + 1))


def spread(vec, count, at):
    rows = vec.shape[0] // PIECES
    runs = [
        vec[rows * p : rows * (p + 1), at + j : at + j + 1] for p in range(PIECES) for j in range(count)
    ]
    tall = jnp.concatenate(runs, axis=0)
    return jnp.broadcast_to(tall, (tall.shape[0], LANES)).T[0:1]


def attend_kernel(
    table, lengths, tokens, s0, s1, s2, s3,
    q_out, k_out, v_out, e_out, attended, attended_full, inv_out, vectors, up_bias,
    weight, vec, bias, sem,
):
    seq, group = pl.program_id(0), pl.program_id(1)
    width = weight.shape[0]
    rows, half = width // PIECES, weight.shape[1] // 2
    stacks = (s0, s1, s2, s3)

    @pl.when((seq == 0) & (group == 0))
    def _():
        small = [
            pltpu.make_async_copy(
                stacks[k // 8].at[k % 8, :, pl.ds(half, LANES)],
                vec.at[pl.ds(pl.multiple_of(table[0, k] * rows, 16), rows)],
                sem.at[0],
            )
            for k in range(PIECES)
        ]
        large = copies_of(table, stacks, rows, half, 0, weight, half, sem.at[1])
        start(small)
        start(large)
        wait(small)
        values = vec[...].astype(FULL)
        vectors[...] = values.T[0:16]
        qv = spread(values, 2, 0)
        up_bias[...] = spread(values, 4, 8)
        bias[...] = jnp.zeros_like(bias)
        bias[:, 0:width] = qv[:, 0:width]
        bias[:, 2 * width : 3 * width] = qv[:, width : 2 * width]
        wait(large)

    rows_in = tokens[...]
    at = pl.multiple_of(group * GROUP, GROUP)

    def project(i):
        columns = pl.ds(i * width + at, GROUP)
        return (dot(rows_in, weight[:, columns]) + bias[:, columns]).astype(LOW)

    q, k, v = project(0), project(1), project(2)
    q_out[...], k_out[...], v_out[...] = q, k, v
    scaled = q * LOW(0.125)
    dims = q.shape
    keep = lax.broadcasted_iota(jnp.int32, (1, dims[0]), 1) < lengths[seq]
    total = jnp.zeros(dims, FULL)
    inv = jnp.zeros(dims, FULL)
    for h in range(HEADS):
        mask = head_mask(h, dims)
        scores = jnp.where(keep, dot(scaled, jnp.where(mask, k, LOW(0)), NT), MASKED)
        exps = jnp.exp(scores - jnp.max(scores, axis=1, keepdims=True))
        row_total = jnp.sum(exps, axis=1, keepdims=True)
        low = exps.astype(LOW)
        e_out[h] = low
        total = total + dot(low, jnp.where(mask, v, LOW(0)))
        inv = jnp.where(mask, 1.0 / row_total, inv)
    result = total * inv
    inv_out[...] = inv
    attended_full[...] = result
    attended[...] = result.astype(LOW)


def attend(table, lengths, tokens, stacks):
    seqs, length, width = tokens.shape
    groups = width // GROUP
    rows = seqs * length
    block = pl.BlockSpec((length, GROUP), lambda s, g, *_: (s, g))
    heads = width // HEAD_DIM
    return pl.pallas_call(
        attend_kernel,
        grid_spec=pltpu.PrefetchScalarGridSpec(
            num_scalar_prefetch=2,
            grid=(seqs, groups),
            in_specs=[pl.BlockSpec((length, width), lambda s, g, *_: (s, 0))] + [ANY] * 4,
            out_specs=[block] * 3
            + [pl.BlockSpec((HEADS, length, length), lambda s, g, *_: (s * groups + g, 0, 0))]
            + [block] * 3
            + [whole((16, width)), whole((1, 4 * width))],
            scratch_shapes=[
                pltpu.VMEM((width, 3 * width), LOW),
                pltpu.VMEM((width, LANES), LOW),
                pltpu.VMEM((1, 3 * width), FULL),
                pltpu.SemaphoreType.DMA((2,)),
            ],
        ),
        out_shape=[shape((rows, width), LOW)] * 3
        + [
            shape((seqs * heads, length, length), LOW),
            shape((rows, width), LOW),
            shape((rows, width), FULL),
            shape((rows, width), FULL),
            shape((16, width), FULL),
            shape((1, 4 * width), FULL),
        ],
        compiler_params=params(),
        cost_estimate=cost(16e9, 30e6),
        name="attend",
    )(table, lengths, tokens.reshape(rows, width), *stacks)


def widen_kernel(
    table, attended, tokens, vectors, up_bias, s0, s1, s2, s3,
    normed, standard, root, active, slope,
    out_weight, up_weight, sem,
):
    width = out_weight.shape[0]
    rows, half = width // PIECES, width // 2
    stacks = (s0, s1, s2, s3)
    first = pl.program_id(0) == 0
    small = copies_of(table, stacks, rows, half, 0, out_weight, half, sem.at[0])
    large = copies_of(table, stacks, rows, 4 * half, half, up_weight, 4 * half, sem.at[1])

    @pl.when(first)
    def _():
        start(small)
        start(large)
        wait(small)

    values = tokens[...].astype(FULL) + dot(attended[...], out_weight[...]) + vectors[2:3]
    n, s = norm_parts(values)
    standard[...] = n
    root[...] = jnp.broadcast_to(s, root.shape)
    low = (n * vectors[3:4] + vectors[4:5]).astype(LOW)
    normed[...] = low

    @pl.when(first)
    def _():
        wait(large)

    for c in range(4):
        columns = slice(c * width, (c + 1) * width)
        hidden = dot(low, up_weight[:, columns]) + up_bias[:, columns]
        part = 0.5 * (1.0 + lax.erf(hidden * 0.7071067811865476))
        density = jnp.exp(-0.5 * hidden * hidden) * 0.3989422804014327
        active[:, columns] = (hidden * part).astype(LOW)
        slope[:, columns] = (part + hidden * density).astype(LOW)


def widen(table, attended, tokens, vectors, up_bias, stacks):
    rows, width = attended.shape
    row = lambda w: pl.BlockSpec((TILE, w), lambda i, *_: (i, 0))
    return pl.pallas_call(
        widen_kernel,
        grid_spec=pltpu.PrefetchScalarGridSpec(
            num_scalar_prefetch=1,
            grid=(rows // TILE,),
            in_specs=[row(width), row(width), whole(vectors.shape), whole(up_bias.shape)] + [ANY] * 4,
            out_specs=[row(width), row(width), row(LANES), row(4 * width), row(4 * width)],
            scratch_shapes=[
                pltpu.VMEM((width, width), LOW),
                pltpu.VMEM((width, 4 * width), LOW),
                pltpu.SemaphoreType.DMA((2,)),
            ],
        ),
        out_shape=[
            shape((rows, width), LOW),
            shape((rows, width), FULL),
            shape((rows, LANES), FULL),
            shape((rows, 4 * width), LOW),
            shape((rows, 4 * width), LOW),
        ],
        compiler_params=params(),
        cost_estimate=cost(12e9, 30e6),
        name="widen",
    )(table, attended, tokens.reshape(rows, width), vectors, up_bias, *stacks)


def narrow_kernel(
    table, active, slope, normed, standard, root, cotangent, vectors, u0, u1, u2, u3, d0, d1, d2, d3,
    output, branch_two, pre_grad, branch_one, attended_grad, sums, up_sum,
    out_weight, up_weight, down_weight, sem,
):
    width = out_weight.shape[0]
    rows, half = width // PIECES, width // 2
    first = pl.program_id(0) == 0
    ups, downs = (u0, u1, u2, u3), (d0, d1, d2, d3)
    out_copies = copies_of(table, ups, rows, half, 0, out_weight, half, sem.at[0])
    up_copies = copies_of(table, ups, rows, 4 * half, half, up_weight, 4 * half, sem.at[1])
    down_copies = copies_of(table, downs, 4 * rows, half, 0, down_weight, half, sem.at[2])

    @pl.when(first)
    def _():
        start(down_copies)
        start(up_copies)
        start(out_copies)
        sums[...] = jnp.zeros_like(sums)
        up_sum[...] = jnp.zeros_like(up_sum)
        wait(down_copies)

    values = normed[...].astype(FULL) + dot(active[...], down_weight[...]) + vectors[5:6]
    n2, s2 = norm_parts(values)
    output[...] = (n2 * vectors[6:7] + vectors[7:8]).astype(LOW)
    grad = cotangent[...].astype(FULL)
    second = norm_back(grad, n2, s2, vectors[6:7])
    low = second.astype(LOW)
    branch_two[...] = low
    sums[0:1] += column_sum(grad * n2)
    sums[1:2] += column_sum(grad)
    sums[2:3] += column_sum(low.astype(FULL))

    @pl.when(first)
    def _():
        wait(up_copies)

    normed_grad = second
    for c in range(4):
        columns = slice(c * width, (c + 1) * width)
        part = (dot(low, down_weight[columns], NT) * slope[:, columns].astype(FULL)).astype(LOW)
        pre_grad[:, columns] = part
        up_sum[:, columns] += column_sum(part.astype(FULL))
        normed_grad = normed_grad + dot(part, up_weight[:, columns], NT)
    n1 = standard[...]
    sums[3:4] += column_sum(normed_grad * n1)
    sums[4:5] += column_sum(normed_grad)
    low = norm_back(normed_grad, n1, root[:, 0:1], vectors[3:4]).astype(LOW)
    branch_one[...] = low
    sums[5:6] += column_sum(low.astype(FULL))

    @pl.when(first)
    def _():
        wait(out_copies)

    attended_grad[...] = dot(low, out_weight[...], NT).astype(LOW)


def narrow(table, active, slope, normed, standard, root, cotangent, vectors, ups, downs):
    rows, width = normed.shape
    row = lambda w: pl.BlockSpec((TILE, w), lambda i, *_: (i, 0))
    return pl.pallas_call(
        narrow_kernel,
        grid_spec=pltpu.PrefetchScalarGridSpec(
            num_scalar_prefetch=1,
            grid=(rows // TILE,),
            in_specs=[row(4 * width), row(4 * width), row(width), row(width), row(LANES), row(width)]
            + [whole(vectors.shape)]
            + [ANY] * 8,
            out_specs=[row(width), row(width), row(4 * width), row(width), row(width)]
            + [whole((8, width)), whole((1, 4 * width))],
            scratch_shapes=[
                pltpu.VMEM((width, width), LOW),
                pltpu.VMEM((width, 4 * width), LOW),
                pltpu.VMEM((4 * width, width), LOW),
                pltpu.SemaphoreType.DMA((3,)),
            ],
        ),
        out_shape=[
            shape((rows, width), LOW),
            shape((rows, width), LOW),
            shape((rows, 4 * width), LOW),
            shape((rows, width), LOW),
            shape((rows, width), LOW),
            shape((8, width), FULL),
            shape((1, 4 * width), FULL),
        ],
        compiler_params=params(),
        cost_estimate=cost(24e9, 40e6),
        name="narrow",
    )(table, active, slope, normed, standard, root, cotangent.reshape(rows, width), vectors, *ups, *downs)


def down_grad_kernel(order, active, branch_two, mine, theirs):
    step = pl.program_id(0)
    width = branch_two.shape[1]
    rows, half = 4 * width // PIECES, width // 2
    result = dot(active[...], branch_two[...], TN).astype(LOW)
    for p in range(4):
        block = result[rows * p : rows * (p + 1)]
        core = order[2, 0]

        @pl.when(core == 0)
        def _():
            mine[order[0, 4 * step + p]] = block[:, :half]
            theirs[order[1, 4 * step + p]] = block[:, half:]

        @pl.when(core == 1)
        def _():
            mine[order[0, 4 * step + p]] = block[:, half:]
            theirs[order[1, 4 * step + p]] = block[:, :half]


def down_grad(order, active, branch_two):
    rows, width = branch_two.shape
    stack = (PIECES, 4 * width // PIECES, width // 2)
    return pl.pallas_call(
        down_grad_kernel,
        grid_spec=pltpu.PrefetchScalarGridSpec(
            num_scalar_prefetch=1,
            grid=(4,),
            in_specs=[pl.BlockSpec((rows, width), lambda i, *_: (0, i)), whole((rows, width))],
            out_specs=[whole(stack)] * 2,
        ),
        out_shape=[shape(stack, LOW)] * 2,
        compiler_params=params(),
        cost_estimate=cost(7e9, 14e6),
        name="down_grad",
    )(order, active, branch_two)


def put_pieces(order, result, mine, theirs, to_mine, at):
    rows = result.shape[0] // PIECES
    width = result.shape[1]
    for p in range(PIECES):
        block = result[rows * p : rows * (p + 1)]

        @pl.when(to_mine)
        def _():
            mine[order[0, p], :, at : at + width] = block

        @pl.when(jnp.logical_not(to_mine))
        def _():
            theirs[order[1, p], :, at : at + width] = block


def up_grad_kernel(order, normed, pre_grad, attended, branch_one, mine, theirs):
    step = pl.program_id(0)
    width = normed.shape[1]
    half = width // 2
    core = order[2, 0]

    @pl.when(step < 4)
    def _():
        result = dot(normed[...], pre_grad[...], TN).astype(LOW)
        for part in range(2):

            @pl.when(step % 2 == part)
            def _():
                put_pieces(order, result, mine, theirs, step // 2 == core, half + part * width)

    @pl.when(step == 4)
    def _():
        result = dot(attended[...], branch_one[...], TN).astype(LOW)
        for c in range(2):
            put_pieces(order, result[:, c * half : (c + 1) * half], mine, theirs, core == c, 0)


def up_grad(order, normed, pre_grad, attended, branch_one):
    rows, width = normed.shape
    stack = (PIECES, width // PIECES, 5 * width // 2)
    return pl.pallas_call(
        up_grad_kernel,
        grid_spec=pltpu.PrefetchScalarGridSpec(
            num_scalar_prefetch=1,
            grid=(5,),
            in_specs=[
                whole((rows, width)),
                pl.BlockSpec((rows, width), lambda i, *_: (0, jnp.minimum(i, 3))),
                whole((rows, width)),
                whole((rows, width)),
            ],
            out_specs=[whole(stack)] * 2,
        ),
        out_shape=[shape(stack, LOW)] * 2,
        compiler_params=params(),
        cost_estimate=cost(9e9, 18e6),
        name="up_grad",
    )(order, normed, pre_grad, attended, branch_one)


def attend_back_kernel(
    q_in, k_in, v_in, e_in, attended_full, inv_in, grad_in, q_grad, k_grad, v_grad, sums
):
    seq = pl.program_id(1)
    q, k, v = q_in[...] * LOW(0.125), k_in[...], v_in[...]
    dims = q.shape
    grad = (grad_in[...].astype(FULL) * inv_in[...]).astype(LOW)
    along = grad.astype(FULL) * attended_full[...]
    q_total, k_total, v_total = (jnp.zeros(dims, FULL) for _ in range(3))
    for h in range(HEADS):
        mask = head_mask(h, dims)
        masked = lambda values: jnp.where(mask, values, LOW(0))
        exps = e_in[h]
        shift = jnp.sum(jnp.where(mask, along, 0.0), axis=1, keepdims=True)
        score = (exps.astype(FULL) * (dot(grad, masked(v), NT) - shift)).astype(LOW)
        q_total = q_total + dot(score, masked(k))
        k_total = k_total + dot(score, masked(q), TN)
        v_total = v_total + dot(exps, masked(grad), TN)
    q_low, k_low, v_low = (q_total * 0.125).astype(LOW), k_total.astype(LOW), v_total.astype(LOW)
    q_grad[...], k_grad[...], v_grad[...] = q_low, k_low, v_low
    both = jnp.concatenate([column_sum(q_low.astype(FULL)), column_sum(v_low.astype(FULL))], axis=0)

    @pl.when(seq == 0)
    def _():
        sums[0:2] = both

    @pl.when(seq != 0)
    def _():
        sums[0:2] += both


def attend_back(q, k, v, exps, attended_full, inv, grad, length):
    rows, width = q.shape
    seqs, groups = rows // length, width // GROUP
    block = pl.BlockSpec((length, GROUP), lambda g, s: (s, g))
    return pl.pallas_call(
        attend_back_kernel,
        grid=(groups, seqs),
        in_specs=[block] * 3
        + [pl.BlockSpec((HEADS, length, length), lambda g, s: (s * groups + g, 0, 0))]
        + [block] * 3,
        out_specs=[block] * 3 + [pl.BlockSpec((8, GROUP), lambda g, s: (0, g))],
        out_shape=[shape((rows, width), LOW)] * 3 + [shape((8, width), FULL)],
        compiler_params=params(),
        cost_estimate=cost(16e9, 25e6),
        name="attend_back",
    )(q, k, v, exps, attended_full, inv, grad)


def qkv_grad_kernel(order, tokens, q_grad, k_grad, v_grad, sums, qv_sums, up_sum, mine, theirs):
    step = pl.program_id(0)
    width = tokens.shape[1]
    half = width // 2
    core = order[2, 0]
    for i, grads in enumerate((q_grad, k_grad, v_grad)):

        @pl.when(step // 2 == i)
        def _():
            result = dot(tokens[...], grads[...], TN).astype(LOW)
            for part in range(3):

                @pl.when(step % 3 == part)
                def _():
                    put_pieces(order, result, mine, theirs, step // 3 == core, part * half)

    @pl.when(step == 0)
    def _():
        rows = width // PIECES
        ones = jnp.concatenate([sums[...], qv_sums[...], jnp.zeros((LANES - 16, width), FULL)], axis=0).T
        lane = lax.broadcasted_iota(jnp.int32, (rows, LANES), 1)

        def tall(row):
            return jnp.broadcast_to(row, (LANES, row.shape[1])).T

        qv = [tall(qv_sums[i : i + 1]) for i in range(2)]
        up = [tall(up_sum[:, i * width : (i + 1) * width]) for i in range(4)]
        for p in range(PIECES):
            block = ones[rows * p : rows * (p + 1)]
            block = jnp.where(lane < 8, block, 0.0)
            for j in range(2):
                run = 2 * p + j
                at = rows * (run % PIECES)
                block = jnp.where(lane == 8 + j, qv[run // PIECES][at : at + rows], block)
            for j in range(4):
                run = 4 * p + j
                at = rows * (run % PIECES)
                block = jnp.where(lane == 10 + j, up[run // PIECES][at : at + rows], block)
            low = block.astype(LOW)
            mine[order[0, p], :, 3 * half :] = low
            theirs[order[1, p], :, 3 * half :] = low


def qkv_grad(order, tokens, q_grad, k_grad, v_grad, sums, qv_sums, up_sum):
    rows, width = q_grad.shape
    half = width // 2
    stack = (PIECES, width // PIECES, 3 * half + LANES)

    def column(i):
        return pl.BlockSpec((rows, half), lambda s, *_: (0, jnp.clip(s - 2 * i, 0, 1)))

    return pl.pallas_call(
        qkv_grad_kernel,
        grid_spec=pltpu.PrefetchScalarGridSpec(
            num_scalar_prefetch=1,
            grid=(6,),
            in_specs=[whole((rows, width)), column(0), column(1), column(2)]
            + [whole(sums.shape), whole(qv_sums.shape), whole(up_sum.shape)],
            out_specs=[whole(stack)] * 2,
        ),
        out_shape=[shape(stack, LOW)] * 2,
        compiler_params=params(),
        cost_estimate=cost(6e9, 14e6),
        name="qkv_grad",
    )(order, tokens.reshape(rows, width), q_grad, k_grad, v_grad, sums, qv_sums, up_sum)


def token_grad_kernel(table, q_grad, k_grad, v_grad, first, s0, s1, s2, s3, out, weight, sem):
    width = weight.shape[0]
    rows, half = width // PIECES, weight.shape[1] // 2
    copies = copies_of(table, (s0, s1, s2, s3), rows, half, 0, weight, half, sem)

    @pl.when(pl.program_id(0) == 0)
    def _():
        start(copies)
        wait(copies)

    total = first[...].astype(FULL)
    for i, grads in enumerate((q_grad, k_grad, v_grad)):
        total = total + dot(grads[...], weight[:, i * width : (i + 1) * width], NT)
    out[...] = total.astype(LOW)


def token_grad(table, q_grad, k_grad, v_grad, first, stacks):
    rows, width = q_grad.shape
    row = pl.BlockSpec((TILE, width), lambda i, *_: (i, 0))
    return pl.pallas_call(
        token_grad_kernel,
        grid_spec=pltpu.PrefetchScalarGridSpec(
            num_scalar_prefetch=1,
            grid=(rows // TILE,),
            in_specs=[row] * 4 + [ANY] * 4,
            out_specs=row,
            scratch_shapes=[pltpu.VMEM((width, 3 * width), LOW), pltpu.SemaphoreType.DMA],
        ),
        out_shape=shape((rows, width), LOW),
        compiler_params=params(),
        cost_estimate=cost(6e9, 12e6),
        name="token_grad",
    )(table, q_grad, k_grad, v_grad, first, *stacks)


def pack(vectors, rows):
    columns = jnp.concatenate([v.reshape(-1, rows) for v in vectors], axis=0).T
    return jnp.pad(columns, ((0, 0), (0, LANES - columns.shape[1])))


def pack_all(chips, rows, qv, out_bias, gain_one, shift_one, up_bias, down_bias, gain_two, shift_two):
    parts = (qv, out_bias, gain_one, shift_one, down_bias, gain_two, shift_two, up_bias)
    if chips == 1:
        return pack(parts, rows)
    return jnp.concatenate(
        [pack([v.reshape(chips, -1)[p] for v in parts], rows) for p in range(chips)], axis=0
    )


def shards(
    chips,
    tokens,
    lengths,
    query_key_value_weight,
    qv_bias,
    output_projection_weight,
    output_projection_bias,
    gain_one,
    shift_one,
    widening_matrix,
    widening_offset_vector,
    down_projection_weight,
    down_projection_bias,
    gain_two,
    shift_two,
    cotangent,
):
    seq_count, seq_length, width = tokens.shape
    core, place = lax.axis_index("dp"), lax.axis_index("fsdp")
    rows = query_key_value_weight.shape[0]
    small = (
        qv_bias,
        output_projection_bias,
        gain_one,
        shift_one,
        widening_offset_vector,
        down_projection_bias,
        gain_two,
        shift_two,
    )
    direct = chips == PIECES
    numbers = range(PIECES)
    if direct:
        qkv_set = gather_halves(
            jnp.concatenate([half_of(query_key_value_weight, core), pack_all(1, rows, *small)], axis=1)
        )
        up_set = gather_halves(
            jnp.concatenate([half_of(output_projection_weight, core), half_of(widening_matrix, core)], axis=1)
        )
        down_set = gather_halves(half_of(down_projection_weight, core))
        owners = [jnp.stack([piece_of(place, c, k) for k in numbers]) for c in (core, 1 - core)]
    else:
        gather = lambda values: lax.all_gather(values, "fsdp", axis=0, tiled=True)
        packed = pack_all(PIECES, width // PIECES, *(gather(v) for v in small))

        def stacks_of(make):
            both = [make(c) for c in (core, 1 - core)]
            both = [values.reshape(2, 8, -1, values.shape[1]) for values in both]
            return both[0][0], both[0][1], both[1][0], both[1][1]

        full_qkv, full_out = gather(query_key_value_weight), gather(output_projection_weight)
        full_up, full_down = gather(widening_matrix), gather(down_projection_weight)
        qkv_set = stacks_of(lambda c: jnp.concatenate([half_of(full_qkv, c), packed], axis=1))
        up_set = stacks_of(lambda c: jnp.concatenate([half_of(full_out, c), half_of(full_up, c)], axis=1))
        down_set = stacks_of(lambda c: half_of(full_down, c))
        owners = [jnp.arange(PIECES), jnp.arange(PIECES)]
    cores = jnp.stack([core, 1 - core] + [core] * 14)
    table = jnp.stack(owners + [cores]).astype(jnp.int32)
    order = jnp.stack([jnp.argsort(o) for o in owners] + [cores]).astype(jnp.int32)

    q, k, v, exps, attended, attended_full, inv, vectors, up_bias = attend(table, lengths, tokens, qkv_set)
    normed, standard, root, active, slope = widen(table, attended, tokens, vectors, up_bias, up_set)
    output, branch_two, pre_grad, branch_one, attended_grad, sums, up_sum = narrow(
        table, active, slope, normed, standard, root, cotangent, vectors, up_set, down_set
    )
    down_pair = down_grad(order, active, branch_two)
    up_pair = up_grad(order, normed, pre_grad, attended, branch_one)
    q_grad, k_grad, v_grad, qv_sums = attend_back(
        q, k, v, exps, attended_full, inv, attended_grad, seq_length
    )
    qkv_pair = qkv_grad(order, tokens, q_grad, k_grad, v_grad, sums, qv_sums, up_sum)
    grad_tokens = token_grad(table, q_grad, k_grad, v_grad, branch_one, qkv_set)

    half = width // 2
    if direct:
        down_sum, up_total, qkv_sum = (scatter_halves(*pair) for pair in (down_pair, up_pair, qkv_pair))
        vec = qkv_sum[:, 3 * half :]
        qkv_sum = qkv_sum[:, : 3 * half]
        vec_columns = lambda at, count: vec[:, at : at + count].T.reshape(-1)
    else:

        def reduce(values):
            return lax.psum_scatter(values, "fsdp", scatter_dimension=0, tiled=True)

        def totals(pair):
            both = pair[0].astype(FULL) + swap_cores(pair[1]).astype(FULL)
            return both.reshape(-1, both.shape[2])

        down_sum, up_total = reduce(totals(down_pair)), reduce(totals(up_pair))
        whole_qkv = totals(qkv_pair)
        qkv_sum = reduce(whole_qkv[:, : 3 * half])
        vec = whole_qkv[:, 3 * half :].reshape(PIECES, -1, LANES)
        vec_columns = lambda at, count: reduce(vec[:, :, at : at + count].transpose(0, 2, 1).reshape(-1))
    out_sum, up_total = up_total[:, :half], up_total[:, half:]
    return (
        output.reshape(tokens.shape),
        grad_tokens.reshape(tokens.shape),
        join_halves(qkv_sum, core),
        vec_columns(8, 2),
        join_halves(out_sum, core),
        vec_columns(5, 1),
        vec_columns(3, 1),
        vec_columns(4, 1),
        join_halves(up_total, core),
        vec_columns(10, 4),
        join_halves(down_sum, core),
        vec_columns(2, 1),
        vec_columns(0, 1),
        vec_columns(1, 1),
    )


def solution(mesh):
    tokens, lengths = P(("dp", "fsdp"), None, None), P(("dp", "fsdp"))
    matrix, vector = P("fsdp", None), P("fsdp")
    return jax.shard_map(
        functools.partial(shards, mesh.shape["fsdp"]),
        mesh=mesh,
        in_specs=(
            tokens, lengths, matrix, vector, matrix, vector, vector, vector,
            matrix, vector, matrix, vector, vector, vector, tokens,
        ),
        out_specs=(
            tokens, tokens, matrix, vector, matrix, vector, vector, vector,
            matrix, vector, matrix, vector, vector, vector,
        ),
        check_vma=False,
    )
```

```python
import functools

import jax
import jax.numpy as jnp
from jax import lax
from jax.experimental import pallas as pl
from jax.experimental.pallas import tpu as pltpu
from jax.sharding import PartitionSpec as P

HEAD_DIM = 64
GROUP = 256
HEADS = GROUP // HEAD_DIM
LANES = 128
PIECES = 16
TILE = 256
EPSILON = 1e-12
MASKED = -1e30
VMEM = 40 << 20
NN = (((1,), (0,)), ((), ()))
NT = (((1,), (1,)), ((), ()))
TN = (((0,), (0,)), ((), ()))
LOW, FULL = jnp.bfloat16, jnp.float32
ANY = pl.BlockSpec(memory_space=pl.ANY)


def dot(left, right, dims=NN):
    return lax.dot_general(left, right, dims, preferred_element_type=FULL)


def shape(dims, dtype):
    return jax.ShapeDtypeStruct(dims, dtype)


def far(dims, dtype):
    return pltpu.HBM(dims, dtype)


def keep_far(values):
    return pltpu.with_memory_space_constraint(values, pltpu.HBM)


def whole(dims):
    return pl.BlockSpec(dims, lambda *at: (0,) * len(dims))


def params():
    return pltpu.CompilerParams(vmem_limit_bytes=VMEM)


def cost(flops, moved, exps=0):
    return pl.CostEstimate(flops=int(flops), bytes_accessed=int(moved), transcendentals=int(exps))


def norm_parts(values):
    centred = values - jnp.mean(values, axis=-1, keepdims=True)
    inv_root = lax.rsqrt(jnp.mean(centred * centred, axis=-1, keepdims=True) + EPSILON)
    return centred * inv_root, inv_root


def norm_back(grad_in, standard, inv_root, gain_vec):
    scaled = grad_in * gain_vec
    return inv_root * (
        scaled
        - jnp.mean(scaled, axis=-1, keepdims=True)
        - standard * jnp.mean(scaled * standard, axis=-1, keepdims=True)
    )


def column_sum(values):
    return jnp.sum(values, axis=0, keepdims=True)


def swap_cores(values):
    return lax.ppermute(values, "dp", [(0, 1), (1, 0)])


def plane_swap(values, step):
    first, second = (1, 2) if step == 0 else (2, 1)
    pairs = [(i, i ^ first) for i in range(16)] + [(16 + i, 16 + (i ^ second)) for i in range(16)]
    return lax.ppermute(values, ("dp", "fsdp"), pairs)


def z_swap(values, m):
    return lax.ppermute(values, "fsdp", [(i, i ^ (4 * m)) for i in range(16)])


def piece_of(place, core, k):
    mz, m1, m2 = k % 4, (k // 4) % 2, k // 8
    low = jnp.where(core == 0, m1 + 2 * m2, 2 * m1 + m2)
    return place ^ (4 * mz + low)


def entry_of(place, core, piece):
    apart = piece ^ place
    mz, x, y = apart // 4, apart % 2, (apart // 2) % 2
    return mz + jnp.where(core == 0, 4 * x + 8 * y, 4 * y + 8 * x)


def gate_kernel(*refs):
    pass


def gate(values, after):
    return pl.pallas_call(
        gate_kernel,
        in_specs=[ANY] * (1 + len(after)),
        out_specs=ANY,
        out_shape=shape(values.shape, values.dtype),
        input_output_aliases={0: 0},
        name="gate",
    )(values, *after)


def stack_kernel(*refs):
    up, down = refs[-2:]
    rows, wide = up.shape[1:]
    half = down.shape[2]
    for i in range(4):
        up[i] = refs[i][:, :wide]
        for j in range(down.shape[1] // rows):
            down[i, rows * j : rows * (j + 1)] = refs[i][:, wide + half * j : wide + half * (j + 1)]


def stack_four(parts, half, after):
    rows = parts[0].shape[0]
    dims = [(4, rows, 5 * half), (4, 4 * rows, half)]
    return pl.pallas_call(
        stack_kernel,
        in_specs=[whole(parts[0].shape)] * 4 + [ANY] * len(after),
        out_specs=[whole(d) for d in dims],
        out_shape=[shape(d, LOW) for d in dims],
        grid=(1,),
        compiler_params=params(),
        name="stack",
    )(*parts, *after)


def line_parts(piece):
    return [piece] + [z_swap(piece, m) for m in (1, 2, 3)]


class Gather:
    def __init__(self, first):
        self.first = first
        self.beside = plane_swap(first, 0)

    def plane(self, after=()):
        if after:
            self.beside = gate(self.beside, after)
        self.second = jnp.concatenate([self.first, self.beside])
        self.third = plane_swap(self.second, 1)
        self.other = swap_cores(self.second)
        return self.second

    def finish(self, after=()):
        if after:
            self.third = gate(self.third, after)
        self.stacks = [self.second, self.third, self.other, swap_cores(self.third)]
        return self.third


def add_low(*parts):
    return sum(p.astype(FULL) for p in parts).astype(LOW)


class Scatter:
    def __init__(self, pair):
        self.mine = pair[0]
        self.came = swap_cores(pair[1])

    def both(self, i):
        return self.mine[4 * i : 4 * i + 4], self.came[4 * i : 4 * i + 4]

    def cores(self):
        self.far, self.near = add_low(*self.both(3)), add_low(*self.both(2))
        self.far_came = plane_swap(self.far, 1)
        return self.far

    def relay(self, after=()):
        if after:
            self.far_came = gate(self.far_came, after)
        self.relayed = add_low(*self.both(1), self.far_came)
        self.relay_came = plane_swap(self.relayed, 0)
        self.near_came = plane_swap(gate(self.near, (self.relayed,)), 1)
        return self.relayed

    def plane(self):
        self.total = add_low(*self.both(0), self.near_came, self.relay_came)
        self.parts = [z_swap(self.total[m], m) for m in (1, 2, 3)]
        return self.total

    def line(self, after=()):
        if after:
            self.parts[0] = gate(self.parts[0], after)
        return self.total[0].astype(FULL) + sum(p.astype(FULL) for p in self.parts)


def half_of(values, which, axis=1):
    width = values.shape[axis] // 2
    return lax.dynamic_slice_in_dim(values, which * width, width, axis)


def join_halves(mine, core):
    other = swap_cores(mine)
    return jnp.where(
        core == 0, jnp.concatenate([mine, other], axis=1), jnp.concatenate([other, mine], axis=1)
    )


def copies_of(table, stacks, rows, width, skip, target, column_stride, sem):
    copies = []
    for half in range(2):
        for k in range(PIECES):
            row = pl.multiple_of(table[half, k] * rows, 16)
            column = pl.multiple_of(table[2, half] * column_stride, LANES)
            copies.append(
                pltpu.make_async_copy(
                    stacks[2 * half + k // 8].at[k % 8, :, pl.ds(skip, width)],
                    target.at[pl.ds(row, rows), pl.ds(column, width)],
                    sem,
                )
            )
    return copies


def start(copies):
    for copy in copies:
        copy.start()


def wait(copies):
    for copy in copies:
        copy.wait()


def head_mask(h, dims):
    lane = lax.broadcasted_iota(jnp.int32, dims, 1)
    return (lane >= HEAD_DIM * h) & (lane < HEAD_DIM * (h + 1))


def spread(vec, count, at):
    rows = vec.shape[0] // PIECES
    runs = [
        vec[rows * p : rows * (p + 1), at + j : at + j + 1] for p in range(PIECES) for j in range(count)
    ]
    tall = jnp.concatenate(runs, axis=0)
    return jnp.broadcast_to(tall, (tall.shape[0], LANES)).T[0:1]


def group_copies(table, stacks, rows, at, target, sem):
    copies = []
    wide = 3 * LANES
    for half in range(2):
        for k in range(PIECES):
            row = pl.multiple_of(table[half, k] * rows, 16)
            column = pl.multiple_of(table[2, half] * wide, LANES)
            copies.append(
                pltpu.make_async_copy(
                    stacks[2 * half + k // 8].at[k % 8, :, pl.ds(at * wide, wide)],
                    target.at[pl.ds(row, rows), pl.ds(column, wide)],
                    sem,
                )
            )
    return copies


def thirds(values):
    return [
        jnp.concatenate([values[:, i * LANES : (i + 1) * LANES], values[:, (i + 3) * LANES : (i + 4) * LANES]], axis=1)
        for i in range(3)
    ]


def attend_kernel(group, table, lengths, tokens, *rest):
    stacks, rest = rest[:4], rest[4:]
    weight, vec, bias, sem = rest[-4:]
    rest = rest[:-4]
    if group == 0:
        vectors, wide_bias = rest[-2:]
        rest = rest[:-2]
    else:
        wide_bias, rest = rest[0], rest[1:]
    q_out, k_out, v_out, e_out, attended, attended_full, inv_out = rest[-7:]
    seq = pl.program_id(0)
    width = weight.shape[0]
    rows = width // PIECES

    @pl.when(seq == 0)
    def _():
        large = group_copies(table, stacks, rows, group, weight, sem.at[1])
        if group == 0:
            small = [
                pltpu.make_async_copy(
                    stacks[k // 8].at[k % 8, :, pl.ds(3 * width // 2, LANES)],
                    vec.at[pl.ds(pl.multiple_of(table[0, k] * rows, 16), rows)],
                    sem.at[0],
                )
                for k in range(PIECES)
            ]
            start(small)
        start(large)
        if group == 0:
            wait(small)
            values = vec[...].astype(FULL)
            vectors[...] = values.T[0:16]
            wide_bias[:, 0 : 2 * width] = spread(values, 2, 0)
            wide_bias[:, 2 * width :] = spread(values, 4, 8)
        bias[...] = jnp.zeros_like(bias)
        for i, at in ((0, 0), (2, width)):
            for half in range(2):
                bias[:, (i + 3 * half) * LANES : (i + 3 * half + 1) * LANES] = wide_bias[
                    :, at + group * GROUP + half * LANES : at + group * GROUP + (half + 1) * LANES
                ]
        wait(large)

    q, k, v = thirds((dot(tokens[...], weight[...]) + bias[...]).astype(LOW))
    q_out[...], k_out[...], v_out[...] = q, k, v
    scaled = q * LOW(0.125)
    dims = q.shape
    keep = lax.broadcasted_iota(jnp.int32, (1, dims[0]), 1) < lengths[seq]
    total = jnp.zeros(dims, FULL)
    inv = jnp.zeros(dims, FULL)
    for h in range(HEADS):
        mask = head_mask(h, dims)
        scores = jnp.where(keep, dot(scaled, jnp.where(mask, k, LOW(0)), NT), MASKED)
        exps = jnp.exp(scores - jnp.max(scores, axis=1, keepdims=True))
        row_total = jnp.sum(exps, axis=1, keepdims=True)
        low = exps.astype(LOW)
        e_out[h] = low
        total = total + dot(low, jnp.where(mask, v, LOW(0)))
        inv = jnp.where(mask, 1.0 / row_total, inv)
    result = total * inv
    inv_out[...] = inv
    attended_full[...] = result
    attended[...] = result.astype(LOW)


def attend(group, table, lengths, tokens, stacks, wide_bias=None, after=()):
    seqs, length, width = tokens.shape
    rows = seqs * length
    block = pl.BlockSpec((length, GROUP), lambda s, *_: (s, 0))
    given = [] if group == 0 else [wide_bias]
    return pl.pallas_call(
        functools.partial(attend_kernel, group),
        grid_spec=pltpu.PrefetchScalarGridSpec(
            num_scalar_prefetch=2,
            grid=(seqs,),
            in_specs=[pl.BlockSpec((length, width), lambda s, *_: (s, 0))]
            + [ANY] * 4
            + [whole(g.shape) for g in given]
            + [ANY] * len(after),
            out_specs=[block] * 3
            + [pl.BlockSpec((HEADS, length, length), lambda s, *_: (s, 0, 0))]
            + [block] * 3
            + ([whole((16, width)), whole((1, 6 * width))] if group == 0 else []),
            scratch_shapes=[
                pltpu.VMEM((width, 3 * GROUP), LOW),
                pltpu.VMEM((width, LANES), LOW),
                pltpu.VMEM((1, 3 * GROUP), FULL),
                pltpu.SemaphoreType.DMA((2,)),
            ],
        ),
        out_shape=[far((rows, GROUP), LOW)] * 3
        + [
            far((seqs * HEADS, length, length), LOW),
            far((rows, GROUP), LOW),
            far((rows, GROUP), FULL),
            far((rows, GROUP), FULL),
        ]
        + ([shape((16, width), FULL), shape((1, 6 * width), FULL)] if group == 0 else []),
        compiler_params=params(),
        cost_estimate=cost(1e6, 1e3),
        name=f"attend_{group}",
    )(table, lengths, tokens.reshape(rows, width), *stacks, *given, *after)


def widen_kernel(
    table, a0, a1, a2, tokens, vectors, wide_bias, *rest
):
    stacks = rest[:4]
    normed, standard, root, active, slope, out_weight, up_weight, sem = rest[-8:]
    width = out_weight.shape[0]
    rows, half = width // PIECES, width // 2
    first = pl.program_id(0) == 0
    small = copies_of(table, stacks, rows, half, 0, out_weight, half, sem.at[0])
    large = copies_of(table, stacks, rows, 4 * half, half, up_weight, 4 * half, sem.at[1])

    @pl.when(first)
    def _():
        start(small)
        start(large)
        wait(small)

    attended = jnp.concatenate([a0[...], a1[...], a2[...]], axis=1)
    values = tokens[...].astype(FULL) + dot(attended, out_weight[...]) + vectors[2:3]
    n, s = norm_parts(values)
    standard[...] = n
    root[...] = jnp.broadcast_to(s, root.shape)
    low = (n * vectors[3:4] + vectors[4:5]).astype(LOW)
    normed[...] = low

    @pl.when(first)
    def _():
        wait(large)

    for c in range(4):
        columns = slice(c * width, (c + 1) * width)
        hidden = dot(low, up_weight[:, columns]) + wide_bias[:, (c + 2) * width : (c + 3) * width]
        part = 0.5 * (1.0 + lax.erf(hidden * 0.7071067811865476))
        density = jnp.exp(-0.5 * hidden * hidden) * 0.3989422804014327
        active[:, columns] = (hidden * part).astype(LOW)
        slope[:, columns] = (part + hidden * density).astype(LOW)


def widen(table, attended, tokens, vectors, wide_bias, stacks):
    width = tokens.shape[2]
    rows = tokens.shape[0] * tokens.shape[1]
    row = lambda w: pl.BlockSpec((TILE, w), lambda i, *_: (i, 0))
    return pl.pallas_call(
        widen_kernel,
        grid_spec=pltpu.PrefetchScalarGridSpec(
            num_scalar_prefetch=1,
            grid=(rows // TILE,),
            in_specs=[row(GROUP)] * 3
            + [row(width), whole(vectors.shape), whole(wide_bias.shape)]
            + [ANY] * 4,
            out_specs=[row(width), row(width), row(LANES), row(4 * width), row(4 * width)],
            scratch_shapes=[
                pltpu.VMEM((width, width), LOW),
                pltpu.VMEM((width, 4 * width), LOW),
                pltpu.SemaphoreType.DMA((2,)),
            ],
        ),
        out_shape=[
            far((rows, width), LOW),
            far((rows, width), FULL),
            far((rows, LANES), FULL),
            far((rows, 4 * width), LOW),
            far((rows, 4 * width), LOW),
        ],
        compiler_params=params(),
        cost_estimate=cost(12e9, 30e6),
        name="widen",
    )(table, *attended, tokens.reshape(rows, width), vectors, wide_bias, *stacks)


def narrow_kernel(
    table, active, slope, normed, standard, root, cotangent, vectors, *rest
):
    ups, downs = rest[:4], rest[4:8]
    output, branch_two, pre_grad, branch_one, attended_grad, sums, up_sum = rest[8:15]
    out_weight, up_weight, down_weight, sem = rest[15:]
    width = out_weight.shape[0]
    rows, half = width // PIECES, width // 2
    first = pl.program_id(0) == 0
    out_copies = copies_of(table, ups, rows, half, 0, out_weight, half, sem.at[0])
    up_copies = copies_of(table, ups, rows, 4 * half, half, up_weight, 4 * half, sem.at[1])
    down_copies = copies_of(table, downs, 4 * rows, half, 0, down_weight, half, sem.at[2])

    @pl.when(first)
    def _():
        start(down_copies)
        start(up_copies)
        start(out_copies)
        sums[...] = jnp.zeros_like(sums)
        up_sum[...] = jnp.zeros_like(up_sum)
        wait(down_copies)

    values = normed[...].astype(FULL) + dot(active[...], down_weight[...]) + vectors[5:6]
    n2, s2 = norm_parts(values)
    output[...] = (n2 * vectors[6:7] + vectors[7:8]).astype(LOW)
    grad = cotangent[...].astype(FULL)
    second = norm_back(grad, n2, s2, vectors[6:7])
    low = second.astype(LOW)
    branch_two[...] = low
    sums[0:1] += column_sum(grad * n2)
    sums[1:2] += column_sum(grad)
    sums[2:3] += column_sum(low.astype(FULL))

    @pl.when(first)
    def _():
        wait(up_copies)

    normed_grad = second
    for c in range(4):
        columns = slice(c * width, (c + 1) * width)
        part = (dot(low, down_weight[columns], NT) * slope[:, columns].astype(FULL)).astype(LOW)
        pre_grad[:, columns] = part
        up_sum[:, columns] += column_sum(part.astype(FULL))
        normed_grad = normed_grad + dot(part, up_weight[:, columns], NT)
    n1 = standard[...]
    sums[3:4] += column_sum(normed_grad * n1)
    sums[4:5] += column_sum(normed_grad)
    low = norm_back(normed_grad, n1, root[:, 0:1], vectors[3:4]).astype(LOW)
    branch_one[...] = low
    sums[5:6] += column_sum(low.astype(FULL))

    @pl.when(first)
    def _():
        wait(out_copies)

    attended_grad[...] = dot(low, out_weight[...], NT).astype(LOW)


def narrow(table, active, slope, normed, standard, root, cotangent, vectors, ups, downs):
    rows, width = normed.shape
    row = lambda w: pl.BlockSpec((TILE, w), lambda i, *_: (i, 0))
    return pl.pallas_call(
        narrow_kernel,
        grid_spec=pltpu.PrefetchScalarGridSpec(
            num_scalar_prefetch=1,
            grid=(rows // TILE,),
            in_specs=[row(4 * width), row(4 * width), row(width), row(width), row(LANES), row(width)]
            + [whole(vectors.shape)]
            + [ANY] * 8,
            out_specs=[row(width), row(width), row(4 * width), row(width), row(width)]
            + [whole((8, width)), whole((1, 4 * width))],
            scratch_shapes=[
                pltpu.VMEM((width, width), LOW),
                pltpu.VMEM((width, 4 * width), LOW),
                pltpu.VMEM((4 * width, width), LOW),
                pltpu.SemaphoreType.DMA((3,)),
            ],
        ),
        out_shape=[
            far((rows, width), LOW),
            far((rows, width), LOW),
            far((rows, 4 * width), LOW),
            far((rows, width), LOW),
            far((rows, width), LOW),
            shape((8, width), FULL),
            shape((1, 4 * width), FULL),
        ],
        compiler_params=params(),
        cost_estimate=cost(24e9, 40e6),
        name="narrow",
    )(
        table,
        *(keep_far(values) for values in (active, slope, normed, standard, root, cotangent.reshape(rows, width))),
        vectors,
        *ups,
        *downs,
    )


def down_grad_kernel(order, active, branch_two, mine, theirs):
    step = pl.program_id(0)
    width = branch_two.shape[1]
    rows, half = 4 * width // PIECES, width // 2
    result = dot(active[...], branch_two[...], TN).astype(LOW)
    for p in range(4):
        block = result[rows * p : rows * (p + 1)]
        core = order[2, 0]

        @pl.when(core == 0)
        def _():
            mine[order[0, 4 * step + p]] = block[:, :half]
            theirs[order[1, 4 * step + p]] = block[:, half:]

        @pl.when(core == 1)
        def _():
            mine[order[0, 4 * step + p]] = block[:, half:]
            theirs[order[1, 4 * step + p]] = block[:, :half]


def down_grad(order, active, branch_two):
    rows, width = branch_two.shape
    stack = (PIECES, 4 * width // PIECES, width // 2)
    return pl.pallas_call(
        down_grad_kernel,
        grid_spec=pltpu.PrefetchScalarGridSpec(
            num_scalar_prefetch=1,
            grid=(4,),
            in_specs=[pl.BlockSpec((rows, width), lambda i, *_: (0, i)), whole((rows, width))],
            out_specs=[whole(stack)] * 2,
        ),
        out_shape=[shape(stack, LOW)] * 2,
        compiler_params=params(),
        cost_estimate=cost(7e9, 14e6),
        name="down_grad",
    )(order, keep_far(active), keep_far(branch_two))


def put_pieces(order, result, mine, theirs, to_mine, at):
    rows = result.shape[0] // PIECES
    width = result.shape[1]
    for p in range(PIECES):
        block = result[rows * p : rows * (p + 1)]

        @pl.when(to_mine)
        def _():
            mine[order[0, p], :, at : at + width] = block

        @pl.when(jnp.logical_not(to_mine))
        def _():
            theirs[order[1, p], :, at : at + width] = block


def up_grad_kernel(order, normed, pre_grad, a0, a1, a2, branch_one, sums, up_sum, *rest):
    mine, theirs = rest[-2:]
    step = pl.program_id(0)
    width = normed.shape[1]
    half = width // 2
    core = order[2, 0]

    @pl.when(step < 4)
    def _():
        result = dot(normed[...], pre_grad[...], TN).astype(LOW)
        for part in range(2):

            @pl.when(step % 2 == part)
            def _():
                put_pieces(order, result, mine, theirs, step // 2 == core, half + part * width)

    @pl.when(step == 4)
    def _():
        attended = jnp.concatenate([a0[...], a1[...], a2[...]], axis=1)
        result = dot(attended, branch_one[...], TN).astype(LOW)
        for c in range(2):
            put_pieces(order, result[:, c * half : (c + 1) * half], mine, theirs, core == c, 0)

    @pl.when(step == 0)
    def _():
        rows = width // PIECES
        lane = lax.broadcasted_iota(jnp.int32, (rows, LANES), 1)
        ones = jnp.concatenate([sums[...], jnp.zeros((LANES - 8, width), FULL)], axis=0).T
        up = [tall(up_sum[:, i * width : (i + 1) * width]) for i in range(4)]
        for p in range(PIECES):
            block = run_columns(ones[rows * p : rows * (p + 1)], lane, up, p, 4, 8).astype(LOW)
            mine[order[0, p], :, 5 * half :] = block
            theirs[order[1, p], :, 5 * half :] = block


def up_grad(order, normed, pre_grad, attended, branch_one, sums, up_sum, after=()):
    rows, width = normed.shape
    stack = (PIECES, width // PIECES, 5 * width // 2 + LANES)
    return pl.pallas_call(
        up_grad_kernel,
        grid_spec=pltpu.PrefetchScalarGridSpec(
            num_scalar_prefetch=1,
            grid=(5,),
            in_specs=[
                whole((rows, width)),
                pl.BlockSpec((rows, width), lambda i, *_: (0, jnp.minimum(i, 3))),
            ]
            + [whole((rows, GROUP))] * 3
            + [whole((rows, width)), whole(sums.shape), whole(up_sum.shape)]
            + [ANY] * len(after),
            out_specs=[whole(stack)] * 2,
        ),
        out_shape=[shape(stack, LOW)] * 2,
        compiler_params=params(),
        cost_estimate=cost(9e9, 18e6),
        name="up_grad",
    )(order, keep_far(normed), keep_far(pre_grad), *attended, branch_one, sums, up_sum, *after)


def attend_back_kernel(q_in, k_in, v_in, e_in, attended_full, inv_in, grad_in, *rest):
    out, sums = rest[-2:]
    seq = pl.program_id(0)
    q, k, v = q_in[...] * LOW(0.125), k_in[...], v_in[...]
    dims = q.shape
    grad = (grad_in[...].astype(FULL) * inv_in[...]).astype(LOW)
    along = grad.astype(FULL) * attended_full[...]
    q_total, k_total, v_total = (jnp.zeros(dims, FULL) for _ in range(3))
    for h in range(HEADS):
        mask = head_mask(h, dims)
        masked = lambda values: jnp.where(mask, values, LOW(0))
        exps = e_in[h]
        shift = jnp.sum(jnp.where(mask, along, 0.0), axis=1, keepdims=True)
        score = (exps.astype(FULL) * (dot(grad, masked(v), NT) - shift)).astype(LOW)
        q_total = q_total + dot(score, masked(k))
        k_total = k_total + dot(score, masked(q), TN)
        v_total = v_total + dot(exps, masked(grad), TN)
    parts = [(q_total * 0.125).astype(LOW), k_total.astype(LOW), v_total.astype(LOW)]
    for half in range(2):
        for i in range(3):
            at = (i + 3 * half) * LANES
            out[:, at : at + LANES] = parts[i][:, half * LANES : (half + 1) * LANES]
    both = jnp.concatenate([column_sum(parts[i].astype(FULL)) for i in (0, 2)], axis=0)

    @pl.when(seq == 0)
    def _():
        sums[0:2] = both

    @pl.when(seq != 0)
    def _():
        sums[0:2] += both


def attend_back(group, q, k, v, exps, attended_full, inv, grad, length, after=()):
    rows = q.shape[0]
    seqs = rows // length
    block = pl.BlockSpec((length, GROUP), lambda s: (s, 0))
    return pl.pallas_call(
        attend_back_kernel,
        grid=(seqs,),
        in_specs=[block] * 3
        + [pl.BlockSpec((HEADS, length, length), lambda s: (s, 0, 0))]
        + [block] * 2
        + [pl.BlockSpec((length, GROUP), lambda s: (s, group))]
        + [ANY] * len(after),
        out_specs=[pl.BlockSpec((length, 3 * GROUP), lambda s: (s, 0)), pl.BlockSpec((8, GROUP), lambda s: (0, 0))],
        out_shape=[shape((rows, 3 * GROUP), LOW), shape((8, GROUP), FULL)],
        compiler_params=params(),
        cost_estimate=cost(6e9, 10e6),
        name=f"attend_back_{group}",
    )(*(keep_far(values) for values in (q, k, v, exps, attended_full, inv)), grad, *after)


def tall(row):
    return jnp.broadcast_to(row, (LANES, row.shape[1])).T


def run_columns(block, lane, columns, piece, count, at):
    rows = block.shape[0]
    for j in range(count):
        run = count * piece + j
        first = rows * (run % PIECES)
        block = jnp.where(lane == at + j, columns[run // PIECES][first : first + rows], block)
    return block


def qkv_grad_kernel(order, tokens, g0, g1, g2, r0, r1, r2, *rest):
    mine, theirs = rest[-2:]
    step = pl.program_id(0)
    width = tokens.shape[1]
    half = width // 2
    core = order[2, 0]
    for i, grads in enumerate((g0, g1, g2)):

        @pl.when(step == i)
        def _():
            result = dot(tokens[...], grads[...], TN).astype(LOW)
            for c in range(2):
                put_pieces(order, result[:, c * half : (c + 1) * half], mine, theirs, core == c, i * half)

    @pl.when(step == 0)
    def _():
        rows = width // PIECES
        lane = lax.broadcasted_iota(jnp.int32, (rows, LANES), 1)
        qv_sums = jnp.concatenate([r0[...], r1[...], r2[...]], axis=1)
        qv = [tall(qv_sums[i : i + 1]) for i in range(2)]
        for p in range(PIECES):
            block = run_columns(jnp.zeros((rows, LANES), FULL), lane, qv, p, 2, 0).astype(LOW)
            mine[order[0, p], :, 3 * half :] = block
            theirs[order[1, p], :, 3 * half :] = block


def qkv_grad(order, tokens, grads, qv_sums, after=()):
    rows = grads[0].shape[0]
    width = tokens.shape[2]
    half = width // 2
    stack = (PIECES, width // PIECES, 3 * half + LANES)
    return pl.pallas_call(
        qkv_grad_kernel,
        grid_spec=pltpu.PrefetchScalarGridSpec(
            num_scalar_prefetch=1,
            grid=(3,),
            in_specs=[whole((rows, width))]
            + [whole((rows, 3 * GROUP))] * 3
            + [whole((8, GROUP))] * 3
            + [ANY] * len(after),
            out_specs=[whole(stack)] * 2,
        ),
        out_shape=[shape(stack, LOW)] * 2,
        compiler_params=params(),
        cost_estimate=cost(6e9, 14e6),
        name="qkv_grad",
    )(order, tokens.reshape(rows, width), *grads, *qv_sums, *after)


def token_grad_kernel(table, g0, g1, g2, first, *rest):
    out, w0, w1, w2, sem = rest[-5:]
    width = out.shape[1]
    rows = width // PIECES
    weights = (w0, w1, w2)
    copies = [
        group_copies(table, rest[:4], rows, i, weights[i], sem.at[i]) for i in range(3)
    ]
    begin = pl.program_id(0) == 0

    @pl.when(begin)
    def _():
        for i in range(3):
            start(copies[i])

    total = first[...].astype(FULL)
    for i, grads in enumerate((g0, g1, g2)):

        @pl.when(begin)
        def _():
            wait(copies[i])

        total = total + dot(grads[...], weights[i][...], NT)
    out[...] = total.astype(LOW)


def token_grad(table, grads, first, stacks, after=()):
    rows, width = first.shape
    row = lambda w: pl.BlockSpec((TILE, w), lambda i, *_: (i, 0))
    return pl.pallas_call(
        token_grad_kernel,
        grid_spec=pltpu.PrefetchScalarGridSpec(
            num_scalar_prefetch=1,
            grid=(rows // TILE,),
            in_specs=[row(3 * GROUP)] * 3 + [row(width)] + [ANY] * (4 + len(after)),
            out_specs=row(width),
            scratch_shapes=[pltpu.VMEM((width, 3 * GROUP), LOW)] * 3 + [pltpu.SemaphoreType.DMA((3,))],
        ),
        out_shape=shape((rows, width), LOW),
        compiler_params=params(),
        cost_estimate=cost(6e9, 12e6),
        name="token_grad",
    )(table, *grads, first, *stacks, *after)


def heads_in_kernel(at, weight, packed, out):
    groups = weight.shape[1] // (3 * GROUP)
    for g in range(groups):
        for i in range(3):
            first = (i * groups + g) * GROUP
            out[:, (3 * g + i) * LANES : (3 * g + i + 1) * LANES] = jnp.where(
                at[0] == 0, weight[:, first : first + LANES], weight[:, first + LANES : first + GROUP]
            )
    out[:, 3 * groups * LANES :] = packed[...]


def heads_in(core, weight, packed):
    rows, columns = weight.shape
    dims = (rows, columns // 2 + LANES)
    return pl.pallas_call(
        heads_in_kernel,
        grid_spec=pltpu.PrefetchScalarGridSpec(
            num_scalar_prefetch=1,
            grid=(1,),
            in_specs=[whole(weight.shape), whole(packed.shape)],
            out_specs=whole(dims),
        ),
        out_shape=shape(dims, LOW),
        name="heads_in",
    )(core.reshape(1), weight, packed)


def heads_out_kernel(at, mine, other, out):
    groups = out.shape[1] // (3 * GROUP)
    for g in range(groups):
        for i in range(3):
            first = (i * groups + g) * GROUP
            columns = slice((3 * g + i) * LANES, (3 * g + i + 1) * LANES)
            left, right = mine[:, columns], other[:, columns]
            out[:, first : first + LANES] = jnp.where(at[0] == 0, left, right)
            out[:, first + LANES : first + GROUP] = jnp.where(at[0] == 0, right, left)


def heads_out(core, mine, other):
    rows, columns = mine.shape
    dims = (rows, 2 * columns)
    return pl.pallas_call(
        heads_out_kernel,
        grid_spec=pltpu.PrefetchScalarGridSpec(
            num_scalar_prefetch=1,
            grid=(1,),
            in_specs=[whole(mine.shape)] * 2,
            out_specs=whole(dims),
        ),
        out_shape=shape(dims, FULL),
        name="heads_out",
    )(core.reshape(1), mine, other)


def pack(vectors, rows):
    columns = jnp.concatenate([v.reshape(-1, rows) for v in vectors], axis=0).T
    return jnp.pad(columns, ((0, 0), (0, LANES - columns.shape[1])))


def pack_all(chips, rows, qv, out_bias, gain_one, shift_one, up_bias, down_bias, gain_two, shift_two):
    parts = (qv, out_bias, gain_one, shift_one, down_bias, gain_two, shift_two, up_bias)
    if chips == 1:
        return pack(parts, rows)
    return jnp.concatenate(
        [pack([v.reshape(chips, -1)[p] for v in parts], rows) for p in range(chips)], axis=0
    )


def shards(
    chips,
    tokens,
    lengths,
    query_key_value_weight,
    qv_bias,
    output_projection_weight,
    output_projection_bias,
    gain_one,
    shift_one,
    widening_matrix,
    widening_offset_vector,
    down_projection_weight,
    down_projection_bias,
    gain_two,
    shift_two,
    cotangent,
):
    seq_count, seq_length, width = tokens.shape
    core, place = lax.axis_index("dp"), lax.axis_index("fsdp")
    rows = query_key_value_weight.shape[0]
    small = (
        qv_bias,
        output_projection_bias,
        gain_one,
        shift_one,
        widening_offset_vector,
        down_projection_bias,
        gain_two,
        shift_two,
    )
    direct = chips == PIECES
    numbers = jnp.arange(PIECES)
    if direct:
        half = width // 2
        down_in = half_of(down_projection_weight, core)
        ffn_in = jnp.concatenate(
            [half_of(output_projection_weight, core), half_of(widening_matrix, core)]
            + [down_in[rows * j : rows * (j + 1)] for j in range(4)],
            axis=1,
        )
        qkv_set = Gather(jnp.stack(line_parts(heads_in(core, query_key_value_weight, pack_all(1, rows, *small)))))
        qkv_set.plane()
        qkv_set.finish()
        up_first, down_first = stack_four(line_parts(ffn_in), half, (qkv_set.third,))
        up_set, down_set = Gather(up_first), Gather(down_first)
        owners = [piece_of(place, c, numbers) for c in (core, 1 - core)]
        entries = [entry_of(place, c, numbers) for c in (core, 1 - core)]
    else:
        gather = lambda values: lax.all_gather(values, "fsdp", axis=0, tiled=True)
        packed = pack_all(PIECES, width // PIECES, *(gather(v) for v in small))

        def stacks_of(make):
            both = [make(c) for c in (core, 1 - core)]
            both = [values.reshape(2, 8, -1, values.shape[1]) for values in both]
            return [values[i] for values in both for i in range(2)]

        full_qkv, full_out = gather(query_key_value_weight), gather(output_projection_weight)
        full_up, full_down = gather(widening_matrix), gather(down_projection_weight)
        qkv_stacks = stacks_of(lambda c: heads_in(c, full_qkv, packed))
        up_set = stacks_of(lambda c: jnp.concatenate([half_of(full_out, c), half_of(full_up, c)], axis=1))
        down_set = stacks_of(lambda c: half_of(full_down, c))
        owners = entries = [numbers, numbers]
    cores = jnp.where(numbers == 1, 1 - core, core)
    table = jnp.stack(owners + [cores]).astype(jnp.int32)
    order = jnp.stack(entries + [cores]).astype(jnp.int32)

    groups = range(width // GROUP)
    parts, wide_bias = [], None
    if direct:
        qkv_stacks = qkv_set.stacks
        *made, vectors, wide_bias = attend(0, table, lengths, tokens, qkv_stacks, None, (up_set.first,))
        parts.append(made)
        done = made[4]
        after = (done, up_set.plane((done,)))
        parts.append(attend(1, table, lengths, tokens, qkv_stacks, wide_bias, after))
        done = parts[1][4]
        after = (done, down_set.plane((done,)))
        parts.append(attend(2, table, lengths, tokens, qkv_stacks, wide_bias, after))
        up_set.finish((parts[2][4],))
        up_set = up_set.stacks
    else:
        for g in groups:
            made = attend(g, table, lengths, tokens, qkv_stacks, wide_bias)
            if g == 0:
                *made, vectors, wide_bias = made
            parts.append(made)
    attended = [part[4] for part in parts]
    normed, standard, root, active, slope = widen(table, attended, tokens, vectors, wide_bias, up_set)
    if direct:
        down_set.finish((normed,))
        down_set = down_set.stacks
    output, branch_two, pre_grad, branch_one, attended_grad, sums, up_sum = narrow(
        table, active, slope, normed, standard, root, cotangent, vectors, up_set, down_set
    )
    half = width // 2
    reduces = []

    def reduce_begin(pair):
        if direct:
            reduces.append(Scatter(pair))
        else:
            both = pair[0].astype(FULL) + swap_cores(pair[1]).astype(FULL)
            reduces.append(both.reshape(-1, both.shape[2]))

    def reduce_step(i, step):
        return (getattr(reduces[i], step)(),) if direct else ()

    def back(g, after):
        q, k, v, exps, _, attended_full, inv = parts[g]
        return attend_back(g, q, k, v, exps, attended_full, inv, attended_grad, seq_length, after)

    down_pair = down_grad(order, active, branch_two)
    reduce_begin(down_pair)
    up_pair = up_grad(
        order, normed, pre_grad, attended, branch_one, sums, up_sum, (down_pair[0],)
    )
    reduce_begin(up_pair)
    grad_0, part_0 = back(0, (up_pair[0],) + reduce_step(0, "cores"))
    grad_1, part_1 = back(1, (grad_0,) + reduce_step(0, "relay") + reduce_step(1, "cores"))
    grad_2, part_2 = back(2, (grad_1,) + reduce_step(0, "plane") + reduce_step(1, "relay"))
    grads = (grad_0, grad_1, grad_2)
    if direct:
        down_sum = reduces[0].line()
        later = (down_sum, reduces[1].plane())
    else:
        later = ()
    qkv_pair = qkv_grad(order, tokens, grads, (part_0, part_1, part_2), later)
    reduce_begin(qkv_pair)
    later = ()
    if direct:
        far = reduces[2].cores()
        up_total = reduces[1].line((far,))
        reduces[2].relay((up_total,))
        later = (reduces[2].plane(),)
    grad_tokens = token_grad(table, grads, branch_one, qkv_stacks, (qkv_pair[0],) + later)
    if direct:
        qkv_sum = reduces[2].line()
        up_vec, qkv_vec = up_total[:, 5 * half :], qkv_sum[:, 3 * half :]

        def vec_columns(at, count):
            values = (up_vec if at < 12 else qkv_vec)
            return values[:, at % 12 : at % 12 + count].T.reshape(-1)

    else:

        def reduce(values):
            return lax.psum_scatter(values, "fsdp", scatter_dimension=0, tiled=True)

        def vec_columns(at, count):
            values = reduces[1][:, 5 * half :] if at < 12 else reduces[2][:, 3 * half :]
            values = values.reshape(PIECES, -1, LANES)[:, :, at % 12 : at % 12 + count]
            return reduce(values.transpose(0, 2, 1).reshape(-1))

        down_sum = reduce(reduces[0])
        up_total, qkv_sum = reduce(reduces[1][:, : 5 * half]), reduce(reduces[2][:, : 3 * half])
    qkv_sum = qkv_sum[:, : 3 * half]
    out_sum, up_total = up_total[:, :half], up_total[:, half : 5 * half]
    return (
        output.reshape(tokens.shape),
        grad_tokens.reshape(tokens.shape),
        heads_out(core, qkv_sum, swap_cores(qkv_sum)),
        vec_columns(12, 2),
        join_halves(out_sum, core),
        vec_columns(5, 1),
        vec_columns(3, 1),
        vec_columns(4, 1),
        join_halves(up_total, core),
        vec_columns(8, 4),
        join_halves(down_sum, core),
        vec_columns(2, 1),
        vec_columns(0, 1),
        vec_columns(1, 1),
    )


def solution(mesh):
    tokens, lengths = P(("dp", "fsdp"), None, None), P(("dp", "fsdp"))
    matrix, vector = P("fsdp", None), P("fsdp")
    return jax.shard_map(
        functools.partial(shards, mesh.shape["fsdp"]),
        mesh=mesh,
        in_specs=(
            tokens, lengths, matrix, vector, matrix, vector, vector, vector,
            matrix, vector, matrix, vector, vector, vector, tokens,
        ),
        out_specs=(
            tokens, tokens, matrix, vector, matrix, vector, vector, vector,
            matrix, vector, matrix, vector, vector, vector,
        ),
        check_vma=False,
    )
```

```python
import functools

import jax
import jax.numpy as jnp
from jax import lax
from jax.experimental import pallas as pl
from jax.experimental.pallas import tpu as pltpu
from jax.sharding import PartitionSpec as P

HEAD_DIM = 64
GROUP = 256
HEADS = GROUP // HEAD_DIM
LANES = 128
PIECES = 16
TILE = 256
EPSILON = 1e-12
MASKED = -1e30
VMEM = 60 << 20
NN = (((1,), (0,)), ((), ()))
NT = (((1,), (1,)), ((), ()))
TN = (((0,), (0,)), ((), ()))
LOW, FULL = jnp.bfloat16, jnp.float32
ANY = pl.BlockSpec(memory_space=pl.ANY)


def dot(left, right, dims=NN):
    return lax.dot_general(left, right, dims, preferred_element_type=FULL)


def shape(dims, dtype):
    return jax.ShapeDtypeStruct(dims, dtype)


def whole(dims):
    return pl.BlockSpec(dims, lambda *at: (0,) * len(dims))


def params():
    return pltpu.CompilerParams(vmem_limit_bytes=VMEM)


def cost(flops, moved, exps=0):
    return pl.CostEstimate(flops=int(flops), bytes_accessed=int(moved), transcendentals=int(exps))


def norm_parts(values):
    centred = values - jnp.mean(values, axis=-1, keepdims=True)
    inv_root = lax.rsqrt(jnp.mean(centred * centred, axis=-1, keepdims=True) + EPSILON)
    return centred * inv_root, inv_root


def norm_back(grad_in, standard, inv_root, gain_vec):
    scaled = grad_in * gain_vec
    return inv_root * (
        scaled
        - jnp.mean(scaled, axis=-1, keepdims=True)
        - standard * jnp.mean(scaled * standard, axis=-1, keepdims=True)
    )


def column_sum(values):
    return jnp.sum(values, axis=0, keepdims=True)


def swap_cores(values):
    return lax.ppermute(values, "dp", [(0, 1), (1, 0)])


def plane_swap(values, step):
    first, second = (1, 2) if step == 0 else (2, 1)
    pairs = [(i, i ^ first) for i in range(16)] + [(16 + i, 16 + (i ^ second)) for i in range(16)]
    return lax.ppermute(values, ("dp", "fsdp"), pairs)


def z_swap(values, m):
    return lax.ppermute(values, "fsdp", [(i, i ^ (4 * m)) for i in range(16)])


def piece_of(place, core, k):
    mz, m1, m2 = k % 4, (k // 4) % 2, k // 8
    low = jnp.where(core == 0, m1 + 2 * m2, 2 * m1 + m2)
    return place ^ (4 * mz + low)


def entry_of(place, core, piece):
    apart = piece ^ place
    mz, x, y = apart // 4, apart % 2, (apart // 2) % 2
    return mz + jnp.where(core == 0, 4 * x + 8 * y, 4 * y + 8 * x)


def gate_kernel(*refs):
    pass


def gate(values, after):
    return pl.pallas_call(
        gate_kernel,
        in_specs=[ANY] * (1 + len(after)),
        out_specs=ANY,
        out_shape=shape(values.shape, values.dtype),
        input_output_aliases={0: 0},
        name="gate",
    )(values, *after)


def stack_kernel(*refs):
    up, down = refs[-2:]
    rows, wide = up.shape[1:]
    half = down.shape[2]
    for i in range(4):
        up[i] = refs[i][:, :wide]
        for j in range(down.shape[1] // rows):
            down[i, rows * j : rows * (j + 1)] = refs[i][:, wide + half * j : wide + half * (j + 1)]


def stack_four(parts, half, after):
    rows = parts[0].shape[0]
    dims = [(4, rows, 5 * half), (4, 4 * rows, half)]
    return pl.pallas_call(
        stack_kernel,
        in_specs=[whole(parts[0].shape)] * 4 + [ANY] * len(after),
        out_specs=[whole(d) for d in dims],
        out_shape=[shape(d, LOW) for d in dims],
        grid=(1,),
        compiler_params=params(),
        name="stack",
    )(*parts, *after)


def line_parts(piece):
    return [piece] + [z_swap(piece, m) for m in (1, 2, 3)]


class Gather:
    def __init__(self, first):
        self.first = first
        self.beside = plane_swap(first, 0)

    def plane(self, after=()):
        if after:
            self.beside = gate(self.beside, after)
        self.second = jnp.concatenate([self.first, self.beside])
        self.third = plane_swap(self.second, 1)
        self.other = swap_cores(self.second)
        return self.second

    def finish(self, after=()):
        if after:
            self.third = gate(self.third, after)
        self.stacks = [self.second, self.third, self.other, swap_cores(self.third)]
        return self.third


def add_low(*parts):
    return sum(p.astype(FULL) for p in parts).astype(LOW)


class Scatter:
    def __init__(self, pair):
        self.mine = pair[0]
        self.came = swap_cores(pair[1])

    def both(self, i):
        return self.mine[4 * i : 4 * i + 4], self.came[4 * i : 4 * i + 4]

    def cores(self):
        self.far, self.near = add_low(*self.both(3)), add_low(*self.both(2))
        self.far_came = plane_swap(self.far, 1)
        return self.far

    def relay(self, after=()):
        if after:
            self.far_came = gate(self.far_came, after)
        self.relayed = add_low(*self.both(1), self.far_came)
        self.relay_came = plane_swap(self.relayed, 0)
        self.near_came = plane_swap(gate(self.near, (self.relayed,)), 1)
        return self.relayed

    def plane(self):
        self.total = add_low(*self.both(0), self.near_came, self.relay_came)
        self.parts = [z_swap(self.total[m], m) for m in (1, 2, 3)]
        return self.total

    def line(self, after=()):
        if after:
            self.parts[0] = gate(self.parts[0], after)
        return self.total[0].astype(FULL) + sum(p.astype(FULL) for p in self.parts)


def half_of(values, which, axis=1):
    width = values.shape[axis] // 2
    return lax.dynamic_slice_in_dim(values, which * width, width, axis)


def join_halves(mine, core):
    other = swap_cores(mine)
    return jnp.where(
        core == 0, jnp.concatenate([mine, other], axis=1), jnp.concatenate([other, mine], axis=1)
    )


def copies_of(table, stacks, rows, width, skip, target, column_stride, sem):
    copies = []
    for half in range(2):
        for k in range(PIECES):
            row = pl.multiple_of(table[half, k] * rows, 16)
            column = pl.multiple_of(table[2, half] * column_stride, LANES)
            copies.append(
                pltpu.make_async_copy(
                    stacks[2 * half + k // 8].at[k % 8, :, pl.ds(skip, width)],
                    target.at[pl.ds(row, rows), pl.ds(column, width)],
                    sem,
                )
            )
    return copies


def start(copies):
    for copy in copies:
        copy.start()


def wait(copies):
    for copy in copies:
        copy.wait()


def head_mask(h, dims):
    lane = lax.broadcasted_iota(jnp.int32, dims, 1)
    return (lane >= HEAD_DIM * h) & (lane < HEAD_DIM * (h + 1))


def spread(vec, count, at):
    rows = vec.shape[0] // PIECES
    runs = [
        vec[rows * p : rows * (p + 1), at + j : at + j + 1] for p in range(PIECES) for j in range(count)
    ]
    tall = jnp.concatenate(runs, axis=0)
    return jnp.broadcast_to(tall, (tall.shape[0], LANES)).T[0:1]


def group_copies(table, stacks, rows, at, target, sem):
    copies = []
    wide = 3 * LANES
    for half in range(2):
        for k in range(PIECES):
            row = pl.multiple_of(table[half, k] * rows, 16)
            column = pl.multiple_of(table[2, half] * wide, LANES)
            copies.append(
                pltpu.make_async_copy(
                    stacks[2 * half + k // 8].at[k % 8, :, pl.ds(at * wide, wide)],
                    target.at[pl.ds(row, rows), pl.ds(column, wide)],
                    sem,
                )
            )
    return copies


def thirds(values):
    return [
        jnp.concatenate([values[:, i * LANES : (i + 1) * LANES], values[:, (i + 3) * LANES : (i + 4) * LANES]], axis=1)
        for i in range(3)
    ]


def attend_kernel(group, table, lengths, tokens, *rest):
    stacks, rest = rest[:4], rest[4:]
    weight, vec, bias, sem = rest[-4:]
    rest = rest[:-4]
    if group == 0:
        vectors, wide_bias = rest[-2:]
        rest = rest[:-2]
    else:
        wide_bias, rest = rest[0], rest[1:]
    q_out, k_out, v_out, e_out, attended, attended_full, inv_out = rest[-7:]
    seq = pl.program_id(0)
    width = weight.shape[0]
    rows = width // PIECES

    @pl.when(seq == 0)
    def _():
        large = group_copies(table, stacks, rows, group, weight, sem.at[1])
        if group == 0:
            small = [
                pltpu.make_async_copy(
                    stacks[k // 8].at[k % 8, :, pl.ds(3 * width // 2, LANES)],
                    vec.at[pl.ds(pl.multiple_of(table[0, k] * rows, 16), rows)],
                    sem.at[0],
                )
                for k in range(PIECES)
            ]
            start(small)
        start(large)
        if group == 0:
            wait(small)
            values = vec[...].astype(FULL)
            vectors[...] = values.T[0:16]
            wide_bias[:, 0 : 2 * width] = spread(values, 2, 0)
            wide_bias[:, 2 * width :] = spread(values, 4, 8)
        bias[...] = jnp.zeros_like(bias)
        for i, at in ((0, 0), (2, width)):
            for half in range(2):
                bias[:, (i + 3 * half) * LANES : (i + 3 * half + 1) * LANES] = wide_bias[
                    :, at + group * GROUP + half * LANES : at + group * GROUP + (half + 1) * LANES
                ]
        wait(large)

    q, k, v = thirds((dot(tokens[...], weight[...]) + bias[...]).astype(LOW))
    q_out[...], k_out[...], v_out[...] = q, k, v
    scaled = q * LOW(0.125)
    dims = q.shape
    keep = lax.broadcasted_iota(jnp.int32, (1, dims[0]), 1) < lengths[seq]
    total = jnp.zeros(dims, FULL)
    inv = jnp.zeros(dims, FULL)
    for h in range(HEADS):
        mask = head_mask(h, dims)
        scores = jnp.where(keep, dot(scaled, jnp.where(mask, k, LOW(0)), NT), MASKED)
        exps = jnp.exp(scores - jnp.max(scores, axis=1, keepdims=True))
        row_total = jnp.sum(exps, axis=1, keepdims=True)
        low = exps.astype(LOW)
        e_out[h] = low
        total = total + dot(low, jnp.where(mask, v, LOW(0)))
        inv = jnp.where(mask, 1.0 / row_total, inv)
    result = total * inv
    inv_out[...] = inv
    attended_full[...] = result
    attended[...] = result.astype(LOW)


def attend(group, table, lengths, tokens, stacks, wide_bias=None, after=()):
    seqs, length, width = tokens.shape
    rows = seqs * length
    block = pl.BlockSpec((length, GROUP), lambda s, *_: (s, 0))
    given = [] if group == 0 else [wide_bias]
    return pl.pallas_call(
        functools.partial(attend_kernel, group),
        grid_spec=pltpu.PrefetchScalarGridSpec(
            num_scalar_prefetch=2,
            grid=(seqs,),
            in_specs=[pl.BlockSpec((length, width), lambda s, *_: (s, 0))]
            + [ANY] * 4
            + [whole(g.shape) for g in given]
            + [ANY] * len(after),
            out_specs=[block] * 3
            + [pl.BlockSpec((HEADS, length, length), lambda s, *_: (s, 0, 0))]
            + [block] * 3
            + ([whole((16, width)), whole((1, 6 * width))] if group == 0 else []),
            scratch_shapes=[
                pltpu.VMEM((width, 3 * GROUP), LOW),
                pltpu.VMEM((width, LANES), LOW),
                pltpu.VMEM((1, 3 * GROUP), FULL),
                pltpu.SemaphoreType.DMA((2,)),
            ],
        ),
        out_shape=[shape((rows, GROUP), LOW)] * 3
        + [
            shape((seqs * HEADS, length, length), LOW),
            shape((rows, GROUP), LOW),
            shape((rows, GROUP), FULL),
            shape((rows, GROUP), FULL),
        ]
        + ([shape((16, width), FULL), shape((1, 6 * width), FULL)] if group == 0 else []),
        compiler_params=params(),
        cost_estimate=cost(1e6, 1e3),
        name=f"attend_{group}",
    )(table, lengths, tokens.reshape(rows, width), *stacks, *given, *after)


def widen_kernel(
    table, a0, a1, a2, tokens, vectors, wide_bias, *rest
):
    stacks = rest[:4]
    normed, standard, root, active, slope, out_weight, up_weight, sem = rest[-8:]
    width = out_weight.shape[0]
    rows, half = width // PIECES, width // 2
    first = pl.program_id(0) == 0
    small = copies_of(table, stacks, rows, half, 0, out_weight, half, sem.at[0])
    large = copies_of(table, stacks, rows, 4 * half, half, up_weight, 4 * half, sem.at[1])

    @pl.when(first)
    def _():
        start(small)
        start(large)
        wait(small)

    attended = jnp.concatenate([a0[...], a1[...], a2[...]], axis=1)
    values = tokens[...].astype(FULL) + dot(attended, out_weight[...]) + vectors[2:3]
    n, s = norm_parts(values)
    standard[...] = n
    root[...] = jnp.broadcast_to(s, root.shape)
    low = (n * vectors[3:4] + vectors[4:5]).astype(LOW)
    normed[...] = low

    @pl.when(first)
    def _():
        wait(large)

    for c in range(4):
        columns = slice(c * width, (c + 1) * width)
        hidden = dot(low, up_weight[:, columns]) + wide_bias[:, (c + 2) * width : (c + 3) * width]
        part = 0.5 * (1.0 + lax.erf(hidden * 0.7071067811865476))
        density = jnp.exp(-0.5 * hidden * hidden) * 0.3989422804014327
        active[:, columns] = (hidden * part).astype(LOW)
        slope[:, columns] = (part + hidden * density).astype(LOW)


def widen(table, attended, tokens, vectors, wide_bias, stacks):
    width = tokens.shape[2]
    rows = tokens.shape[0] * tokens.shape[1]
    row = lambda w: pl.BlockSpec((TILE, w), lambda i, *_: (i, 0))
    return pl.pallas_call(
        widen_kernel,
        grid_spec=pltpu.PrefetchScalarGridSpec(
            num_scalar_prefetch=1,
            grid=(rows // TILE,),
            in_specs=[row(GROUP)] * 3
            + [row(width), whole(vectors.shape), whole(wide_bias.shape)]
            + [ANY] * 4,
            out_specs=[row(width), row(width), row(LANES), row(4 * width), row(4 * width)],
            scratch_shapes=[
                pltpu.VMEM((width, width), LOW),
                pltpu.VMEM((width, 4 * width), LOW),
                pltpu.SemaphoreType.DMA((2,)),
            ],
        ),
        out_shape=[
            shape((rows, width), LOW),
            shape((rows, width), FULL),
            shape((rows, LANES), FULL),
            shape((rows, 4 * width), LOW),
            shape((rows, 4 * width), LOW),
        ],
        compiler_params=params(),
        cost_estimate=cost(12e9, 30e6),
        name="widen",
    )(table, *attended, tokens.reshape(rows, width), vectors, wide_bias, *stacks)


def narrow_kernel(
    table, active, slope, normed, standard, root, cotangent, vectors, *rest
):
    ups, downs = rest[:4], rest[4:8]
    output, branch_two, pre_grad, branch_one, attended_grad, sums, up_sum = rest[8:15]
    out_weight, up_weight, down_weight, sem = rest[15:]
    width = out_weight.shape[0]
    rows, half = width // PIECES, width // 2
    first = pl.program_id(0) == 0
    out_copies = copies_of(table, ups, rows, half, 0, out_weight, half, sem.at[0])
    up_copies = copies_of(table, ups, rows, 4 * half, half, up_weight, 4 * half, sem.at[1])
    down_copies = copies_of(table, downs, 4 * rows, half, 0, down_weight, half, sem.at[2])

    @pl.when(first)
    def _():
        start(down_copies)
        start(up_copies)
        start(out_copies)
        sums[...] = jnp.zeros_like(sums)
        up_sum[...] = jnp.zeros_like(up_sum)
        wait(down_copies)

    values = normed[...].astype(FULL) + dot(active[...], down_weight[...]) + vectors[5:6]
    n2, s2 = norm_parts(values)
    output[...] = (n2 * vectors[6:7] + vectors[7:8]).astype(LOW)
    grad = cotangent[...].astype(FULL)
    second = norm_back(grad, n2, s2, vectors[6:7])
    low = second.astype(LOW)
    branch_two[...] = low
    sums[0:1] += column_sum(grad * n2)
    sums[1:2] += column_sum(grad)
    sums[2:3] += column_sum(low.astype(FULL))

    @pl.when(first)
    def _():
        wait(up_copies)

    normed_grad = second
    for c in range(4):
        columns = slice(c * width, (c + 1) * width)
        part = (dot(low, down_weight[columns], NT) * slope[:, columns].astype(FULL)).astype(LOW)
        pre_grad[:, columns] = part
        up_sum[:, columns] += column_sum(part.astype(FULL))
        normed_grad = normed_grad + dot(part, up_weight[:, columns], NT)
    n1 = standard[...]
    sums[3:4] += column_sum(normed_grad * n1)
    sums[4:5] += column_sum(normed_grad)
    low = norm_back(normed_grad, n1, root[:, 0:1], vectors[3:4]).astype(LOW)
    branch_one[...] = low
    sums[5:6] += column_sum(low.astype(FULL))

    @pl.when(first)
    def _():
        wait(out_copies)

    attended_grad[...] = dot(low, out_weight[...], NT).astype(LOW)


def narrow(table, active, slope, normed, standard, root, cotangent, vectors, ups, downs):
    rows, width = normed.shape
    row = lambda w: pl.BlockSpec((TILE, w), lambda i, *_: (i, 0))
    return pl.pallas_call(
        narrow_kernel,
        grid_spec=pltpu.PrefetchScalarGridSpec(
            num_scalar_prefetch=1,
            grid=(rows // TILE,),
            in_specs=[row(4 * width), row(4 * width), row(width), row(width), row(LANES), row(width)]
            + [whole(vectors.shape)]
            + [ANY] * 8,
            out_specs=[row(width), row(width), row(4 * width), row(width), row(width)]
            + [whole((8, width)), whole((1, 4 * width))],
            scratch_shapes=[
                pltpu.VMEM((width, width), LOW),
                pltpu.VMEM((width, 4 * width), LOW),
                pltpu.VMEM((4 * width, width), LOW),
                pltpu.SemaphoreType.DMA((3,)),
            ],
        ),
        out_shape=[
            shape((rows, width), LOW),
            shape((rows, width), LOW),
            shape((rows, 4 * width), LOW),
            shape((rows, width), LOW),
            shape((rows, width), LOW),
            shape((8, width), FULL),
            shape((1, 4 * width), FULL),
        ],
        compiler_params=params(),
        cost_estimate=cost(24e9, 40e6),
        name="narrow",
    )(table, active, slope, normed, standard, root, cotangent.reshape(rows, width), vectors, *ups, *downs)


def down_grad_kernel(order, active, branch_two, mine, theirs):
    step = pl.program_id(0)
    width = branch_two.shape[1]
    rows, half = 4 * width // PIECES, width // 2
    result = dot(active[...], branch_two[...], TN).astype(LOW)
    for p in range(4):
        block = result[rows * p : rows * (p + 1)]
        core = order[2, 0]

        @pl.when(core == 0)
        def _():
            mine[order[0, 4 * step + p]] = block[:, :half]
            theirs[order[1, 4 * step + p]] = block[:, half:]

        @pl.when(core == 1)
        def _():
            mine[order[0, 4 * step + p]] = block[:, half:]
            theirs[order[1, 4 * step + p]] = block[:, :half]


def down_grad(order, active, branch_two):
    rows, width = branch_two.shape
    stack = (PIECES, 4 * width // PIECES, width // 2)
    return pl.pallas_call(
        down_grad_kernel,
        grid_spec=pltpu.PrefetchScalarGridSpec(
            num_scalar_prefetch=1,
            grid=(4,),
            in_specs=[pl.BlockSpec((rows, width), lambda i, *_: (0, i)), whole((rows, width))],
            out_specs=[whole(stack)] * 2,
        ),
        out_shape=[shape(stack, LOW)] * 2,
        compiler_params=params(),
        cost_estimate=cost(7e9, 14e6),
        name="down_grad",
    )(order, active, branch_two)


def put_pieces(order, result, mine, theirs, to_mine, at):
    rows = result.shape[0] // PIECES
    width = result.shape[1]
    for p in range(PIECES):
        block = result[rows * p : rows * (p + 1)]

        @pl.when(to_mine)
        def _():
            mine[order[0, p], :, at : at + width] = block

        @pl.when(jnp.logical_not(to_mine))
        def _():
            theirs[order[1, p], :, at : at + width] = block


def up_grad_kernel(order, normed, pre_grad, a0, a1, a2, branch_one, sums, up_sum, *rest):
    mine, theirs = rest[-2:]
    step = pl.program_id(0)
    width = normed.shape[1]
    half = width // 2
    core = order[2, 0]

    @pl.when(step < 4)
    def _():
        result = dot(normed[...], pre_grad[...], TN).astype(LOW)
        for part in range(2):

            @pl.when(step % 2 == part)
            def _():
                put_pieces(order, result, mine, theirs, step // 2 == core, half + part * width)

    @pl.when(step == 4)
    def _():
        attended = jnp.concatenate([a0[...], a1[...], a2[...]], axis=1)
        result = dot(attended, branch_one[...], TN).astype(LOW)
        for c in range(2):
            put_pieces(order, result[:, c * half : (c + 1) * half], mine, theirs, core == c, 0)

    @pl.when(step == 0)
    def _():
        rows = width // PIECES
        lane = lax.broadcasted_iota(jnp.int32, (rows, LANES), 1)
        ones = jnp.concatenate([sums[...], jnp.zeros((LANES - 8, width), FULL)], axis=0).T
        up = [tall(up_sum[:, i * width : (i + 1) * width]) for i in range(4)]
        for p in range(PIECES):
            block = run_columns(ones[rows * p : rows * (p + 1)], lane, up, p, 4, 8).astype(LOW)
            mine[order[0, p], :, 5 * half :] = block
            theirs[order[1, p], :, 5 * half :] = block


def up_grad(order, normed, pre_grad, attended, branch_one, sums, up_sum, after=()):
    rows, width = normed.shape
    stack = (PIECES, width // PIECES, 5 * width // 2 + LANES)
    return pl.pallas_call(
        up_grad_kernel,
        grid_spec=pltpu.PrefetchScalarGridSpec(
            num_scalar_prefetch=1,
            grid=(5,),
            in_specs=[
                whole((rows, width)),
                pl.BlockSpec((rows, width), lambda i, *_: (0, jnp.minimum(i, 3))),
            ]
            + [whole((rows, GROUP))] * 3
            + [whole((rows, width)), whole(sums.shape), whole(up_sum.shape)]
            + [ANY] * len(after),
            out_specs=[whole(stack)] * 2,
        ),
        out_shape=[shape(stack, LOW)] * 2,
        compiler_params=params(),
        cost_estimate=cost(9e9, 18e6),
        name="up_grad",
    )(order, normed, pre_grad, *attended, branch_one, sums, up_sum, *after)


def attend_back_kernel(q_in, k_in, v_in, e_in, attended_full, inv_in, grad_in, *rest):
    out, sums = rest[-2:]
    seq = pl.program_id(0)
    q, k, v = q_in[...] * LOW(0.125), k_in[...], v_in[...]
    dims = q.shape
    grad = (grad_in[...].astype(FULL) * inv_in[...]).astype(LOW)
    along = grad.astype(FULL) * attended_full[...]
    q_total, k_total, v_total = (jnp.zeros(dims, FULL) for _ in range(3))
    for h in range(HEADS):
        mask = head_mask(h, dims)
        masked = lambda values: jnp.where(mask, values, LOW(0))
        exps = e_in[h]
        shift = jnp.sum(jnp.where(mask, along, 0.0), axis=1, keepdims=True)
        score = (exps.astype(FULL) * (dot(grad, masked(v), NT) - shift)).astype(LOW)
        q_total = q_total + dot(score, masked(k))
        k_total = k_total + dot(score, masked(q), TN)
        v_total = v_total + dot(exps, masked(grad), TN)
    parts = [(q_total * 0.125).astype(LOW), k_total.astype(LOW), v_total.astype(LOW)]
    for half in range(2):
        for i in range(3):
            at = (i + 3 * half) * LANES
            out[:, at : at + LANES] = parts[i][:, half * LANES : (half + 1) * LANES]
    both = jnp.concatenate([column_sum(parts[i].astype(FULL)) for i in (0, 2)], axis=0)

    @pl.when(seq == 0)
    def _():
        sums[0:2] = both

    @pl.when(seq != 0)
    def _():
        sums[0:2] += both


def attend_back(group, q, k, v, exps, attended_full, inv, grad, length, after=()):
    rows = q.shape[0]
    seqs = rows // length
    block = pl.BlockSpec((length, GROUP), lambda s: (s, 0))
    return pl.pallas_call(
        attend_back_kernel,
        grid=(seqs,),
        in_specs=[block] * 3
        + [pl.BlockSpec((HEADS, length, length), lambda s: (s, 0, 0))]
        + [block] * 2
        + [pl.BlockSpec((length, GROUP), lambda s: (s, group))]
        + [ANY] * len(after),
        out_specs=[pl.BlockSpec((length, 3 * GROUP), lambda s: (s, 0)), pl.BlockSpec((8, GROUP), lambda s: (0, 0))],
        out_shape=[shape((rows, 3 * GROUP), LOW), shape((8, GROUP), FULL)],
        compiler_params=params(),
        cost_estimate=cost(6e9, 10e6),
        name=f"attend_back_{group}",
    )(q, k, v, exps, attended_full, inv, grad, *after)


def tall(row):
    return jnp.broadcast_to(row, (LANES, row.shape[1])).T


def run_columns(block, lane, columns, piece, count, at):
    rows = block.shape[0]
    for j in range(count):
        run = count * piece + j
        first = rows * (run % PIECES)
        block = jnp.where(lane == at + j, columns[run // PIECES][first : first + rows], block)
    return block


def qkv_grad_kernel(order, tokens, g0, g1, g2, r0, r1, r2, *rest):
    mine, theirs = rest[-2:]
    step = pl.program_id(0)
    width = tokens.shape[1]
    half = width // 2
    core = order[2, 0]
    for i, grads in enumerate((g0, g1, g2)):

        @pl.when(step == i)
        def _():
            result = dot(tokens[...], grads[...], TN).astype(LOW)
            for c in range(2):
                put_pieces(order, result[:, c * half : (c + 1) * half], mine, theirs, core == c, i * half)

    @pl.when(step == 0)
    def _():
        rows = width // PIECES
        lane = lax.broadcasted_iota(jnp.int32, (rows, LANES), 1)
        qv_sums = jnp.concatenate([r0[...], r1[...], r2[...]], axis=1)
        qv = [tall(qv_sums[i : i + 1]) for i in range(2)]
        for p in range(PIECES):
            block = run_columns(jnp.zeros((rows, LANES), FULL), lane, qv, p, 2, 0).astype(LOW)
            mine[order[0, p], :, 3 * half :] = block
            theirs[order[1, p], :, 3 * half :] = block


def qkv_grad(order, tokens, grads, qv_sums, after=()):
    rows = grads[0].shape[0]
    width = tokens.shape[2]
    half = width // 2
    stack = (PIECES, width // PIECES, 3 * half + LANES)
    return pl.pallas_call(
        qkv_grad_kernel,
        grid_spec=pltpu.PrefetchScalarGridSpec(
            num_scalar_prefetch=1,
            grid=(3,),
            in_specs=[whole((rows, width))]
            + [whole((rows, 3 * GROUP))] * 3
            + [whole((8, GROUP))] * 3
            + [ANY] * len(after),
            out_specs=[whole(stack)] * 2,
        ),
        out_shape=[shape(stack, LOW)] * 2,
        compiler_params=params(),
        cost_estimate=cost(6e9, 14e6),
        name="qkv_grad",
    )(order, tokens.reshape(rows, width), *grads, *qv_sums, *after)


def token_grad_kernel(table, g0, g1, g2, first, *rest):
    out, w0, w1, w2, sem = rest[-5:]
    width = out.shape[1]
    rows = width // PIECES
    weights = (w0, w1, w2)
    copies = [
        group_copies(table, rest[:4], rows, i, weights[i], sem.at[i]) for i in range(3)
    ]
    begin = pl.program_id(0) == 0

    @pl.when(begin)
    def _():
        for i in range(3):
            start(copies[i])

    total = first[...].astype(FULL)
    for i, grads in enumerate((g0, g1, g2)):

        @pl.when(begin)
        def _():
            wait(copies[i])

        total = total + dot(grads[...], weights[i][...], NT)
    out[...] = total.astype(LOW)


def token_grad(table, grads, first, stacks, after=()):
    rows, width = first.shape
    row = lambda w: pl.BlockSpec((TILE, w), lambda i, *_: (i, 0))
    return pl.pallas_call(
        token_grad_kernel,
        grid_spec=pltpu.PrefetchScalarGridSpec(
            num_scalar_prefetch=1,
            grid=(rows // TILE,),
            in_specs=[row(3 * GROUP)] * 3 + [row(width)] + [ANY] * (4 + len(after)),
            out_specs=row(width),
            scratch_shapes=[pltpu.VMEM((width, 3 * GROUP), LOW)] * 3 + [pltpu.SemaphoreType.DMA((3,))],
        ),
        out_shape=shape((rows, width), LOW),
        compiler_params=params(),
        cost_estimate=cost(6e9, 12e6),
        name="token_grad",
    )(table, *grads, first, *stacks, *after)


def heads_in_kernel(at, weight, packed, out):
    groups = weight.shape[1] // (3 * GROUP)
    for g in range(groups):
        for i in range(3):
            first = (i * groups + g) * GROUP
            out[:, (3 * g + i) * LANES : (3 * g + i + 1) * LANES] = jnp.where(
                at[0] == 0, weight[:, first : first + LANES], weight[:, first + LANES : first + GROUP]
            )
    out[:, 3 * groups * LANES :] = packed[...]


def heads_in(core, weight, packed):
    rows, columns = weight.shape
    dims = (rows, columns // 2 + LANES)
    return pl.pallas_call(
        heads_in_kernel,
        grid_spec=pltpu.PrefetchScalarGridSpec(
            num_scalar_prefetch=1,
            grid=(1,),
            in_specs=[whole(weight.shape), whole(packed.shape)],
            out_specs=whole(dims),
        ),
        out_shape=shape(dims, LOW),
        name="heads_in",
    )(core.reshape(1), weight, packed)


def heads_out_kernel(at, mine, other, out):
    groups = out.shape[1] // (3 * GROUP)
    for g in range(groups):
        for i in range(3):
            first = (i * groups + g) * GROUP
            columns = slice((3 * g + i) * LANES, (3 * g + i + 1) * LANES)
            left, right = mine[:, columns], other[:, columns]
            out[:, first : first + LANES] = jnp.where(at[0] == 0, left, right)
            out[:, first + LANES : first + GROUP] = jnp.where(at[0] == 0, right, left)


def heads_out(core, mine, other):
    rows, columns = mine.shape
    dims = (rows, 2 * columns)
    return pl.pallas_call(
        heads_out_kernel,
        grid_spec=pltpu.PrefetchScalarGridSpec(
            num_scalar_prefetch=1,
            grid=(1,),
            in_specs=[whole(mine.shape)] * 2,
            out_specs=whole(dims),
        ),
        out_shape=shape(dims, FULL),
        name="heads_out",
    )(core.reshape(1), mine, other)


def pack(vectors, rows):
    columns = jnp.concatenate([v.reshape(-1, rows) for v in vectors], axis=0).T
    return jnp.pad(columns, ((0, 0), (0, LANES - columns.shape[1])))


def pack_all(chips, rows, qv, out_bias, gain_one, shift_one, up_bias, down_bias, gain_two, shift_two):
    parts = (qv, out_bias, gain_one, shift_one, down_bias, gain_two, shift_two, up_bias)
    if chips == 1:
        return pack(parts, rows)
    return jnp.concatenate(
        [pack([v.reshape(chips, -1)[p] for v in parts], rows) for p in range(chips)], axis=0
    )


def shards(
    chips,
    tokens,
    lengths,
    query_key_value_weight,
    qv_bias,
    output_projection_weight,
    output_projection_bias,
    gain_one,
    shift_one,
    widening_matrix,
    widening_offset_vector,
    down_projection_weight,
    down_projection_bias,
    gain_two,
    shift_two,
    cotangent,
):
    seq_count, seq_length, width = tokens.shape
    core, place = lax.axis_index("dp"), lax.axis_index("fsdp")
    rows = query_key_value_weight.shape[0]
    small = (
        qv_bias,
        output_projection_bias,
        gain_one,
        shift_one,
        widening_offset_vector,
        down_projection_bias,
        gain_two,
        shift_two,
    )
    direct = chips == PIECES
    numbers = jnp.arange(PIECES)
    if direct:
        half = width // 2
        down_in = half_of(down_projection_weight, core)
        ffn_in = jnp.concatenate(
            [half_of(output_projection_weight, core), half_of(widening_matrix, core)]
            + [down_in[rows * j : rows * (j + 1)] for j in range(4)],
            axis=1,
        )
        qkv_set = Gather(jnp.stack(line_parts(heads_in(core, query_key_value_weight, pack_all(1, rows, *small)))))
        qkv_set.plane()
        qkv_set.finish()
        up_first, down_first = stack_four(line_parts(ffn_in), half, (qkv_set.third,))
        up_set, down_set = Gather(up_first), Gather(down_first)
        owners = [piece_of(place, c, numbers) for c in (core, 1 - core)]
        entries = [entry_of(place, c, numbers) for c in (core, 1 - core)]
    else:
        gather = lambda values: lax.all_gather(values, "fsdp", axis=0, tiled=True)
        packed = pack_all(PIECES, width // PIECES, *(gather(v) for v in small))

        def stacks_of(make):
            both = [make(c) for c in (core, 1 - core)]
            both = [values.reshape(2, 8, -1, values.shape[1]) for values in both]
            return [values[i] for values in both for i in range(2)]

        full_qkv, full_out = gather(query_key_value_weight), gather(output_projection_weight)
        full_up, full_down = gather(widening_matrix), gather(down_projection_weight)
        qkv_stacks = stacks_of(lambda c: heads_in(c, full_qkv, packed))
        up_set = stacks_of(lambda c: jnp.concatenate([half_of(full_out, c), half_of(full_up, c)], axis=1))
        down_set = stacks_of(lambda c: half_of(full_down, c))
        owners = entries = [numbers, numbers]
    cores = jnp.where(numbers == 1, 1 - core, core)
    table = jnp.stack(owners + [cores]).astype(jnp.int32)
    order = jnp.stack(entries + [cores]).astype(jnp.int32)

    groups = range(width // GROUP)
    parts, wide_bias = [], None
    if direct:
        qkv_stacks = qkv_set.stacks
        *made, vectors, wide_bias = attend(0, table, lengths, tokens, qkv_stacks, None, (up_set.first,))
        parts.append(made)
        done = made[4]
        after = (done, up_set.plane((done,)))
        parts.append(attend(1, table, lengths, tokens, qkv_stacks, wide_bias, after))
        done = parts[1][4]
        after = (done, down_set.plane((done,)))
        parts.append(attend(2, table, lengths, tokens, qkv_stacks, wide_bias, after))
        up_set.finish((parts[2][4],))
        up_set = up_set.stacks
    else:
        for g in groups:
            made = attend(g, table, lengths, tokens, qkv_stacks, wide_bias)
            if g == 0:
                *made, vectors, wide_bias = made
            parts.append(made)
    attended = [part[4] for part in parts]
    normed, standard, root, active, slope = widen(table, attended, tokens, vectors, wide_bias, up_set)
    if direct:
        down_set.finish((normed,))
        down_set = down_set.stacks
    output, branch_two, pre_grad, branch_one, attended_grad, sums, up_sum = narrow(
        table, active, slope, normed, standard, root, cotangent, vectors, up_set, down_set
    )
    half = width // 2
    reduces = []

    def reduce_begin(pair):
        if direct:
            reduces.append(Scatter(pair))
        else:
            both = pair[0].astype(FULL) + swap_cores(pair[1]).astype(FULL)
            reduces.append(both.reshape(-1, both.shape[2]))

    def reduce_step(i, step):
        return (getattr(reduces[i], step)(),) if direct else ()

    def back(g, after):
        q, k, v, exps, _, attended_full, inv = parts[g]
        return attend_back(g, q, k, v, exps, attended_full, inv, attended_grad, seq_length, after)

    down_pair = down_grad(order, active, branch_two)
    reduce_begin(down_pair)
    up_pair = up_grad(
        order, normed, pre_grad, attended, branch_one, sums, up_sum, (down_pair[0],)
    )
    reduce_begin(up_pair)
    grad_0, part_0 = back(0, (up_pair[0],) + reduce_step(0, "cores"))
    grad_1, part_1 = back(1, (grad_0,) + reduce_step(0, "relay") + reduce_step(1, "cores"))
    grad_2, part_2 = back(2, (grad_1,) + reduce_step(0, "plane") + reduce_step(1, "relay"))
    grads = (grad_0, grad_1, grad_2)
    if direct:
        down_sum = reduces[0].line()
        later = (down_sum, reduces[1].plane())
    else:
        later = ()
    qkv_pair = qkv_grad(order, tokens, grads, (part_0, part_1, part_2), later)
    reduce_begin(qkv_pair)
    later = ()
    if direct:
        far = reduces[2].cores()
        up_total = reduces[1].line((far,))
        reduces[2].relay((up_total,))
        later = (reduces[2].plane(),)
    grad_tokens = token_grad(table, grads, branch_one, qkv_stacks, (qkv_pair[0],) + later)
    if direct:
        qkv_sum = reduces[2].line()
        up_vec, qkv_vec = up_total[:, 5 * half :], qkv_sum[:, 3 * half :]

        def vec_columns(at, count):
            values = (up_vec if at < 12 else qkv_vec)
            return values[:, at % 12 : at % 12 + count].T.reshape(-1)

    else:

        def reduce(values):
            return lax.psum_scatter(values, "fsdp", scatter_dimension=0, tiled=True)

        def vec_columns(at, count):
            values = reduces[1][:, 5 * half :] if at < 12 else reduces[2][:, 3 * half :]
            values = values.reshape(PIECES, -1, LANES)[:, :, at % 12 : at % 12 + count]
            return reduce(values.transpose(0, 2, 1).reshape(-1))

        down_sum = reduce(reduces[0])
        up_total, qkv_sum = reduce(reduces[1][:, : 5 * half]), reduce(reduces[2][:, : 3 * half])
    qkv_sum = qkv_sum[:, : 3 * half]
    out_sum, up_total = up_total[:, :half], up_total[:, half : 5 * half]
    return (
        output.reshape(tokens.shape),
        grad_tokens.reshape(tokens.shape),
        heads_out(core, qkv_sum, swap_cores(qkv_sum)),
        vec_columns(12, 2),
        join_halves(out_sum, core),
        vec_columns(5, 1),
        vec_columns(3, 1),
        vec_columns(4, 1),
        join_halves(up_total, core),
        vec_columns(8, 4),
        join_halves(down_sum, core),
        vec_columns(2, 1),
        vec_columns(0, 1),
        vec_columns(1, 1),
    )


def solution(mesh):
    tokens, lengths = P(("dp", "fsdp"), None, None), P(("dp", "fsdp"))
    matrix, vector = P("fsdp", None), P("fsdp")
    return jax.shard_map(
        functools.partial(shards, mesh.shape["fsdp"]),
        mesh=mesh,
        in_specs=(
            tokens, lengths, matrix, vector, matrix, vector, vector, vector,
            matrix, vector, matrix, vector, vector, vector, tokens,
        ),
        out_specs=(
            tokens, tokens, matrix, vector, matrix, vector, vector, vector,
            matrix, vector, matrix, vector, vector, vector,
        ),
        check_vma=False,
    )
```

```python
import functools

import jax
import jax.numpy as jnp
from jax import lax
from jax.experimental import pallas as pl
from jax.experimental.pallas import tpu as pltpu
from jax.sharding import PartitionSpec as P

HEAD_DIM = 64
GROUP = 256
HEADS = GROUP // HEAD_DIM
LANES = 128
PIECES = 16
TILE = 256
EPSILON = 1e-12
MASKED = -1e30
VMEM = 40 << 20
NN = (((1,), (0,)), ((), ()))
NT = (((1,), (1,)), ((), ()))
TN = (((0,), (0,)), ((), ()))
LOW, FULL = jnp.bfloat16, jnp.float32
ANY = pl.BlockSpec(memory_space=pl.ANY)


def dot(left, right, dims=NN):
    return lax.dot_general(left, right, dims, preferred_element_type=FULL)


def shape(dims, dtype):
    return jax.ShapeDtypeStruct(dims, dtype)


def far(dims, dtype):
    return pltpu.HBM(dims, dtype)


def keep_far(values):
    return pltpu.with_memory_space_constraint(values, pltpu.HBM)


def whole(dims):
    return pl.BlockSpec(dims, lambda *at: (0,) * len(dims))


def params():
    return pltpu.CompilerParams(vmem_limit_bytes=VMEM)


def cost(flops, moved, exps=0):
    return pl.CostEstimate(flops=int(flops), bytes_accessed=int(moved), transcendentals=int(exps))


def norm_parts(values):
    centred = values - jnp.mean(values, axis=-1, keepdims=True)
    inv_root = lax.rsqrt(jnp.mean(centred * centred, axis=-1, keepdims=True) + EPSILON)
    return centred * inv_root, inv_root


def norm_back(grad_in, standard, inv_root, gain_vec):
    scaled = grad_in * gain_vec
    return inv_root * (
        scaled
        - jnp.mean(scaled, axis=-1, keepdims=True)
        - standard * jnp.mean(scaled * standard, axis=-1, keepdims=True)
    )


def column_sum(values):
    return jnp.sum(values, axis=0, keepdims=True)


def swap_cores(values):
    return lax.ppermute(values, "dp", [(0, 1), (1, 0)])


def plane_swap(values, step):
    first, second = (1, 2) if step == 0 else (2, 1)
    pairs = [(i, i ^ first) for i in range(16)] + [(16 + i, 16 + (i ^ second)) for i in range(16)]
    return lax.ppermute(values, ("dp", "fsdp"), pairs)


def z_swap(values, m):
    return lax.ppermute(values, "fsdp", [(i, i ^ (4 * m)) for i in range(16)])


def piece_of(place, core, k):
    mz, m1, m2 = k % 4, (k // 4) % 2, k // 8
    low = jnp.where(core == 0, m1 + 2 * m2, 2 * m1 + m2)
    return place ^ (4 * mz + low)


def entry_of(place, core, piece):
    apart = piece ^ place
    mz, x, y = apart // 4, apart % 2, (apart // 2) % 2
    return mz + jnp.where(core == 0, 4 * x + 8 * y, 4 * y + 8 * x)


def gate_kernel(*refs):
    pass


def gate(values, after):
    return pl.pallas_call(
        gate_kernel,
        in_specs=[ANY] * (1 + len(after)),
        out_specs=ANY,
        out_shape=shape(values.shape, values.dtype),
        input_output_aliases={0: 0},
        name="gate",
    )(values, *after)


def stack_kernel(count, *refs):
    out = refs[-1]
    at = 0
    for ref in refs[:count]:
        if len(ref.shape) == 2:
            out[at] = ref[...]
            at += 1
        else:
            out[at : at + ref.shape[0]] = ref[...]
            at += ref.shape[0]


def stack(parts, after=()):
    dims = parts[0].shape[-2:]
    total = sum(1 if part.ndim == 2 else part.shape[0] for part in parts)
    return pl.pallas_call(
        functools.partial(stack_kernel, len(parts)),
        in_specs=[whole(part.shape) for part in parts] + [ANY] * len(after),
        out_specs=whole((total,) + dims),
        out_shape=shape((total,) + dims, LOW),
        grid=(1,),
        compiler_params=params(),
        name="stack",
    )(*parts, *after)


class Gather:
    def __init__(self, piece):
        self.parts = [piece] + [z_swap(piece, m) for m in (1, 2, 3)]

    def line(self, after=()):
        self.first = stack(self.parts, after) if after else jnp.stack(self.parts)
        self.beside = plane_swap(self.first, 0)
        return self.first

    def plane(self, after=()):
        self.second = stack([self.first, self.beside], after) if after else jnp.concatenate([self.first, self.beside])
        self.third = plane_swap(self.second, 1)
        self.other = swap_cores(self.second)
        return self.second

    def finish(self, after=()):
        if after:
            self.third = gate(self.third, after)
        self.stacks = [self.second, self.third, self.other, swap_cores(self.third)]
        return self.stacks


def add_low(*parts):
    return sum(p.astype(FULL) for p in parts).astype(LOW)


class Scatter:
    def __init__(self, pair):
        self.mine = pair[0]
        self.came = swap_cores(pair[1])

    def both(self, i):
        return self.mine[4 * i : 4 * i + 4], self.came[4 * i : 4 * i + 4]

    def cores(self):
        self.far, self.near = add_low(*self.both(3)), add_low(*self.both(2))
        self.far_came = plane_swap(self.far, 1)
        return self.far

    def relay(self, after=()):
        if after:
            self.far_came = gate(self.far_came, after)
        self.relayed = add_low(*self.both(1), self.far_came)
        self.relay_came = plane_swap(self.relayed, 0)
        self.near_came = plane_swap(gate(self.near, (self.relayed,)), 1)
        return self.relayed

    def plane(self):
        self.total = add_low(*self.both(0), self.near_came, self.relay_came)
        self.parts = [z_swap(self.total[m], m) for m in (1, 2, 3)]
        return self.total

    def line(self, after=()):
        if after:
            self.parts[0] = gate(self.parts[0], after)
        return self.total[0].astype(FULL) + sum(p.astype(FULL) for p in self.parts)


def half_of(values, which, axis=1):
    width = values.shape[axis] // 2
    return lax.dynamic_slice_in_dim(values, which * width, width, axis)


def join_halves(mine, core):
    other = swap_cores(mine)
    return jnp.where(
        core == 0, jnp.concatenate([mine, other], axis=1), jnp.concatenate([other, mine], axis=1)
    )


def copies_of(table, stacks, rows, width, skip, target, column_stride, sem):
    copies = []
    for half in range(2):
        for k in range(PIECES):
            row = pl.multiple_of(table[half, k] * rows, 16)
            column = pl.multiple_of(table[2, half] * column_stride, LANES)
            copies.append(
                pltpu.make_async_copy(
                    stacks[2 * half + k // 8].at[k % 8, :, pl.ds(skip, width)],
                    target.at[pl.ds(row, rows), pl.ds(column, width)],
                    sem,
                )
            )
    return copies


def start(copies):
    for copy in copies:
        copy.start()


def wait(copies):
    for copy in copies:
        copy.wait()


def head_mask(h, dims):
    lane = lax.broadcasted_iota(jnp.int32, dims, 1)
    return (lane >= HEAD_DIM * h) & (lane < HEAD_DIM * (h + 1))


def spread(vec, count, at):
    rows = vec.shape[0] // PIECES
    runs = [
        vec[rows * p : rows * (p + 1), at + j : at + j + 1] for p in range(PIECES) for j in range(count)
    ]
    tall = jnp.concatenate(runs, axis=0)
    return jnp.broadcast_to(tall, (tall.shape[0], LANES)).T[0:1]


def group_copies(table, stacks, rows, at, target, sem):
    copies = []
    wide = 3 * LANES
    for half in range(2):
        for k in range(PIECES):
            row = pl.multiple_of(table[half, k] * rows, 16)
            column = pl.multiple_of(table[2, half] * wide, LANES)
            copies.append(
                pltpu.make_async_copy(
                    stacks[2 * half + k // 8].at[k % 8, :, pl.ds(at * wide, wide)],
                    target.at[pl.ds(row, rows), pl.ds(column, wide)],
                    sem,
                )
            )
    return copies


def thirds(values):
    return [
        jnp.concatenate([values[:, i * LANES : (i + 1) * LANES], values[:, (i + 3) * LANES : (i + 4) * LANES]], axis=1)
        for i in range(3)
    ]


def attend_kernel(group, table, lengths, tokens, *rest):
    stacks, rest = rest[:4], rest[4:]
    weight, vec, bias, sem = rest[-4:]
    rest = rest[:-4]
    if group == 0:
        vectors, wide_bias = rest[-2:]
        rest = rest[:-2]
    else:
        wide_bias, rest = rest[0], rest[1:]
    q_out, k_out, v_out, e_out, attended, attended_full, inv_out = rest[-7:]
    seq = pl.program_id(0)
    width = weight.shape[0]
    rows = width // PIECES

    @pl.when(seq == 0)
    def _():
        large = group_copies(table, stacks, rows, group, weight, sem.at[1])
        if group == 0:
            small = [
                pltpu.make_async_copy(
                    stacks[k // 8].at[k % 8, :, pl.ds(3 * width // 2, LANES)],
                    vec.at[pl.ds(pl.multiple_of(table[0, k] * rows, 16), rows)],
                    sem.at[0],
                )
                for k in range(PIECES)
            ]
            start(small)
        start(large)
        if group == 0:
            wait(small)
            values = vec[...].astype(FULL)
            vectors[...] = values.T[0:16]
            wide_bias[:, 0 : 2 * width] = spread(values, 2, 0)
            wide_bias[:, 2 * width :] = spread(values, 4, 8)
        bias[...] = jnp.zeros_like(bias)
        for i, at in ((0, 0), (2, width)):
            for half in range(2):
                bias[:, (i + 3 * half) * LANES : (i + 3 * half + 1) * LANES] = wide_bias[
                    :, at + group * GROUP + half * LANES : at + group * GROUP + (half + 1) * LANES
                ]
        wait(large)

    q, k, v = thirds((dot(tokens[...], weight[...]) + bias[...]).astype(LOW))
    q_out[...], k_out[...], v_out[...] = q, k, v
    scaled = q * LOW(0.125)
    dims = q.shape
    keep = lax.broadcasted_iota(jnp.int32, (1, dims[0]), 1) < lengths[seq]
    total = jnp.zeros(dims, FULL)
    inv = jnp.zeros(dims, FULL)
    for h in range(HEADS):
        mask = head_mask(h, dims)
        scores = jnp.where(keep, dot(scaled, jnp.where(mask, k, LOW(0)), NT), MASKED)
        exps = jnp.exp(scores - jnp.max(scores, axis=1, keepdims=True))
        row_total = jnp.sum(exps, axis=1, keepdims=True)
        low = exps.astype(LOW)
        e_out[h] = low
        total = total + dot(low, jnp.where(mask, v, LOW(0)))
        inv = jnp.where(mask, 1.0 / row_total, inv)
    result = total * inv
    inv_out[...] = inv
    attended_full[...] = result
    attended[...] = result.astype(LOW)


def attend(group, table, lengths, tokens, stacks, wide_bias=None, after=()):
    seqs, length, width = tokens.shape
    rows = seqs * length
    block = pl.BlockSpec((length, GROUP), lambda s, *_: (s, 0))
    given = [] if group == 0 else [wide_bias]
    return pl.pallas_call(
        functools.partial(attend_kernel, group),
        grid_spec=pltpu.PrefetchScalarGridSpec(
            num_scalar_prefetch=2,
            grid=(seqs,),
            in_specs=[pl.BlockSpec((length, width), lambda s, *_: (s, 0))]
            + [ANY] * 4
            + [whole(g.shape) for g in given]
            + [ANY] * len(after),
            out_specs=[block] * 3
            + [pl.BlockSpec((HEADS, length, length), lambda s, *_: (s, 0, 0))]
            + [block] * 3
            + ([whole((16, width)), whole((1, 6 * width))] if group == 0 else []),
            scratch_shapes=[
                pltpu.VMEM((width, 3 * GROUP), LOW),
                pltpu.VMEM((width, LANES), LOW),
                pltpu.VMEM((1, 3 * GROUP), FULL),
                pltpu.SemaphoreType.DMA((2,)),
            ],
        ),
        out_shape=[far((rows, GROUP), LOW)] * 3
        + [
            far((seqs * HEADS, length, length), LOW),
            far((rows, GROUP), LOW),
            far((rows, GROUP), FULL),
            far((rows, GROUP), FULL),
        ]
        + ([shape((16, width), FULL), shape((1, 6 * width), FULL)] if group == 0 else []),
        compiler_params=params(),
        cost_estimate=cost(1e6, 1e3),
        name=f"attend_{group}",
    )(table, lengths, tokens.reshape(rows, width), *stacks, *given, *after)


def widen_kernel(
    table, a0, a1, a2, tokens, vectors, wide_bias, *rest
):
    stacks = rest[:4]
    normed, standard, root, active, slope, out_weight, up_weight, sem = rest[-8:]
    width = out_weight.shape[0]
    rows, half = width // PIECES, width // 2
    first = pl.program_id(0) == 0
    small = copies_of(table, stacks, rows, half, 0, out_weight, half, sem.at[0])
    large = copies_of(table, stacks, rows, 4 * half, half, up_weight, 4 * half, sem.at[1])

    @pl.when(first)
    def _():
        start(small)
        start(large)
        wait(small)

    attended = jnp.concatenate([a0[...], a1[...], a2[...]], axis=1)
    values = tokens[...].astype(FULL) + dot(attended, out_weight[...]) + vectors[2:3]
    n, s = norm_parts(values)
    standard[...] = n
    root[...] = jnp.broadcast_to(s, root.shape)
    low = (n * vectors[3:4] + vectors[4:5]).astype(LOW)
    normed[...] = low

    @pl.when(first)
    def _():
        wait(large)

    for c in range(4):
        columns = slice(c * width, (c + 1) * width)
        hidden = dot(low, up_weight[:, columns]) + wide_bias[:, (c + 2) * width : (c + 3) * width]
        part = 0.5 * (1.0 + lax.erf(hidden * 0.7071067811865476))
        density = jnp.exp(-0.5 * hidden * hidden) * 0.3989422804014327
        active[:, columns] = (hidden * part).astype(LOW)
        slope[:, columns] = (part + hidden * density).astype(LOW)


def widen(table, attended, tokens, vectors, wide_bias, stacks):
    width = tokens.shape[2]
    rows = tokens.shape[0] * tokens.shape[1]
    row = lambda w: pl.BlockSpec((TILE, w), lambda i, *_: (i, 0))
    return pl.pallas_call(
        widen_kernel,
        grid_spec=pltpu.PrefetchScalarGridSpec(
            num_scalar_prefetch=1,
            grid=(rows // TILE,),
            in_specs=[row(GROUP)] * 3
            + [row(width), whole(vectors.shape), whole(wide_bias.shape)]
            + [ANY] * 4,
            out_specs=[row(width), row(width), row(LANES), row(4 * width), row(4 * width)],
            scratch_shapes=[
                pltpu.VMEM((width, width), LOW),
                pltpu.VMEM((width, 4 * width), LOW),
                pltpu.SemaphoreType.DMA((2,)),
            ],
        ),
        out_shape=[
            far((rows, width), LOW),
            far((rows, width), FULL),
            far((rows, LANES), FULL),
            far((rows, 4 * width), LOW),
            far((rows, 4 * width), LOW),
        ],
        compiler_params=params(),
        cost_estimate=cost(12e9, 30e6),
        name="widen",
    )(table, *attended, tokens.reshape(rows, width), vectors, wide_bias, *stacks)


def narrow_kernel(
    table, active, slope, normed, standard, root, cotangent, vectors, *rest
):
    ups, downs = rest[:4], rest[4:8]
    output, branch_two, pre_grad, branch_one, attended_grad, sums, up_sum = rest[8:15]
    out_weight, up_weight, down_weight, sem = rest[15:]
    width = out_weight.shape[0]
    rows, half = width // PIECES, width // 2
    first = pl.program_id(0) == 0
    out_copies = copies_of(table, ups, rows, half, 0, out_weight, half, sem.at[0])
    up_copies = copies_of(table, ups, rows, 4 * half, half, up_weight, 4 * half, sem.at[1])
    down_copies = copies_of(table, downs, 4 * rows, half, 0, down_weight, half, sem.at[2])

    @pl.when(first)
    def _():
        start(down_copies)
        start(up_copies)
        start(out_copies)
        sums[...] = jnp.zeros_like(sums)
        up_sum[...] = jnp.zeros_like(up_sum)
        wait(down_copies)

    values = normed[...].astype(FULL) + dot(active[...], down_weight[...]) + vectors[5:6]
    n2, s2 = norm_parts(values)
    output[...] = (n2 * vectors[6:7] + vectors[7:8]).astype(LOW)
    grad = cotangent[...].astype(FULL)
    second = norm_back(grad, n2, s2, vectors[6:7])
    low = second.astype(LOW)
    branch_two[...] = low
    sums[0:1] += column_sum(grad * n2)
    sums[1:2] += column_sum(grad)
    sums[2:3] += column_sum(low.astype(FULL))

    @pl.when(first)
    def _():
        wait(up_copies)

    normed_grad = second
    for c in range(4):
        columns = slice(c * width, (c + 1) * width)
        part = (dot(low, down_weight[columns], NT) * slope[:, columns].astype(FULL)).astype(LOW)
        pre_grad[:, columns] = part
        up_sum[:, columns] += column_sum(part.astype(FULL))
        normed_grad = normed_grad + dot(part, up_weight[:, columns], NT)
    n1 = standard[...]
    sums[3:4] += column_sum(normed_grad * n1)
    sums[4:5] += column_sum(normed_grad)
    low = norm_back(normed_grad, n1, root[:, 0:1], vectors[3:4]).astype(LOW)
    branch_one[...] = low
    sums[5:6] += column_sum(low.astype(FULL))

    @pl.when(first)
    def _():
        wait(out_copies)

    attended_grad[...] = dot(low, out_weight[...], NT).astype(LOW)


def narrow(table, active, slope, normed, standard, root, cotangent, vectors, ups, downs):
    rows, width = normed.shape
    row = lambda w: pl.BlockSpec((TILE, w), lambda i, *_: (i, 0))
    return pl.pallas_call(
        narrow_kernel,
        grid_spec=pltpu.PrefetchScalarGridSpec(
            num_scalar_prefetch=1,
            grid=(rows // TILE,),
            in_specs=[row(4 * width), row(4 * width), row(width), row(width), row(LANES), row(width)]
            + [whole(vectors.shape)]
            + [ANY] * 8,
            out_specs=[row(width), row(width), row(4 * width), row(width), row(width)]
            + [whole((8, width)), whole((1, 4 * width))],
            scratch_shapes=[
                pltpu.VMEM((width, width), LOW),
                pltpu.VMEM((width, 4 * width), LOW),
                pltpu.VMEM((4 * width, width), LOW),
                pltpu.SemaphoreType.DMA((3,)),
            ],
        ),
        out_shape=[
            far((rows, width), LOW),
            far((rows, width), LOW),
            far((rows, 4 * width), LOW),
            far((rows, width), LOW),
            far((rows, width), LOW),
            shape((8, width), FULL),
            shape((1, 4 * width), FULL),
        ],
        compiler_params=params(),
        cost_estimate=cost(24e9, 40e6),
        name="narrow",
    )(
        table,
        *(keep_far(values) for values in (active, slope, normed, standard, root, cotangent.reshape(rows, width))),
        vectors,
        *ups,
        *downs,
    )


def down_grad_kernel(order, active, branch_two, mine, theirs):
    step = pl.program_id(0)
    width = branch_two.shape[1]
    rows, half = 4 * width // PIECES, width // 2
    result = dot(active[...], branch_two[...], TN).astype(LOW)
    for p in range(4):
        block = result[rows * p : rows * (p + 1)]
        core = order[2, 0]

        @pl.when(core == 0)
        def _():
            mine[order[0, 4 * step + p]] = block[:, :half]
            theirs[order[1, 4 * step + p]] = block[:, half:]

        @pl.when(core == 1)
        def _():
            mine[order[0, 4 * step + p]] = block[:, half:]
            theirs[order[1, 4 * step + p]] = block[:, :half]


def down_grad(order, active, branch_two):
    rows, width = branch_two.shape
    stack = (PIECES, 4 * width // PIECES, width // 2)
    return pl.pallas_call(
        down_grad_kernel,
        grid_spec=pltpu.PrefetchScalarGridSpec(
            num_scalar_prefetch=1,
            grid=(4,),
            in_specs=[pl.BlockSpec((rows, width), lambda i, *_: (0, i)), whole((rows, width))],
            out_specs=[whole(stack)] * 2,
        ),
        out_shape=[shape(stack, LOW)] * 2,
        compiler_params=params(),
        cost_estimate=cost(7e9, 14e6),
        name="down_grad",
    )(order, keep_far(active), keep_far(branch_two))


def put_pieces(order, result, mine, theirs, to_mine, at):
    rows = result.shape[0] // PIECES
    width = result.shape[1]
    for p in range(PIECES):
        block = result[rows * p : rows * (p + 1)]

        @pl.when(to_mine)
        def _():
            mine[order[0, p], :, at : at + width] = block

        @pl.when(jnp.logical_not(to_mine))
        def _():
            theirs[order[1, p], :, at : at + width] = block


def up_grad_kernel(order, normed, pre_grad, a0, a1, a2, branch_one, sums, up_sum, *rest):
    mine, theirs = rest[-2:]
    step = pl.program_id(0)
    width = normed.shape[1]
    half = width // 2
    core = order[2, 0]

    @pl.when(step < 4)
    def _():
        result = dot(normed[...], pre_grad[...], TN).astype(LOW)
        for part in range(2):

            @pl.when(step % 2 == part)
            def _():
                put_pieces(order, result, mine, theirs, step // 2 == core, half + part * width)

    @pl.when(step == 4)
    def _():
        attended = jnp.concatenate([a0[...], a1[...], a2[...]], axis=1)
        result = dot(attended, branch_one[...], TN).astype(LOW)
        for c in range(2):
            put_pieces(order, result[:, c * half : (c + 1) * half], mine, theirs, core == c, 0)

    @pl.when(step == 0)
    def _():
        rows = width // PIECES
        lane = lax.broadcasted_iota(jnp.int32, (rows, LANES), 1)
        ones = jnp.concatenate([sums[...], jnp.zeros((LANES - 8, width), FULL)], axis=0).T
        up = [tall(up_sum[:, i * width : (i + 1) * width]) for i in range(4)]
        for p in range(PIECES):
            block = run_columns(ones[rows * p : rows * (p + 1)], lane, up, p, 4, 8).astype(LOW)
            mine[order[0, p], :, 5 * half :] = block
            theirs[order[1, p], :, 5 * half :] = block


def up_grad(order, normed, pre_grad, attended, branch_one, sums, up_sum, after=()):
    rows, width = normed.shape
    stack = (PIECES, width // PIECES, 5 * width // 2 + LANES)
    return pl.pallas_call(
        up_grad_kernel,
        grid_spec=pltpu.PrefetchScalarGridSpec(
            num_scalar_prefetch=1,
            grid=(5,),
            in_specs=[
                whole((rows, width)),
                pl.BlockSpec((rows, width), lambda i, *_: (0, jnp.minimum(i, 3))),
            ]
            + [whole((rows, GROUP))] * 3
            + [whole((rows, width)), whole(sums.shape), whole(up_sum.shape)]
            + [ANY] * len(after),
            out_specs=[whole(stack)] * 2,
        ),
        out_shape=[shape(stack, LOW)] * 2,
        compiler_params=params(),
        cost_estimate=cost(9e9, 18e6),
        name="up_grad",
    )(order, keep_far(normed), keep_far(pre_grad), *attended, branch_one, sums, up_sum, *after)


def attend_back_kernel(q_in, k_in, v_in, e_in, attended_full, inv_in, grad_in, *rest):
    out, sums = rest[-2:]
    seq = pl.program_id(0)
    q, k, v = q_in[...] * LOW(0.125), k_in[...], v_in[...]
    dims = q.shape
    grad = (grad_in[...].astype(FULL) * inv_in[...]).astype(LOW)
    along = grad.astype(FULL) * attended_full[...]
    q_total, k_total, v_total = (jnp.zeros(dims, FULL) for _ in range(3))
    for h in range(HEADS):
        mask = head_mask(h, dims)
        masked = lambda values: jnp.where(mask, values, LOW(0))
        exps = e_in[h]
        shift = jnp.sum(jnp.where(mask, along, 0.0), axis=1, keepdims=True)
        score = (exps.astype(FULL) * (dot(grad, masked(v), NT) - shift)).astype(LOW)
        q_total = q_total + dot(score, masked(k))
        k_total = k_total + dot(score, masked(q), TN)
        v_total = v_total + dot(exps, masked(grad), TN)
    parts = [(q_total * 0.125).astype(LOW), k_total.astype(LOW), v_total.astype(LOW)]
    for half in range(2):
        for i in range(3):
            at = (i + 3 * half) * LANES
            out[:, at : at + LANES] = parts[i][:, half * LANES : (half + 1) * LANES]
    both = jnp.concatenate([column_sum(parts[i].astype(FULL)) for i in (0, 2)], axis=0)

    @pl.when(seq == 0)
    def _():
        sums[0:2] = both

    @pl.when(seq != 0)
    def _():
        sums[0:2] += both


def attend_back(group, q, k, v, exps, attended_full, inv, grad, length, after=()):
    rows = q.shape[0]
    seqs = rows // length
    block = pl.BlockSpec((length, GROUP), lambda s: (s, 0))
    return pl.pallas_call(
        attend_back_kernel,
        grid=(seqs,),
        in_specs=[block] * 3
        + [pl.BlockSpec((HEADS, length, length), lambda s: (s, 0, 0))]
        + [block] * 2
        + [pl.BlockSpec((length, GROUP), lambda s: (s, group))]
        + [ANY] * len(after),
        out_specs=[pl.BlockSpec((length, 3 * GROUP), lambda s: (s, 0)), pl.BlockSpec((8, GROUP), lambda s: (0, 0))],
        out_shape=[shape((rows, 3 * GROUP), LOW), shape((8, GROUP), FULL)],
        compiler_params=params(),
        cost_estimate=cost(6e9, 10e6),
        name=f"attend_back_{group}",
    )(*(keep_far(values) for values in (q, k, v, exps, attended_full, inv)), grad, *after)


def tall(row):
    return jnp.broadcast_to(row, (LANES, row.shape[1])).T


def run_columns(block, lane, columns, piece, count, at):
    rows = block.shape[0]
    for j in range(count):
        run = count * piece + j
        first = rows * (run % PIECES)
        block = jnp.where(lane == at + j, columns[run // PIECES][first : first + rows], block)
    return block


def qkv_grad_kernel(order, tokens, g0, g1, g2, r0, r1, r2, *rest):
    mine, theirs = rest[-2:]
    step = pl.program_id(0)
    width = tokens.shape[1]
    half = width // 2
    core = order[2, 0]
    for i, grads in enumerate((g0, g1, g2)):

        @pl.when(step == i)
        def _():
            result = dot(tokens[...], grads[...], TN).astype(LOW)
            for c in range(2):
                put_pieces(order, result[:, c * half : (c + 1) * half], mine, theirs, core == c, i * half)

    @pl.when(step == 0)
    def _():
        rows = width // PIECES
        lane = lax.broadcasted_iota(jnp.int32, (rows, LANES), 1)
        qv_sums = jnp.concatenate([r0[...], r1[...], r2[...]], axis=1)
        qv = [tall(qv_sums[i : i + 1]) for i in range(2)]
        for p in range(PIECES):
            block = run_columns(jnp.zeros((rows, LANES), FULL), lane, qv, p, 2, 0).astype(LOW)
            mine[order[0, p], :, 3 * half :] = block
            theirs[order[1, p], :, 3 * half :] = block


def qkv_grad(order, tokens, grads, qv_sums, after=()):
    rows = grads[0].shape[0]
    width = tokens.shape[2]
    half = width // 2
    stack = (PIECES, width // PIECES, 3 * half + LANES)
    return pl.pallas_call(
        qkv_grad_kernel,
        grid_spec=pltpu.PrefetchScalarGridSpec(
            num_scalar_prefetch=1,
            grid=(3,),
            in_specs=[whole((rows, width))]
            + [whole((rows, 3 * GROUP))] * 3
            + [whole((8, GROUP))] * 3
            + [ANY] * len(after),
            out_specs=[whole(stack)] * 2,
        ),
        out_shape=[shape(stack, LOW)] * 2,
        compiler_params=params(),
        cost_estimate=cost(6e9, 14e6),
        name="qkv_grad",
    )(order, tokens.reshape(rows, width), *grads, *qv_sums, *after)


def token_grad_kernel(table, g0, g1, g2, first, *rest):
    out, w0, w1, w2, sem = rest[-5:]
    width = out.shape[1]
    rows = width // PIECES
    weights = (w0, w1, w2)
    copies = [
        group_copies(table, rest[:4], rows, i, weights[i], sem.at[i]) for i in range(3)
    ]
    begin = pl.program_id(0) == 0

    @pl.when(begin)
    def _():
        for i in range(3):
            start(copies[i])

    total = first[...].astype(FULL)
    for i, grads in enumerate((g0, g1, g2)):

        @pl.when(begin)
        def _():
            wait(copies[i])

        total = total + dot(grads[...], weights[i][...], NT)
    out[...] = total.astype(LOW)


def token_grad(table, grads, first, stacks, after=()):
    rows, width = first.shape
    row = lambda w: pl.BlockSpec((TILE, w), lambda i, *_: (i, 0))
    return pl.pallas_call(
        token_grad_kernel,
        grid_spec=pltpu.PrefetchScalarGridSpec(
            num_scalar_prefetch=1,
            grid=(rows // TILE,),
            in_specs=[row(3 * GROUP)] * 3 + [row(width)] + [ANY] * (4 + len(after)),
            out_specs=row(width),
            scratch_shapes=[pltpu.VMEM((width, 3 * GROUP), LOW)] * 3 + [pltpu.SemaphoreType.DMA((3,))],
        ),
        out_shape=shape((rows, width), LOW),
        compiler_params=params(),
        cost_estimate=cost(6e9, 12e6),
        name="token_grad",
    )(table, *grads, first, *stacks, *after)


def heads_in_kernel(at, weight, packed, out):
    groups = weight.shape[1] // (3 * GROUP)
    for g in range(groups):
        for i in range(3):
            first = (i * groups + g) * GROUP
            out[:, (3 * g + i) * LANES : (3 * g + i + 1) * LANES] = jnp.where(
                at[0] == 0, weight[:, first : first + LANES], weight[:, first + LANES : first + GROUP]
            )
    out[:, 3 * groups * LANES :] = packed[...]


def heads_in(core, weight, packed):
    rows, columns = weight.shape
    dims = (rows, columns // 2 + LANES)
    return pl.pallas_call(
        heads_in_kernel,
        grid_spec=pltpu.PrefetchScalarGridSpec(
            num_scalar_prefetch=1,
            grid=(1,),
            in_specs=[whole(weight.shape), whole(packed.shape)],
            out_specs=whole(dims),
        ),
        out_shape=shape(dims, LOW),
        name="heads_in",
    )(core.reshape(1), weight, packed)


def join_heads(core, mine):
    rows, columns = mine.shape
    ordered = mine.reshape(rows, columns // (3 * LANES), 3, LANES).transpose(0, 2, 1, 3)
    other = swap_cores(mine).reshape(rows, columns // (3 * LANES), 3, LANES).transpose(0, 2, 1, 3)
    both = jnp.where(core == 0, jnp.stack([ordered, other], axis=3), jnp.stack([other, ordered], axis=3))
    return both.reshape(rows, 2 * columns)


def pack(vectors, rows):
    columns = jnp.concatenate([v.reshape(-1, rows) for v in vectors], axis=0).T
    return jnp.pad(columns, ((0, 0), (0, LANES - columns.shape[1])))


def pack_all(chips, rows, qv, out_bias, gain_one, shift_one, up_bias, down_bias, gain_two, shift_two):
    parts = (qv, out_bias, gain_one, shift_one, down_bias, gain_two, shift_two, up_bias)
    if chips == 1:
        return pack(parts, rows)
    return jnp.concatenate(
        [pack([v.reshape(chips, -1)[p] for v in parts], rows) for p in range(chips)], axis=0
    )


def shards(
    chips,
    tokens,
    lengths,
    query_key_value_weight,
    qv_bias,
    output_projection_weight,
    output_projection_bias,
    gain_one,
    shift_one,
    widening_matrix,
    widening_offset_vector,
    down_projection_weight,
    down_projection_bias,
    gain_two,
    shift_two,
    cotangent,
):
    seq_count, seq_length, width = tokens.shape
    core, place = lax.axis_index("dp"), lax.axis_index("fsdp")
    rows = query_key_value_weight.shape[0]
    small = (
        qv_bias,
        output_projection_bias,
        gain_one,
        shift_one,
        widening_offset_vector,
        down_projection_bias,
        gain_two,
        shift_two,
    )
    direct = chips == PIECES
    numbers = jnp.arange(PIECES)
    if direct:
        up_in = jnp.concatenate([half_of(output_projection_weight, core), half_of(widening_matrix, core)], axis=1)
        qkv_set = Gather(heads_in(core, query_key_value_weight, pack_all(1, rows, *small)))
        up_set, down_set = Gather(up_in), Gather(half_of(down_projection_weight, core))
        qkv_set.line()
        qkv_set.plane()
        owners = [piece_of(place, c, numbers) for c in (core, 1 - core)]
        entries = [entry_of(place, c, numbers) for c in (core, 1 - core)]
    else:
        gather = lambda values: lax.all_gather(values, "fsdp", axis=0, tiled=True)
        packed = pack_all(PIECES, width // PIECES, *(gather(v) for v in small))

        def stacks_of(make):
            both = [make(c) for c in (core, 1 - core)]
            both = [values.reshape(2, 8, -1, values.shape[1]) for values in both]
            return [values[i] for values in both for i in range(2)]

        full_qkv, full_out = gather(query_key_value_weight), gather(output_projection_weight)
        full_up, full_down = gather(widening_matrix), gather(down_projection_weight)
        qkv_stacks = stacks_of(lambda c: heads_in(c, full_qkv, packed))
        up_set = stacks_of(lambda c: jnp.concatenate([half_of(full_out, c), half_of(full_up, c)], axis=1))
        down_set = stacks_of(lambda c: half_of(full_down, c))
        owners = entries = [numbers, numbers]
    cores = jnp.where(numbers == 1, 1 - core, core)
    table = jnp.stack(owners + [cores]).astype(jnp.int32)
    order = jnp.stack(entries + [cores]).astype(jnp.int32)

    groups = range(width // GROUP)
    parts, wide_bias = [], None
    if direct:
        qkv_stacks = qkv_set.finish()
        *made, vectors, wide_bias = attend(0, table, lengths, tokens, qkv_stacks)
        parts.append(made)
        first = up_set.line((made[4],))
        parts.append(attend(1, table, lengths, tokens, qkv_stacks, wide_bias, (first,)))
        first = down_set.line((parts[1][4],))
        second = up_set.plane((first,))
        parts.append(attend(2, table, lengths, tokens, qkv_stacks, wide_bias, (second,)))
        second = down_set.plane((parts[2][4],))
        up_set = up_set.finish((second,))
    else:
        for g in groups:
            made = attend(g, table, lengths, tokens, qkv_stacks, wide_bias)
            if g == 0:
                *made, vectors, wide_bias = made
            parts.append(made)
    attended = [part[4] for part in parts]
    normed, standard, root, active, slope = widen(table, attended, tokens, vectors, wide_bias, up_set)
    if direct:
        down_set = down_set.finish((normed,))
    output, branch_two, pre_grad, branch_one, attended_grad, sums, up_sum = narrow(
        table, active, slope, normed, standard, root, cotangent, vectors, up_set, down_set
    )
    half = width // 2
    reduces = []

    def reduce_begin(pair):
        if direct:
            reduces.append(Scatter(pair))
        else:
            both = pair[0].astype(FULL) + swap_cores(pair[1]).astype(FULL)
            reduces.append(both.reshape(-1, both.shape[2]))

    def reduce_step(i, step):
        return (getattr(reduces[i], step)(),) if direct else ()

    def back(g, after):
        q, k, v, exps, _, attended_full, inv = parts[g]
        return attend_back(g, q, k, v, exps, attended_full, inv, attended_grad, seq_length, after)

    down_pair = down_grad(order, active, branch_two)
    reduce_begin(down_pair)
    up_pair = up_grad(
        order, normed, pre_grad, attended, branch_one, sums, up_sum, (down_pair[0],)
    )
    reduce_begin(up_pair)
    grad_0, part_0 = back(0, (up_pair[0],) + reduce_step(0, "cores"))
    grad_1, part_1 = back(1, (grad_0,) + reduce_step(0, "relay") + reduce_step(1, "cores"))
    grad_2, part_2 = back(2, (grad_1,) + reduce_step(0, "plane") + reduce_step(1, "relay"))
    grads = (grad_0, grad_1, grad_2)
    if direct:
        down_sum = reduces[0].line()
        later = (down_sum, reduces[1].plane())
    else:
        later = ()
    qkv_pair = qkv_grad(order, tokens, grads, (part_0, part_1, part_2), later)
    reduce_begin(qkv_pair)
    later = ()
    if direct:
        far = reduces[2].cores()
        up_total = reduces[1].line((far,))
        reduces[2].relay((up_total,))
        later = (reduces[2].plane(),)
    grad_tokens = token_grad(table, grads, branch_one, qkv_stacks, (qkv_pair[0],) + later)
    if direct:
        qkv_sum = reduces[2].line()
        up_vec, qkv_vec = up_total[:, 5 * half :], qkv_sum[:, 3 * half :]

        def vec_columns(at, count):
            values = (up_vec if at < 12 else qkv_vec)
            return values[:, at % 12 : at % 12 + count].T.reshape(-1)

    else:

        def reduce(values):
            return lax.psum_scatter(values, "fsdp", scatter_dimension=0, tiled=True)

        def vec_columns(at, count):
            values = reduces[1][:, 5 * half :] if at < 12 else reduces[2][:, 3 * half :]
            values = values.reshape(PIECES, -1, LANES)[:, :, at % 12 : at % 12 + count]
            return reduce(values.transpose(0, 2, 1).reshape(-1))

        down_sum = reduce(reduces[0])
        up_total, qkv_sum = reduce(reduces[1][:, : 5 * half]), reduce(reduces[2][:, : 3 * half])
    qkv_sum = qkv_sum[:, : 3 * half]
    out_sum, up_total = up_total[:, :half], up_total[:, half : 5 * half]
    return (
        output.reshape(tokens.shape),
        grad_tokens.reshape(tokens.shape),
        join_heads(core, qkv_sum),
        vec_columns(12, 2),
        join_halves(out_sum, core),
        vec_columns(5, 1),
        vec_columns(3, 1),
        vec_columns(4, 1),
        join_halves(up_total, core),
        vec_columns(8, 4),
        join_halves(down_sum, core),
        vec_columns(2, 1),
        vec_columns(0, 1),
        vec_columns(1, 1),
    )


def solution(mesh):
    tokens, lengths = P(("dp", "fsdp"), None, None), P(("dp", "fsdp"))
    matrix, vector = P("fsdp", None), P("fsdp")
    return jax.shard_map(
        functools.partial(shards, mesh.shape["fsdp"]),
        mesh=mesh,
        in_specs=(
            tokens, lengths, matrix, vector, matrix, vector, vector, vector,
            matrix, vector, matrix, vector, vector, vector, tokens,
        ),
        out_specs=(
            tokens, tokens, matrix, vector, matrix, vector, vector, vector,
            matrix, vector, matrix, vector, vector, vector,
        ),
        check_vma=False,
    )
```

```python
import functools

import jax
import jax.numpy as jnp
from jax import lax
from jax.experimental import pallas as pl
from jax.experimental.pallas import tpu as pltpu
from jax.sharding import PartitionSpec as P

HEAD_DIM = 64
GROUP = 256
HEADS = GROUP // HEAD_DIM
LANES = 128
PIECES = 16
TILE = 256
EPSILON = 1e-12
MASKED = -1e30
VMEM = 40 << 20
NN = (((1,), (0,)), ((), ()))
NT = (((1,), (1,)), ((), ()))
TN = (((0,), (0,)), ((), ()))
LOW, FULL = jnp.bfloat16, jnp.float32
ANY = pl.BlockSpec(memory_space=pl.ANY)


def dot(left, right, dims=NN):
    return lax.dot_general(left, right, dims, preferred_element_type=FULL)


def shape(dims, dtype):
    return jax.ShapeDtypeStruct(dims, dtype)


def far(dims, dtype):
    return pltpu.HBM(dims, dtype)


def keep_far(values):
    return pltpu.with_memory_space_constraint(values, pltpu.HBM)


def whole(dims):
    return pl.BlockSpec(dims, lambda *at: (0,) * len(dims))


def params():
    return pltpu.CompilerParams(vmem_limit_bytes=VMEM)


def cost(flops, moved, exps=0):
    return pl.CostEstimate(flops=int(flops), bytes_accessed=int(moved), transcendentals=int(exps))


def norm_parts(values):
    centred = values - jnp.mean(values, axis=-1, keepdims=True)
    inv_root = lax.rsqrt(jnp.mean(centred * centred, axis=-1, keepdims=True) + EPSILON)
    return centred * inv_root, inv_root


def norm_back(grad_in, standard, inv_root, gain_vec):
    scaled = grad_in * gain_vec
    return inv_root * (
        scaled
        - jnp.mean(scaled, axis=-1, keepdims=True)
        - standard * jnp.mean(scaled * standard, axis=-1, keepdims=True)
    )


def column_sum(values):
    return jnp.sum(values, axis=0, keepdims=True)


def swap_cores(values):
    return lax.ppermute(values, "dp", [(0, 1), (1, 0)])


def plane_swap(values, step):
    first, second = (1, 2) if step == 0 else (2, 1)
    pairs = [(i, i ^ first) for i in range(16)] + [(16 + i, 16 + (i ^ second)) for i in range(16)]
    return lax.ppermute(values, ("dp", "fsdp"), pairs)


def z_swap(values, m):
    return lax.ppermute(values, "fsdp", [(i, i ^ (4 * m)) for i in range(16)])


def piece_of(place, core, k):
    mz, m1, m2 = k % 4, (k // 4) % 2, k // 8
    low = jnp.where(core == 0, m1 + 2 * m2, 2 * m1 + m2)
    return place ^ (4 * mz + low)


def entry_of(place, core, piece):
    apart = piece ^ place
    mz, x, y = apart // 4, apart % 2, (apart // 2) % 2
    return mz + jnp.where(core == 0, 4 * x + 8 * y, 4 * y + 8 * x)


def gate_kernel(*refs):
    pass


def gate(values, after):
    return pl.pallas_call(
        gate_kernel,
        in_specs=[ANY] * (1 + len(after)),
        out_specs=ANY,
        out_shape=shape(values.shape, values.dtype),
        input_output_aliases={0: 0},
        name="gate",
    )(values, *after)


def stack_kernel(count, *refs):
    out = refs[-1]
    at = 0
    for ref in refs[:count]:
        if len(ref.shape) == 2:
            out[at] = ref[...]
            at += 1
        else:
            out[at : at + ref.shape[0]] = ref[...]
            at += ref.shape[0]


def stack(parts, after=()):
    dims = parts[0].shape[-2:]
    total = sum(1 if part.ndim == 2 else part.shape[0] for part in parts)
    return pl.pallas_call(
        functools.partial(stack_kernel, len(parts)),
        in_specs=[whole(part.shape) for part in parts] + [ANY] * len(after),
        out_specs=whole((total,) + dims),
        out_shape=shape((total,) + dims, LOW),
        grid=(1,),
        compiler_params=params(),
        name="stack",
    )(*parts, *after)


class Gather:
    def __init__(self, piece):
        self.parts = [piece] + [z_swap(piece, m) for m in (1, 2, 3)]

    def line(self, after=()):
        self.first = stack(self.parts, after) if after else jnp.stack(self.parts)
        self.beside = plane_swap(self.first, 0)
        return self.first

    def plane(self, after=()):
        self.second = stack([self.first, self.beside], after) if after else jnp.concatenate([self.first, self.beside])
        self.third = plane_swap(self.second, 1)
        self.other = swap_cores(self.second)
        return self.second

    def finish(self, after=()):
        if after:
            self.third = gate(self.third, after)
        self.stacks = [self.second, self.third, self.other, swap_cores(self.third)]
        return self.stacks


def add_low(*parts):
    return sum(p.astype(FULL) for p in parts).astype(LOW)


class Scatter:
    def __init__(self, pair):
        self.mine = pair[0]
        self.came = swap_cores(pair[1])

    def cores(self, after=()):
        if after:
            self.came = gate(self.came, after)
        self.far = add_low(self.mine[8:], self.came[8:])
        self.far_came = plane_swap(self.far, 1)
        return self.far

    def relay(self, after=()):
        if after:
            self.far_came = gate(self.far_came, after)
        self.relayed = add_low(self.mine[4:8], self.came[4:8], self.far_came[4:])
        self.relay_came = plane_swap(self.relayed, 0)
        return self.relayed

    def plane(self, after=()):
        if after:
            self.relay_came = gate(self.relay_came, after)
        self.total = add_low(self.mine[:4], self.came[:4], self.far_came[:4], self.relay_came)
        self.parts = [z_swap(self.total[m], m) for m in (1, 2, 3)]
        return self.total

    def line(self, after=()):
        if after:
            self.parts[0] = gate(self.parts[0], after)
        return self.total[0].astype(FULL) + sum(p.astype(FULL) for p in self.parts)


def half_of(values, which, axis=1):
    width = values.shape[axis] // 2
    return lax.dynamic_slice_in_dim(values, which * width, width, axis)


def join_halves(mine, core):
    other = swap_cores(mine)
    return jnp.where(
        core == 0, jnp.concatenate([mine, other], axis=1), jnp.concatenate([other, mine], axis=1)
    )


def copies_of(table, stacks, rows, width, skip, target, column_stride, sem):
    copies = []
    for half in range(2):
        for k in range(PIECES):
            row = pl.multiple_of(table[half, k] * rows, 16)
            column = pl.multiple_of(table[2, half] * column_stride, LANES)
            copies.append(
                pltpu.make_async_copy(
                    stacks[2 * half + k // 8].at[k % 8, :, pl.ds(skip, width)],
                    target.at[pl.ds(row, rows), pl.ds(column, width)],
                    sem,
                )
            )
    return copies


def start(copies):
    for copy in copies:
        copy.start()


def wait(copies):
    for copy in copies:
        copy.wait()


def head_mask(h, dims):
    lane = lax.broadcasted_iota(jnp.int32, dims, 1)
    return (lane >= HEAD_DIM * h) & (lane < HEAD_DIM * (h + 1))


def spread(vec, count, at):
    rows = vec.shape[0] // PIECES
    runs = [
        vec[rows * p : rows * (p + 1), at + j : at + j + 1] for p in range(PIECES) for j in range(count)
    ]
    tall = jnp.concatenate(runs, axis=0)
    return jnp.broadcast_to(tall, (tall.shape[0], LANES)).T[0:1]


def group_copies(table, stacks, rows, at, target, sem):
    copies = []
    wide = 3 * LANES
    for half in range(2):
        for k in range(PIECES):
            row = pl.multiple_of(table[half, k] * rows, 16)
            column = pl.multiple_of(table[2, half] * wide, LANES)
            copies.append(
                pltpu.make_async_copy(
                    stacks[2 * half + k // 8].at[k % 8, :, pl.ds(at * wide, wide)],
                    target.at[pl.ds(row, rows), pl.ds(column, wide)],
                    sem,
                )
            )
    return copies


def thirds(values):
    return [
        jnp.concatenate([values[:, i * LANES : (i + 1) * LANES], values[:, (i + 3) * LANES : (i + 4) * LANES]], axis=1)
        for i in range(3)
    ]


def attend_kernel(group, table, lengths, tokens, *rest):
    stacks, rest = rest[:4], rest[4:]
    weight, vec, bias, sem = rest[-4:]
    rest = rest[:-4]
    if group == 0:
        vectors, wide_bias = rest[-2:]
        rest = rest[:-2]
    else:
        wide_bias, rest = rest[0], rest[1:]
    q_out, k_out, v_out, e_out, attended, attended_full, inv_out = rest[-7:]
    seq = pl.program_id(0)
    width = weight.shape[0]
    rows = width // PIECES

    @pl.when(seq == 0)
    def _():
        large = group_copies(table, stacks, rows, group, weight, sem.at[1])
        if group == 0:
            small = [
                pltpu.make_async_copy(
                    stacks[k // 8].at[k % 8, :, pl.ds(3 * width // 2, LANES)],
                    vec.at[pl.ds(pl.multiple_of(table[0, k] * rows, 16), rows)],
                    sem.at[0],
                )
                for k in range(PIECES)
            ]
            start(small)
        start(large)
        if group == 0:
            wait(small)
            values = vec[...].astype(FULL)
            vectors[...] = values.T[0:16]
            wide_bias[:, 0 : 2 * width] = spread(values, 2, 0)
            wide_bias[:, 2 * width :] = spread(values, 4, 8)
        bias[...] = jnp.zeros_like(bias)
        for i, at in ((0, 0), (2, width)):
            for half in range(2):
                bias[:, (i + 3 * half) * LANES : (i + 3 * half + 1) * LANES] = wide_bias[
                    :, at + group * GROUP + half * LANES : at + group * GROUP + (half + 1) * LANES
                ]
        wait(large)

    q, k, v = thirds((dot(tokens[...], weight[...]) + bias[...]).astype(LOW))
    q_out[...], k_out[...], v_out[...] = q, k, v
    scaled = q * LOW(0.125)
    dims = q.shape
    keep = lax.broadcasted_iota(jnp.int32, (1, dims[0]), 1) < lengths[seq]
    total = jnp.zeros(dims, FULL)
    inv = jnp.zeros(dims, FULL)
    for h in range(HEADS):
        mask = head_mask(h, dims)
        scores = jnp.where(keep, dot(scaled, jnp.where(mask, k, LOW(0)), NT), MASKED)
        exps = jnp.exp(scores - jnp.max(scores, axis=1, keepdims=True))
        row_total = jnp.sum(exps, axis=1, keepdims=True)
        low = exps.astype(LOW)
        e_out[h] = low
        total = total + dot(low, jnp.where(mask, v, LOW(0)))
        inv = jnp.where(mask, 1.0 / row_total, inv)
    result = total * inv
    inv_out[...] = inv
    attended_full[...] = result
    attended[...] = result.astype(LOW)


def attend(group, table, lengths, tokens, stacks, wide_bias=None, after=()):
    seqs, length, width = tokens.shape
    rows = seqs * length
    block = pl.BlockSpec((length, GROUP), lambda s, *_: (s, 0))
    given = [] if group == 0 else [wide_bias]
    return pl.pallas_call(
        functools.partial(attend_kernel, group),
        grid_spec=pltpu.PrefetchScalarGridSpec(
            num_scalar_prefetch=2,
            grid=(seqs,),
            in_specs=[pl.BlockSpec((length, width), lambda s, *_: (s, 0))]
            + [ANY] * 4
            + [whole(g.shape) for g in given]
            + [ANY] * len(after),
            out_specs=[block] * 3
            + [pl.BlockSpec((HEADS, length, length), lambda s, *_: (s, 0, 0))]
            + [block] * 3
            + ([whole((16, width)), whole((1, 6 * width))] if group == 0 else []),
            scratch_shapes=[
                pltpu.VMEM((width, 3 * GROUP), LOW),
                pltpu.VMEM((width, LANES), LOW),
                pltpu.VMEM((1, 3 * GROUP), FULL),
                pltpu.SemaphoreType.DMA((2,)),
            ],
        ),
        out_shape=[far((rows, GROUP), LOW)] * 3
        + [
            far((seqs * HEADS, length, length), LOW),
            far((rows, GROUP), LOW),
            far((rows, GROUP), FULL),
            far((rows, GROUP), FULL),
        ]
        + ([shape((16, width), FULL), shape((1, 6 * width), FULL)] if group == 0 else []),
        compiler_params=params(),
        cost_estimate=cost(1e6, 1e3),
        name=f"attend_{group}",
    )(table, lengths, tokens.reshape(rows, width), *stacks, *given, *after)


def widen_kernel(
    table, a0, a1, a2, tokens, vectors, wide_bias, *rest
):
    stacks = rest[:4]
    normed, standard, root, active, slope, out_weight, up_weight, sem = rest[-8:]
    width = out_weight.shape[0]
    rows, half = width // PIECES, width // 2
    first = pl.program_id(0) == 0
    small = copies_of(table, stacks, rows, half, 0, out_weight, half, sem.at[0])
    large = copies_of(table, stacks, rows, 4 * half, half, up_weight, 4 * half, sem.at[1])

    @pl.when(first)
    def _():
        start(small)
        start(large)
        wait(small)

    attended = jnp.concatenate([a0[...], a1[...], a2[...]], axis=1)
    values = tokens[...].astype(FULL) + dot(attended, out_weight[...]) + vectors[2:3]
    n, s = norm_parts(values)
    standard[...] = n
    root[...] = jnp.broadcast_to(s, root.shape)
    low = (n * vectors[3:4] + vectors[4:5]).astype(LOW)
    normed[...] = low

    @pl.when(first)
    def _():
        wait(large)

    for c in range(4):
        columns = slice(c * width, (c + 1) * width)
        hidden = dot(low, up_weight[:, columns]) + wide_bias[:, (c + 2) * width : (c + 3) * width]
        part = 0.5 * (1.0 + lax.erf(hidden * 0.7071067811865476))
        density = jnp.exp(-0.5 * hidden * hidden) * 0.3989422804014327
        active[:, columns] = (hidden * part).astype(LOW)
        slope[:, columns] = (part + hidden * density).astype(LOW)


def widen(table, attended, tokens, vectors, wide_bias, stacks):
    width = tokens.shape[2]
    rows = tokens.shape[0] * tokens.shape[1]
    row = lambda w: pl.BlockSpec((TILE, w), lambda i, *_: (i, 0))
    return pl.pallas_call(
        widen_kernel,
        grid_spec=pltpu.PrefetchScalarGridSpec(
            num_scalar_prefetch=1,
            grid=(rows // TILE,),
            in_specs=[row(GROUP)] * 3
            + [row(width), whole(vectors.shape), whole(wide_bias.shape)]
            + [ANY] * 4,
            out_specs=[row(width), row(width), row(LANES), row(4 * width), row(4 * width)],
            scratch_shapes=[
                pltpu.VMEM((width, width), LOW),
                pltpu.VMEM((width, 4 * width), LOW),
                pltpu.SemaphoreType.DMA((2,)),
            ],
        ),
        out_shape=[
            far((rows, width), LOW),
            far((rows, width), FULL),
            far((rows, LANES), FULL),
            far((rows, 4 * width), LOW),
            far((rows, 4 * width), LOW),
        ],
        compiler_params=params(),
        cost_estimate=cost(12e9, 30e6),
        name="widen",
    )(table, *attended, tokens.reshape(rows, width), vectors, wide_bias, *stacks)


def narrow_kernel(
    table, active, slope, normed, standard, root, cotangent, vectors, *rest
):
    ups, downs = rest[:4], rest[4:8]
    output, branch_two, pre_grad, branch_one, attended_grad, sums, up_sum = rest[8:15]
    out_weight, up_weight, down_weight, sem = rest[15:]
    width = out_weight.shape[0]
    rows, half = width // PIECES, width // 2
    first = pl.program_id(0) == 0
    out_copies = copies_of(table, ups, rows, half, 0, out_weight, half, sem.at[0])
    up_copies = copies_of(table, ups, rows, 4 * half, half, up_weight, 4 * half, sem.at[1])
    down_copies = copies_of(table, downs, 4 * rows, half, 0, down_weight, half, sem.at[2])

    @pl.when(first)
    def _():
        start(down_copies)
        start(up_copies)
        start(out_copies)
        sums[...] = jnp.zeros_like(sums)
        up_sum[...] = jnp.zeros_like(up_sum)
        wait(down_copies)

    values = normed[...].astype(FULL) + dot(active[...], down_weight[...]) + vectors[5:6]
    n2, s2 = norm_parts(values)
    output[...] = (n2 * vectors[6:7] + vectors[7:8]).astype(LOW)
    grad = cotangent[...].astype(FULL)
    second = norm_back(grad, n2, s2, vectors[6:7])
    low = second.astype(LOW)
    branch_two[...] = low
    sums[0:1] += column_sum(grad * n2)
    sums[1:2] += column_sum(grad)
    sums[2:3] += column_sum(low.astype(FULL))

    @pl.when(first)
    def _():
        wait(up_copies)

    normed_grad = second
    for c in range(4):
        columns = slice(c * width, (c + 1) * width)
        part = (dot(low, down_weight[columns], NT) * slope[:, columns].astype(FULL)).astype(LOW)
        pre_grad[:, columns] = part
        up_sum[:, columns] += column_sum(part.astype(FULL))
        normed_grad = normed_grad + dot(part, up_weight[:, columns], NT)
    n1 = standard[...]
    sums[3:4] += column_sum(normed_grad * n1)
    sums[4:5] += column_sum(normed_grad)
    low = norm_back(normed_grad, n1, root[:, 0:1], vectors[3:4]).astype(LOW)
    branch_one[...] = low
    sums[5:6] += column_sum(low.astype(FULL))

    @pl.when(first)
    def _():
        wait(out_copies)

    attended_grad[...] = dot(low, out_weight[...], NT).astype(LOW)


def narrow(table, active, slope, normed, standard, root, cotangent, vectors, ups, downs):
    rows, width = normed.shape
    row = lambda w: pl.BlockSpec((TILE, w), lambda i, *_: (i, 0))
    return pl.pallas_call(
        narrow_kernel,
        grid_spec=pltpu.PrefetchScalarGridSpec(
            num_scalar_prefetch=1,
            grid=(rows // TILE,),
            in_specs=[row(4 * width), row(4 * width), row(width), row(width), row(LANES), row(width)]
            + [whole(vectors.shape)]
            + [ANY] * 8,
            out_specs=[row(width), row(width), row(4 * width), row(width), row(width)]
            + [whole((8, width)), whole((1, 4 * width))],
            scratch_shapes=[
                pltpu.VMEM((width, width), LOW),
                pltpu.VMEM((width, 4 * width), LOW),
                pltpu.VMEM((4 * width, width), LOW),
                pltpu.SemaphoreType.DMA((3,)),
            ],
        ),
        out_shape=[
            far((rows, width), LOW),
            far((rows, width), LOW),
            far((rows, 4 * width), LOW),
            far((rows, width), LOW),
            far((rows, width), LOW),
            shape((8, width), FULL),
            shape((1, 4 * width), FULL),
        ],
        compiler_params=params(),
        cost_estimate=cost(24e9, 40e6),
        name="narrow",
    )(
        table,
        *(keep_far(values) for values in (active, slope, normed, standard, root, cotangent.reshape(rows, width))),
        vectors,
        *ups,
        *downs,
    )


def down_grad_kernel(order, active, branch_two, mine, theirs):
    step = pl.program_id(0)
    width = branch_two.shape[1]
    rows, half = 4 * width // PIECES, width // 2
    result = dot(active[...], branch_two[...], TN).astype(LOW)
    for p in range(4):
        block = result[rows * p : rows * (p + 1)]
        core = order[2, 0]

        @pl.when(core == 0)
        def _():
            mine[order[0, 4 * step + p]] = block[:, :half]
            theirs[order[1, 4 * step + p]] = block[:, half:]

        @pl.when(core == 1)
        def _():
            mine[order[0, 4 * step + p]] = block[:, half:]
            theirs[order[1, 4 * step + p]] = block[:, :half]


def down_grad(order, active, branch_two):
    rows, width = branch_two.shape
    stack = (PIECES, 4 * width // PIECES, width // 2)
    return pl.pallas_call(
        down_grad_kernel,
        grid_spec=pltpu.PrefetchScalarGridSpec(
            num_scalar_prefetch=1,
            grid=(4,),
            in_specs=[pl.BlockSpec((rows, width), lambda i, *_: (0, i)), whole((rows, width))],
            out_specs=[whole(stack)] * 2,
        ),
        out_shape=[shape(stack, LOW)] * 2,
        compiler_params=params(),
        cost_estimate=cost(7e9, 14e6),
        name="down_grad",
    )(order, keep_far(active), keep_far(branch_two))


def put_pieces(order, result, mine, theirs, to_mine, at):
    rows = result.shape[0] // PIECES
    width = result.shape[1]
    for p in range(PIECES):
        block = result[rows * p : rows * (p + 1)]

        @pl.when(to_mine)
        def _():
            mine[order[0, p], :, at : at + width] = block

        @pl.when(jnp.logical_not(to_mine))
        def _():
            theirs[order[1, p], :, at : at + width] = block


def up_grad_kernel(order, normed, pre_grad, a0, a1, a2, branch_one, sums, up_sum, *rest):
    mine, theirs = rest[-2:]
    step = pl.program_id(0)
    width = normed.shape[1]
    half = width // 2
    core = order[2, 0]

    @pl.when(step < 4)
    def _():
        result = dot(normed[...], pre_grad[...], TN).astype(LOW)
        for part in range(2):

            @pl.when(step % 2 == part)
            def _():
                put_pieces(order, result, mine, theirs, step // 2 == core, half + part * width)

    @pl.when(step == 4)
    def _():
        attended = jnp.concatenate([a0[...], a1[...], a2[...]], axis=1)
        result = dot(attended, branch_one[...], TN).astype(LOW)
        for c in range(2):
            put_pieces(order, result[:, c * half : (c + 1) * half], mine, theirs, core == c, 0)

    @pl.when(step == 0)
    def _():
        rows = width // PIECES
        lane = lax.broadcasted_iota(jnp.int32, (rows, LANES), 1)
        ones = jnp.concatenate([sums[...], jnp.zeros((LANES - 8, width), FULL)], axis=0).T
        up = [tall(up_sum[:, i * width : (i + 1) * width]) for i in range(4)]
        for p in range(PIECES):
            block = run_columns(ones[rows * p : rows * (p + 1)], lane, up, p, 4, 8).astype(LOW)
            mine[order[0, p], :, 5 * half :] = block
            theirs[order[1, p], :, 5 * half :] = block


def up_grad(order, normed, pre_grad, attended, branch_one, sums, up_sum, after=()):
    rows, width = normed.shape
    stack = (PIECES, width // PIECES, 5 * width // 2 + LANES)
    return pl.pallas_call(
        up_grad_kernel,
        grid_spec=pltpu.PrefetchScalarGridSpec(
            num_scalar_prefetch=1,
            grid=(5,),
            in_specs=[
                whole((rows, width)),
                pl.BlockSpec((rows, width), lambda i, *_: (0, jnp.minimum(i, 3))),
            ]
            + [whole((rows, GROUP))] * 3
            + [whole((rows, width)), whole(sums.shape), whole(up_sum.shape)]
            + [ANY] * len(after),
            out_specs=[whole(stack)] * 2,
        ),
        out_shape=[shape(stack, LOW)] * 2,
        compiler_params=params(),
        cost_estimate=cost(9e9, 18e6),
        name="up_grad",
    )(order, keep_far(normed), keep_far(pre_grad), *attended, branch_one, sums, up_sum, *after)


def attend_back_kernel(q_in, k_in, v_in, e_in, attended_full, inv_in, grad_in, *rest):
    out, sums = rest[-2:]
    seq = pl.program_id(0)
    q, k, v = q_in[...] * LOW(0.125), k_in[...], v_in[...]
    dims = q.shape
    grad = (grad_in[...].astype(FULL) * inv_in[...]).astype(LOW)
    along = grad.astype(FULL) * attended_full[...]
    q_total, k_total, v_total = (jnp.zeros(dims, FULL) for _ in range(3))
    for h in range(HEADS):
        mask = head_mask(h, dims)
        masked = lambda values: jnp.where(mask, values, LOW(0))
        exps = e_in[h]
        shift = jnp.sum(jnp.where(mask, along, 0.0), axis=1, keepdims=True)
        score = (exps.astype(FULL) * (dot(grad, masked(v), NT) - shift)).astype(LOW)
        q_total = q_total + dot(score, masked(k))
        k_total = k_total + dot(score, masked(q), TN)
        v_total = v_total + dot(exps, masked(grad), TN)
    parts = [(q_total * 0.125).astype(LOW), k_total.astype(LOW), v_total.astype(LOW)]
    for half in range(2):
        for i in range(3):
            at = (i + 3 * half) * LANES
            out[:, at : at + LANES] = parts[i][:, half * LANES : (half + 1) * LANES]
    both = jnp.concatenate([column_sum(parts[i].astype(FULL)) for i in (0, 2)], axis=0)

    @pl.when(seq == 0)
    def _():
        sums[0:2] = both

    @pl.when(seq != 0)
    def _():
        sums[0:2] += both


def attend_back(group, q, k, v, exps, attended_full, inv, grad, length, after=()):
    rows = q.shape[0]
    seqs = rows // length
    block = pl.BlockSpec((length, GROUP), lambda s: (s, 0))
    return pl.pallas_call(
        attend_back_kernel,
        grid=(seqs,),
        in_specs=[block] * 3
        + [pl.BlockSpec((HEADS, length, length), lambda s: (s, 0, 0))]
        + [block] * 2
        + [pl.BlockSpec((length, GROUP), lambda s: (s, group))]
        + [ANY] * len(after),
        out_specs=[pl.BlockSpec((length, 3 * GROUP), lambda s: (s, 0)), pl.BlockSpec((8, GROUP), lambda s: (0, 0))],
        out_shape=[shape((rows, 3 * GROUP), LOW), shape((8, GROUP), FULL)],
        compiler_params=params(),
        cost_estimate=cost(6e9, 10e6),
        name=f"attend_back_{group}",
    )(*(keep_far(values) for values in (q, k, v, exps, attended_full, inv)), grad, *after)


def tall(row):
    return jnp.broadcast_to(row, (LANES, row.shape[1])).T


def run_columns(block, lane, columns, piece, count, at):
    rows = block.shape[0]
    for j in range(count):
        run = count * piece + j
        first = rows * (run % PIECES)
        block = jnp.where(lane == at + j, columns[run // PIECES][first : first + rows], block)
    return block


def qkv_grad_kernel(order, tokens, g0, g1, g2, r0, r1, r2, *rest):
    mine, theirs = rest[-2:]
    step = pl.program_id(0)
    width = tokens.shape[1]
    half = width // 2
    core = order[2, 0]
    for i, grads in enumerate((g0, g1, g2)):

        @pl.when(step == i)
        def _():
            result = dot(tokens[...], grads[...], TN).astype(LOW)
            for c in range(2):
                put_pieces(order, result[:, c * half : (c + 1) * half], mine, theirs, core == c, i * half)

    @pl.when(step == 0)
    def _():
        rows = width // PIECES
        lane = lax.broadcasted_iota(jnp.int32, (rows, LANES), 1)
        qv_sums = jnp.concatenate([r0[...], r1[...], r2[...]], axis=1)
        qv = [tall(qv_sums[i : i + 1]) for i in range(2)]
        for p in range(PIECES):
            block = run_columns(jnp.zeros((rows, LANES), FULL), lane, qv, p, 2, 0).astype(LOW)
            mine[order[0, p], :, 3 * half :] = block
            theirs[order[1, p], :, 3 * half :] = block


def qkv_grad(order, tokens, grads, qv_sums, after=()):
    rows = grads[0].shape[0]
    width = tokens.shape[2]
    half = width // 2
    stack = (PIECES, width // PIECES, 3 * half + LANES)
    return pl.pallas_call(
        qkv_grad_kernel,
        grid_spec=pltpu.PrefetchScalarGridSpec(
            num_scalar_prefetch=1,
            grid=(3,),
            in_specs=[whole((rows, width))]
            + [whole((rows, 3 * GROUP))] * 3
            + [whole((8, GROUP))] * 3
            + [ANY] * len(after),
            out_specs=[whole(stack)] * 2,
        ),
        out_shape=[shape(stack, LOW)] * 2,
        compiler_params=params(),
        cost_estimate=cost(6e9, 14e6),
        name="qkv_grad",
    )(order, tokens.reshape(rows, width), *grads, *qv_sums, *after)


def token_grad_kernel(table, g0, g1, g2, first, *rest):
    out, w0, w1, w2, sem = rest[-5:]
    width = out.shape[1]
    rows = width // PIECES
    weights = (w0, w1, w2)
    copies = [
        group_copies(table, rest[:4], rows, i, weights[i], sem.at[i]) for i in range(3)
    ]
    begin = pl.program_id(0) == 0

    @pl.when(begin)
    def _():
        for i in range(3):
            start(copies[i])

    total = first[...].astype(FULL)
    for i, grads in enumerate((g0, g1, g2)):

        @pl.when(begin)
        def _():
            wait(copies[i])

        total = total + dot(grads[...], weights[i][...], NT)
    out[...] = total.astype(LOW)


def token_grad(table, grads, first, stacks, after=()):
    rows, width = first.shape
    row = lambda w: pl.BlockSpec((TILE, w), lambda i, *_: (i, 0))
    return pl.pallas_call(
        token_grad_kernel,
        grid_spec=pltpu.PrefetchScalarGridSpec(
            num_scalar_prefetch=1,
            grid=(rows // TILE,),
            in_specs=[row(3 * GROUP)] * 3 + [row(width)] + [ANY] * (4 + len(after)),
            out_specs=row(width),
            scratch_shapes=[pltpu.VMEM((width, 3 * GROUP), LOW)] * 3 + [pltpu.SemaphoreType.DMA((3,))],
        ),
        out_shape=shape((rows, width), LOW),
        compiler_params=params(),
        cost_estimate=cost(6e9, 12e6),
        name="token_grad",
    )(table, *(keep_far(values) for values in (*grads, first)), *stacks, *after)


def heads_in_kernel(at, weight, packed, out):
    groups = weight.shape[1] // (3 * GROUP)
    for g in range(groups):
        for i in range(3):
            first = (i * groups + g) * GROUP
            out[:, (3 * g + i) * LANES : (3 * g + i + 1) * LANES] = jnp.where(
                at[0] == 0, weight[:, first : first + LANES], weight[:, first + LANES : first + GROUP]
            )
    out[:, 3 * groups * LANES :] = packed[...]


def heads_in(core, weight, packed):
    rows, columns = weight.shape
    dims = (rows, columns // 2 + LANES)
    return pl.pallas_call(
        heads_in_kernel,
        grid_spec=pltpu.PrefetchScalarGridSpec(
            num_scalar_prefetch=1,
            grid=(1,),
            in_specs=[whole(weight.shape), whole(packed.shape)],
            out_specs=whole(dims),
        ),
        out_shape=shape(dims, LOW),
        name="heads_in",
    )(core.reshape(1), weight, packed)


def join_heads(core, mine):
    rows, columns = mine.shape
    ordered = mine.reshape(rows, columns // (3 * LANES), 3, LANES).transpose(0, 2, 1, 3)
    other = swap_cores(mine).reshape(rows, columns // (3 * LANES), 3, LANES).transpose(0, 2, 1, 3)
    both = jnp.where(core == 0, jnp.stack([ordered, other], axis=3), jnp.stack([other, ordered], axis=3))
    return both.reshape(rows, 2 * columns)


def pack(vectors, rows):
    columns = jnp.concatenate([v.reshape(-1, rows) for v in vectors], axis=0).T
    return jnp.pad(columns, ((0, 0), (0, LANES - columns.shape[1])))


def pack_all(chips, rows, qv, out_bias, gain_one, shift_one, up_bias, down_bias, gain_two, shift_two):
    parts = (qv, out_bias, gain_one, shift_one, down_bias, gain_two, shift_two, up_bias)
    if chips == 1:
        return pack(parts, rows)
    return jnp.concatenate(
        [pack([v.reshape(chips, -1)[p] for v in parts], rows) for p in range(chips)], axis=0
    )


def shards(
    chips,
    tokens,
    lengths,
    query_key_value_weight,
    qv_bias,
    output_projection_weight,
    output_projection_bias,
    gain_one,
    shift_one,
    widening_matrix,
    widening_offset_vector,
    down_projection_weight,
    down_projection_bias,
    gain_two,
    shift_two,
    cotangent,
):
    seq_count, seq_length, width = tokens.shape
    core, place = lax.axis_index("dp"), lax.axis_index("fsdp")
    rows = query_key_value_weight.shape[0]
    small = (
        qv_bias,
        output_projection_bias,
        gain_one,
        shift_one,
        widening_offset_vector,
        down_projection_bias,
        gain_two,
        shift_two,
    )
    direct = chips == PIECES
    numbers = jnp.arange(PIECES)
    if direct:
        up_in = jnp.concatenate([half_of(output_projection_weight, core), half_of(widening_matrix, core)], axis=1)
        qkv_set = Gather(heads_in(core, query_key_value_weight, pack_all(1, rows, *small)))
        up_set, down_set = Gather(up_in), Gather(half_of(down_projection_weight, core))
        qkv_set.line()
        qkv_set.plane()
        owners = [piece_of(place, c, numbers) for c in (core, 1 - core)]
        entries = [entry_of(place, c, numbers) for c in (core, 1 - core)]
    else:
        gather = lambda values: lax.all_gather(values, "fsdp", axis=0, tiled=True)
        packed = pack_all(PIECES, width // PIECES, *(gather(v) for v in small))

        def stacks_of(make):
            both = [make(c) for c in (core, 1 - core)]
            both = [values.reshape(2, 8, -1, values.shape[1]) for values in both]
            return [values[i] for values in both for i in range(2)]

        full_qkv, full_out = gather(query_key_value_weight), gather(output_projection_weight)
        full_up, full_down = gather(widening_matrix), gather(down_projection_weight)
        qkv_stacks = stacks_of(lambda c: heads_in(c, full_qkv, packed))
        up_set = stacks_of(lambda c: jnp.concatenate([half_of(full_out, c), half_of(full_up, c)], axis=1))
        down_set = stacks_of(lambda c: half_of(full_down, c))
        owners = entries = [numbers, numbers]
    cores = jnp.where(numbers == 1, 1 - core, core)
    table = jnp.stack(owners + [cores]).astype(jnp.int32)
    order = jnp.stack(entries + [cores]).astype(jnp.int32)

    groups = range(width // GROUP)
    parts, wide_bias = [], None
    if direct:
        qkv_stacks = qkv_set.finish()
        *made, vectors, wide_bias = attend(0, table, lengths, tokens, qkv_stacks)
        parts.append(made)
        first = up_set.line((made[4],))
        parts.append(attend(1, table, lengths, tokens, qkv_stacks, wide_bias, (first,)))
        first = down_set.line((parts[1][4],))
        second = up_set.plane((first,))
        parts.append(attend(2, table, lengths, tokens, qkv_stacks, wide_bias, (second,)))
        second = down_set.plane((parts[2][4],))
        up_set = up_set.finish((second,))
    else:
        for g in groups:
            made = attend(g, table, lengths, tokens, qkv_stacks, wide_bias)
            if g == 0:
                *made, vectors, wide_bias = made
            parts.append(made)
    attended = [part[4] for part in parts]
    normed, standard, root, active, slope = widen(table, attended, tokens, vectors, wide_bias, up_set)
    if direct:
        down_set = down_set.finish((normed,))
    output, branch_two, pre_grad, branch_one, attended_grad, sums, up_sum = narrow(
        table, active, slope, normed, standard, root, cotangent, vectors, up_set, down_set
    )
    half = width // 2
    reduces = []

    def reduce_begin(pair):
        if direct:
            reduces.append(Scatter(pair))
        else:
            both = pair[0].astype(FULL) + swap_cores(pair[1]).astype(FULL)
            reduces.append(both.reshape(-1, both.shape[2]))

    def reduce_step(i, step):
        return (getattr(reduces[i], step)(),) if direct else ()

    def back(g, after):
        q, k, v, exps, _, attended_full, inv = parts[g]
        return attend_back(g, q, k, v, exps, attended_full, inv, attended_grad, seq_length, after)

    down_pair = down_grad(order, active, branch_two)
    reduce_begin(down_pair)
    up_pair = up_grad(
        order, normed, pre_grad, attended, branch_one, sums, up_sum, (down_pair[0],)
    )
    reduce_begin(up_pair)
    grad_0, part_0 = back(0, (up_pair[0],) + reduce_step(0, "cores"))
    grad_1, part_1 = back(1, (grad_0,) + reduce_step(0, "relay") + reduce_step(1, "cores"))
    grad_2, part_2 = back(2, (grad_1,) + reduce_step(0, "plane") + reduce_step(1, "relay"))
    grads = (grad_0, grad_1, grad_2)
    if direct:
        down_sum = reduces[0].line((grad_2,))
        later = (down_sum, reduces[1].plane())
    else:
        later = ()
    qkv_pair = qkv_grad(order, tokens, grads, (part_0, part_1, part_2), later)
    reduce_begin(qkv_pair)
    later = ()
    if direct:
        far = reduces[2].cores()
        up_total = reduces[1].line((far,))
        reduces[2].relay((up_total,))
        later = (reduces[2].plane(),)
    grad_tokens = token_grad(table, grads, branch_one, qkv_stacks, (qkv_pair[0],) + later)
    if direct:
        qkv_sum = reduces[2].line()
        up_vec, qkv_vec = up_total[:, 5 * half :], qkv_sum[:, 3 * half :]

        def vec_columns(at, count):
            values = (up_vec if at < 12 else qkv_vec)
            return values[:, at % 12 : at % 12 + count].T.reshape(-1)

    else:

        def reduce(values):
            return lax.psum_scatter(values, "fsdp", scatter_dimension=0, tiled=True)

        def vec_columns(at, count):
            values = reduces[1][:, 5 * half :] if at < 12 else reduces[2][:, 3 * half :]
            values = values.reshape(PIECES, -1, LANES)[:, :, at % 12 : at % 12 + count]
            return reduce(values.transpose(0, 2, 1).reshape(-1))

        down_sum = reduce(reduces[0])
        up_total, qkv_sum = reduce(reduces[1][:, : 5 * half]), reduce(reduces[2][:, : 3 * half])
    qkv_sum = qkv_sum[:, : 3 * half]
    out_sum, up_total = up_total[:, :half], up_total[:, half : 5 * half]
    return (
        output.reshape(tokens.shape),
        grad_tokens.reshape(tokens.shape),
        join_heads(core, qkv_sum),
        vec_columns(12, 2),
        join_halves(out_sum, core),
        vec_columns(5, 1),
        vec_columns(3, 1),
        vec_columns(4, 1),
        join_halves(up_total, core),
        vec_columns(8, 4),
        join_halves(down_sum, core),
        vec_columns(2, 1),
        vec_columns(0, 1),
        vec_columns(1, 1),
    )


def solution(mesh):
    tokens, lengths = P(("dp", "fsdp"), None, None), P(("dp", "fsdp"))
    matrix, vector = P("fsdp", None), P("fsdp")
    return jax.shard_map(
        functools.partial(shards, mesh.shape["fsdp"]),
        mesh=mesh,
        in_specs=(
            tokens, lengths, matrix, vector, matrix, vector, vector, vector,
            matrix, vector, matrix, vector, vector, vector, tokens,
        ),
        out_specs=(
            tokens, tokens, matrix, vector, matrix, vector, vector, vector,
            matrix, vector, matrix, vector, vector, vector,
        ),
        check_vma=False,
    )
```
